32 devices in a mesh: dp: 8 (over z, y), chan: 4 (over x, core).
Axes of the slice: x: 2, y: 2, z: 4, core: 2. Of those that a mesh axis runs over, the one named last changes fastest.
Arguments:
- mel: bfloat16 [16, 2816, 80], P('dp', 'chan'), may hold values from -6 to 6
- lang_group: int32 [16], P('dp'), may hold values from 0 to 15
- clip_count: int32 [8], replicated, may hold values from 1 to 2, as said below
- conv_one: bfloat16 [240, 768], P(None, 'chan'), may hold values from -0.375 to 0.375
- conv_one_bias: bfloat16 [768], P('chan'), may hold values from -1.796875 to 1.796875
- conv_two: bfloat16 [3, 768, 768], P(None, 'chan'), may hold values from -0.125 to 0.125
- conv_two_bias: bfloat16 [768], replicated, may hold values from -1.796875 to 1.796875
- lang_table: bfloat16 [16, 768], replicated, may hold values from -3 to 3
- ln_one_gain: bfloat16 [768], replicated, may hold values from 0.5 to 1.5
- ln_one_bias: bfloat16 [768], replicated, may hold values from -1.796875 to 1.796875
- w_qkv: bfloat16 [768, 2304], P('chan'), may hold values from -0.3125 to 0.3125
- q_bias: bfloat16 [768], replicated, may hold values from -1.796875 to 1.796875
- v_bias: bfloat16 [768], replicated, may hold values from -1.796875 to 1.796875
- w_out: bfloat16 [768, 768], P('chan'), may hold values from -0.875 to 0.875
- out_bias: bfloat16 [768], replicated, may hold values from -1.796875 to 1.796875
- ln_two_gain: bfloat16 [768], replicated, may hold values from 0.5 to 1.5
- ln_two_bias: bfloat16 [768], replicated, may hold values from -1.796875 to 1.796875
- w_fc_one: bfloat16 [768, 3072], P('chan'), may hold values from -0.21875 to 0.21875
- fc_one_bias: bfloat16 [3072], replicated, may hold values from -1.796875 to 1.796875
- w_fc_two: bfloat16 [3072, 768], P('chan'), may hold values from -0.109375 to 0.109375
- fc_two_bias: bfloat16 [768], replicated, may hold values from -1.796875 to 1.796875
- grad_out: bfloat16 [16, 1408, 768], P('dp', 'chan'), may hold values from -6 to 6
Outputs:
- encoded: bfloat16 [16, 1408, 768], P('dp', 'chan')
- mel_grad: float32 [16, 2816, 80], P('dp', 'chan')
- conv_one_grad: float32 [240, 768], P(None, 'chan')
- conv_one_bias_grad: float32 [768], P('chan')
- conv_two_grad: float32 [3, 768, 768], P(None, 'chan')
- conv_two_bias_grad: float32 [768], replicated
- lang_table_grad: float32 [16, 768], replicated
- ln_one_gain_grad: float32 [768], replicated
- ln_one_bias_grad: float32 [768], replicated
- w_qkv_grad: float32 [768, 2304], P('chan')
- q_bias_grad: float32 [768], replicated
- v_bias_grad: float32 [768], replicated
- w_out_grad: float32 [768, 768], P('chan')
- out_bias_grad: float32 [768], replicated
- ln_two_gain_grad: float32 [768], replicated
- ln_two_bias_grad: float32 [768], replicated
- w_fc_one_grad: float32 [768, 3072], P('chan')
- fc_one_bias_grad: float32 [3072], replicated
- w_fc_two_grad: float32 [3072, 768], P('chan')
- fc_two_bias_grad: float32 [768], replicated
The draws below stay inside these ranges and needn't reach their ends.
Inputs may be any that keep to these rules, and one draw needn't show every extreme that they name: Slot s of index i of dp holds a live clip when s < clip_count[i]; some index has 2 live clips and some has 1.
All inputs are finite; a program needn't handle non-finite values.
Results may differ from the reference program's by a relative error of at most 0.02.
Values may be sent and summed in bfloat16 or wider, within the bound.
No kernel may reach another device: no remote copies, remote signals or barrier semaphores. Data moves between devices by JAX's collectives and lax.ppermute only.
A program may use at most 320 MiB of HBM per device.

```python
import math
import jax
import jax.numpy as jnp
from jax import lax

D = 768
HEADS = 12
HEAD_DIM = 64
FF = 3072
MEL = 80
GROUPS = 16
FRAMES = 1408
SLOT_DEV = 2
CLIPS = 16
N_DP = 8


def draw_clip_count(key, part):
    key = jax.random.fold_in(key, 11)
    count_key, order_key = jax.random.split(key)
    counts = jax.random.randint(count_key, (N_DP,), 1, SLOT_DEV + 1)
    rank_order = jax.random.permutation(order_key, N_DP)
    counts = jnp.where(rank_order == 0, SLOT_DEV, jnp.where(rank_order == 1, 1, counts))
    return counts.astype(jnp.int32)


def with_ends(entries, key, smallest, largest):
    longest = entries.shape.index(max(entries.shape))
    spots = []
    for shift in (0, 1):
        where = [jax.random.randint(jax.random.fold_in(key, axis), (), 0, length) for axis, length in enumerate(entries.shape)]
        where[longest] = (where[longest] + shift) % entries.shape[longest]
        spots.append(tuple(where))
    return entries.at[spots[0]].set(smallest).at[spots[1]].set(largest)


def levels(stream_key, extent, shards, low, high):
    gain = 1.0
    for position, shards_of in shards:
        steps = jax.random.uniform(jax.random.fold_in(jax.random.fold_in(stream_key, 6), position), (shards_of,), jnp.float32, low / len(shards), high / len(shards))
        gain = gain * jnp.repeat(jnp.exp(steps), extent[position] // shards_of).reshape((-1,) + (1,) * (len(extent) - 1 - position))
    return gain


def bell_draw(key, shape, deviation, reach, pieces=(), kind=jnp.bfloat16):
    drawn = deviation * jax.random.normal(key, shape, jnp.float32)
    if pieces:
        drawn = drawn * levels(key, shape, pieces, -0.22, 0.18)
    return jnp.clip(drawn, -reach, reach).astype(kind)


def setup_inputs(seed: int = 0) -> dict:
    arg_keys = jax.random.split(jax.random.key(seed), 23)
    return {
        "mel": bell_draw(arg_keys[0], (CLIPS, 2 * FRAMES, MEL), 1.0, 6.0, ((0, 8), (1, 4))),
        "lang_group": with_ends(jax.random.randint(arg_keys[1], (CLIPS,), 0, GROUPS), jax.random.fold_in(arg_keys[1], 1), 0, GROUPS - 1).astype(jnp.int32),
        "clip_count": draw_clip_count(jax.random.fold_in(arg_keys[22], 71), 0),
        "conv_one": bell_draw(arg_keys[3], (3 * MEL, D), (3 * MEL) ** -0.5, 0.375, ((1, 4),)),
        "conv_one_bias": bell_draw(arg_keys[4], (D,), 0.3, 1.796875, ((0, 4),)),
        "conv_two": bell_draw(arg_keys[5], (3, D, D), (3 * D) ** -0.5, 0.125, ((1, 4),)),
        "conv_two_bias": bell_draw(arg_keys[6], (D,), 0.3, 1.796875),
        "lang_table": bell_draw(arg_keys[7], (GROUPS, D), 0.5, 3.0),
        "ln_one_gain": jnp.clip(1.0 + 0.1 * jax.random.normal(arg_keys[8], (D,), jnp.float32), 0.5, 1.5).astype(jnp.bfloat16),
        "ln_one_bias": bell_draw(arg_keys[9], (D,), 0.3, 1.796875),
        "w_qkv": bell_draw(arg_keys[10], (D, 3 * D), (D // 2) ** -0.5, 0.3125, ((0, 4),)),
        "q_bias": bell_draw(arg_keys[11], (D,), 0.3, 1.796875),
        "v_bias": bell_draw(arg_keys[12], (D,), 0.3, 1.796875),
        "w_out": bell_draw(arg_keys[13], (D, D), (D // 16) ** -0.5, 0.875, ((0, 4),)),
        "out_bias": bell_draw(arg_keys[14], (D,), 0.3, 1.796875),
        "ln_two_gain": jnp.clip(1.0 + 0.1 * jax.random.normal(arg_keys[15], (D,), jnp.float32), 0.5, 1.5).astype(jnp.bfloat16),
        "ln_two_bias": bell_draw(arg_keys[16], (D,), 0.3, 1.796875),
        "w_fc_one": bell_draw(arg_keys[17], (D, FF), D ** -0.5, 0.21875, ((0, 4),)),
        "fc_one_bias": bell_draw(arg_keys[18], (FF,), 0.3, 1.796875),
        "w_fc_two": bell_draw(arg_keys[19], (FF, D), FF ** -0.5, 0.109375, ((0, 4),)),
        "fc_two_bias": bell_draw(arg_keys[20], (D,), 0.3, 1.796875),
        "grad_out": bell_draw(arg_keys[21], (CLIPS, FRAMES, D), 1.0, 6.0, ((0, 8), (1, 4))),
    }


@jax.custom_vjp
def low(v):
    return lax.optimization_barrier(v.astype(jnp.bfloat16)).astype(jnp.float32)

@jax.custom_vjp
def low_back(v):
    return v

def low_keep(v):
    return (low(v), None)

def low_pass(kept, grad):
    return (grad,)

def back_keep(v):
    return (v, None)

def back_low(kept, grad):
    return (low(grad),)
low.defvjp(low_keep, low_pass)
low_back.defvjp(back_keep, back_low)

def matmul(left, right):
    return jnp.dot(left, right, precision=lax.Precision.HIGHEST)

def gelu_exact(inputs):
    return jax.nn.gelu(inputs, approximate=False)

def layer_norm(inputs, gain_vec, shift_vec):
    row_mean = lax.optimization_barrier(jnp.mean(inputs, axis=-1, keepdims=True))
    centered = inputs - row_mean
    variance = lax.optimization_barrier(jnp.mean(centered * centered, axis=-1, keepdims=True))
    return centered * lax.rsqrt(variance + 1e-05) * gain_vec + shift_vec

def positions(frame_count, model_width, first_frame):
    increment = math.log(10000.0) / (model_width // 2 - 1)
    inverse = jnp.exp(-increment * jnp.arange(model_width // 2, dtype=jnp.float32))
    angles = (first_frame + jnp.arange(frame_count)).astype(jnp.float32)[:, None] * inverse[None, :]
    return jnp.concatenate([jnp.sin(angles), jnp.cos(angles)], axis=1)

def cols_three(frames):
    length = frames.shape[1] - 2
    return jnp.concatenate([frames[:, 0:length], frames[:, 1:length + 1], frames[:, 2:length + 2]], axis=2)

def taps_two(frames):
    length = (frames.shape[1] - 1) // 2
    return jnp.concatenate([frames[:, 0:2 * length:2], frames[:, 1:2 * length:2], frames[:, 2:2 * length + 1:2]], axis=2)

def clip_forward(params, mel_clip, group_id, live_flag):
    conv_one, conv_one_bias, conv_two, conv_two_bias, lang_table, ln_one_gain, ln_one_bias, w_qkv, q_bias, v_bias, w_out, out_bias, ln_two_gain, ln_two_bias, w_fc_one, fc_one_bias, w_fc_two, fc_two_bias = params
    model_width = w_out.shape[0]
    padded = jnp.pad(mel_clip, ((1, 1), (0, 0)))[None]
    pre_one = low_back(matmul(cols_three(padded)[0], conv_one) + conv_one_bias)
    hid_one = low(gelu_exact(pre_one))
    hid_taps = taps_two(jnp.pad(hid_one, ((1, 0), (0, 0)))[None])[0]
    pre_two = low_back(matmul(hid_taps, conv_two.reshape(-1, model_width)) + conv_two_bias)
    lang_hot = (jnp.arange(lang_table.shape[0]) == group_id).astype(lang_table.dtype)
    stem_rows = gelu_exact(pre_two) + positions(FRAMES, model_width, 0) + matmul(lang_hot[None], lang_table)
    normed = low(layer_norm(stem_rows, ln_one_gain, ln_one_bias))
    qkv_shift = jnp.concatenate([q_bias, jnp.zeros_like(q_bias), v_bias])
    packed = low(low_back(matmul(normed, w_qkv) + qkv_shift))
    queries = packed[:, 0:model_width].reshape(FRAMES, HEADS, HEAD_DIM)
    key_rows = packed[:, model_width:2 * model_width].reshape(FRAMES, HEADS, HEAD_DIM)
    value_rows = packed[:, 2 * model_width:].reshape(FRAMES, HEADS, HEAD_DIM)
    scores = jnp.einsum('qhd,khd->hqk', queries, key_rows, precision=lax.Precision.HIGHEST)
    scores = low_back(scores * HEAD_DIM ** (-0.5))
    soft_probs = low(jax.nn.softmax(scores, axis=-1))
    attended = jnp.einsum('hqk,khd->qhd', soft_probs, value_rows, precision=lax.Precision.HIGHEST)
    attended = low(low_back(attended.reshape(FRAMES, model_width)))
    branch = low_back(matmul(attended, w_out) + out_bias)
    residual = stem_rows + branch
    normed_two = low(layer_norm(residual, ln_two_gain, ln_two_bias))
    upper_pre = low_back(matmul(normed_two, w_fc_one) + fc_one_bias)
    active = low(gelu_exact(upper_pre))
    mlp_out = low_back(matmul(active, w_fc_two) + fc_two_bias)
    return (residual + mlp_out) * live_flag

def reference(mel, lang_group, clip_count, conv_one, conv_one_bias, conv_two, conv_two_bias, lang_table, ln_one_gain, ln_one_bias, w_qkv, q_bias, v_bias, w_out, out_bias, ln_two_gain, ln_two_bias, w_fc_one, fc_one_bias, w_fc_two, fc_two_bias, grad_out):
    clip_ids = jnp.arange(CLIPS)
    live_mask = (clip_ids % SLOT_DEV < clip_count[clip_ids // SLOT_DEV]).astype(jnp.float32)
    params = tuple((weight.astype(jnp.float32) for weight in (conv_one, conv_one_bias, conv_two, conv_two_bias, lang_table, ln_one_gain, ln_one_bias, w_qkv, q_bias, v_bias, w_out, out_bias, ln_two_gain, ln_two_bias, w_fc_one, fc_one_bias, w_fc_two, fc_two_bias)))

    def forward(weights, mel_full):

        def one_clip(bundle):
            return clip_forward(weights, bundle[0], bundle[1], bundle[2])
        return lax.map(jax.checkpoint(one_clip), (mel_full, lang_group, live_mask))
    encoded, pullback = jax.vjp(forward, params, mel.astype(jnp.float32))
    weight_grads, mel_grad = pullback(grad_out.astype(jnp.float32))
    return (encoded.astype(jnp.bfloat16), mel_grad, weight_grads[0], weight_grads[1], weight_grads[2], weight_grads[3], weight_grads[4], weight_grads[5], weight_grads[6], weight_grads[7], weight_grads[8], weight_grads[9], weight_grads[10], weight_grads[11], weight_grads[12], weight_grads[13], weight_grads[14], weight_grads[15], weight_grads[16], weight_grads[17])
```

```python
import math

import jax
import jax.numpy as jnp
from jax import lax
from jax.experimental import pallas as pl
from jax.experimental.pallas import tpu as pltpu
from jax.sharding import PartitionSpec as P

HEAD_DIM = 64
PAIR = 2 * HEAD_DIM
SCALE = HEAD_DIM ** (-0.5)
BF16 = jnp.bfloat16
F32 = jnp.float32

CORE = [(j, j ^ 1) for j in range(4)]
CROSS = [(j, j ^ 2) for j in range(4)]
SAME = [(2 * x + c, 2 * c + x) for x in range(2) for c in range(2)]
OTHER = [(2 * x + c, 2 * (1 - c) + x) for x in range(2) for c in range(2)]
SAME_BACK = [(b, a) for a, b in SAME]
OTHER_BACK = [(b, a) for a, b in OTHER]


def send(block, perm):
    return lax.ppermute(block, "chan", perm)


def ordered(first_is_own, own, other, axis=0, stack=False):
    join = jnp.stack if stack else jnp.concatenate
    return jnp.where(first_is_own, join([own, other], axis), join([other, own], axis))


def pick(block, index, axis):
    return lax.dynamic_index_in_dim(block, index, axis, keepdims=False)


def gelu_both(inputs):
    cdf = 0.5 * (1.0 + lax.erf(inputs * math.sqrt(0.5)))
    pdf = jnp.exp(-0.5 * inputs * inputs) * (1.0 / math.sqrt(2.0 * math.pi))
    return inputs * cdf, cdf + inputs * pdf


def norm_stats(inputs):
    row_mean = jnp.mean(inputs, axis=-1, keepdims=True)
    centered = inputs - row_mean
    variance = jnp.mean(centered * centered, axis=-1, keepdims=True)
    return row_mean, lax.rsqrt(variance + 1e-05)


def norm_back(inputs, stats, gain_vec, cotangent):
    row_mean, inverse = stats
    unit = (inputs - row_mean) * inverse
    scaled = cotangent * gain_vec
    mean_one = jnp.mean(scaled, axis=-1, keepdims=True)
    mean_two = jnp.mean(scaled * unit, axis=-1, keepdims=True)
    grad = inverse * (scaled - mean_one - unit * mean_two)
    return grad, jnp.sum(cotangent * unit, axis=0), jnp.sum(cotangent, axis=0)


def positions(frame_count, model_width, first_frame):
    increment = math.log(10000.0) / (model_width // 2 - 1)
    inverse = jnp.exp(-increment * jnp.arange(model_width // 2, dtype=jnp.float32))
    angles = (first_frame + jnp.arange(frame_count)).astype(jnp.float32)[:, None] * inverse[None, :]
    return jnp.concatenate([jnp.sin(angles), jnp.cos(angles)], axis=1)


def mm(left, right):
    return jnp.dot(left, right, preferred_element_type=F32)


def mm_nt(left, right):
    return lax.dot_general(left, right, (((1,), (1,)), ((), ())), preferred_element_type=F32)


def mm_tn(left, right):
    return lax.dot_general(left, right, (((0,), (0,)), ((), ())), preferred_element_type=F32)


def head_stack(block):
    lane = lax.broadcasted_iota(jnp.int32, block.shape, 1)
    zero = jnp.zeros_like(block)
    return jnp.concatenate(
        [jnp.where(lane < HEAD_DIM, block, zero), jnp.where(lane < HEAD_DIM, zero, block)], axis=0
    )


def head_join(stacked):
    rows = stacked.shape[0] // 2
    lane = lax.broadcasted_iota(jnp.int32, (rows, stacked.shape[1]), 1)
    return jnp.where(lane < HEAD_DIM, stacked[:rows], stacked[rows:])


def attend_kernel(chunk, q_ref, k_own, k_oth, v_own, v_oth, att_ref, lse_ref, k_all, v_all):
    rows = q_ref.shape[0]
    k_all[0:rows] = k_own[...]
    k_all[rows:] = k_oth[...]
    v_all[0:rows] = v_own[...]
    v_all[rows:] = v_oth[...]

    @pl.loop(0, rows // chunk)
    def _(step):
        at = pl.ds(pl.multiple_of(step * chunk, chunk), chunk)
        queries = head_stack(q_ref[at] * SCALE)
        scores = mm_nt(queries, k_all[...])
        top = jnp.max(scores, axis=1, keepdims=True)
        weights = jnp.exp(scores - top)
        total = jnp.sum(weights, axis=1, keepdims=True)
        out = mm(weights.astype(BF16), v_all[...]) / total
        att_ref[at] = head_join(out).astype(BF16)
        lse_ref[at] = head_join(jnp.broadcast_to(top + jnp.log(total), out.shape))


def attend(q, kv_own, kv_oth, heads):
    rows = q.shape[0]
    pairs = heads // 2
    chunk = 176
    spec = lambda shift: pl.BlockSpec((rows, PAIR), lambda p: (0, p + shift))
    return pl.pallas_call(
        lambda *refs: attend_kernel(chunk, *refs),
        grid=(pairs,),
        in_specs=[spec(0), spec(0), spec(0), spec(pairs), spec(pairs)],
        out_specs=[spec(0), spec(0)],
        out_shape=[
            jax.ShapeDtypeStruct((rows, pairs * PAIR), BF16),
            jax.ShapeDtypeStruct((rows, pairs * PAIR), F32),
        ],
        scratch_shapes=[pltpu.VMEM((2 * rows, PAIR), BF16)] * 2,
        compiler_params=pltpu.CompilerParams(vmem_limit_bytes=48 * 1024 * 1024),
        cost_estimate=pl.CostEstimate(
            flops=pairs * 16 * rows * rows * PAIR,
            bytes_accessed=pairs * PAIR * rows * 16,
            transcendentals=4 * pairs * rows * rows,
        ),
        name="attend",
    )(q, kv_own, kv_oth, kv_own, kv_oth)


def attend_back_kernel(
    chunk,
    q_ref, k_own, k_oth, v_own, v_oth, lse_ref, g_ref,
    dq_ref, dk_own, dk_oth, dv_own, dv_oth,
    k_all, v_all, q_all, g_all, p_all, s_all,
):
    rows = q_ref.shape[0]
    k_all[0:rows] = k_own[...]
    k_all[rows:] = k_oth[...]
    v_all[0:rows] = v_own[...]
    v_all[rows:] = v_oth[...]

    @pl.loop(0, rows // chunk)
    def _(step):
        at = pl.ds(pl.multiple_of(step * chunk, chunk), chunk)
        both = pl.ds(pl.multiple_of(2 * step * chunk, 2 * chunk), 2 * chunk)
        queries = head_stack(q_ref[at] * SCALE)
        grads = head_stack(g_ref[at])
        q_all[both] = queries
        g_all[both] = grads
        lse = jnp.concatenate([lse_ref[at, 0:1], lse_ref[at, HEAD_DIM : HEAD_DIM + 1]], axis=0)
        probs = jnp.exp(mm_nt(queries, k_all[...]) - lse)
        grad_probs = mm_nt(grads, v_all[...])
        inner = jnp.sum(probs * grad_probs, axis=1, keepdims=True)
        grad_scores = (probs * (grad_probs - inner)).astype(BF16)
        p_all[both] = probs.astype(BF16)
        s_all[both] = grad_scores
        dq_ref[at] = (head_join(mm(grad_scores, k_all[...])) * SCALE).astype(BF16)

    dv = mm_tn(g_all[...], p_all[...]).T.astype(BF16)
    dv_own[...] = dv[0:rows]
    dv_oth[...] = dv[rows:]
    dk = mm_tn(q_all[...], s_all[...]).T.astype(BF16)
    dk_own[...] = dk[0:rows]
    dk_oth[...] = dk[rows:]


def attend_back(q, kv_own, kv_oth, lse, grad_att, heads):
    rows = q.shape[0]
    pairs = heads // 2
    chunk = 176
    spec = lambda shift: pl.BlockSpec((rows, PAIR), lambda p: (0, p + shift))
    shape = jax.ShapeDtypeStruct((rows, pairs * PAIR), BF16)
    return pl.pallas_call(
        lambda *refs: attend_back_kernel(chunk, *refs),
        grid=(pairs,),
        in_specs=[spec(0), spec(0), spec(0), spec(pairs), spec(pairs), spec(0), spec(0)],
        out_specs=[spec(0)] * 5,
        out_shape=[shape] * 5,
        scratch_shapes=[pltpu.VMEM((2 * rows, PAIR), BF16)] * 4
        + [pltpu.VMEM((2 * rows, 2 * rows), BF16)] * 2,
        compiler_params=pltpu.CompilerParams(vmem_limit_bytes=48 * 1024 * 1024),
        cost_estimate=pl.CostEstimate(
            flops=pairs * 40 * rows * rows * PAIR,
            bytes_accessed=pairs * PAIR * rows * 26,
            transcendentals=4 * pairs * rows * rows,
        ),
        name="attend_back",
    )(q, kv_own, kv_oth, kv_own, kv_oth, lse, grad_att)


def gather_rows(part, x, c, axis=0):
    across = send(part, CROSS)
    column = ordered(x == 0, part, across, axis, stack=True)
    beside = send(column, CORE)
    whole = ordered(c == 0, column, beside, axis + 1, stack=True)
    shape = list(part.shape)
    shape[axis] *= 4
    return whole.reshape(shape)


def round_sum(*terms):
    return sum(term.astype(F32) for term in terms).astype(BF16)


def share_rows(make, x, c):
    beside = send(make(1 - c).astype(BF16), CORE)
    column = (make(c) + beside.astype(F32)).astype(BF16)
    across = send(pick(column, 1 - x, 0), CROSS)
    return round_sum(pick(column, x, 0), across)


def sum_dp(share):
    count = lax.axis_size("dp")
    index = lax.axis_index("dp")
    bits = []
    step = 1
    while step < count:
        bits.append(step)
        step *= 2
    for bit in bits:
        side = (index // bit) % 2
        halves = share.reshape((2, share.shape[0] // 2) + share.shape[1:])
        perm = [(d, d ^ bit) for d in range(count)]
        arrived = lax.ppermute(pick(halves, 1 - side, 0), "dp", perm)
        share = round_sum(pick(halves, side, 0), arrived)
    for bit in reversed(bits):
        side = (index // bit) % 2
        perm = [(d, d ^ bit) for d in range(count)]
        arrived = lax.ppermute(share, "dp", perm)
        share = ordered(side == 0, share, arrived)
    return share


def on_device(
    mel,
    lang_group,
    clip_count,
    conv_one,
    conv_one_bias,
    conv_two,
    conv_two_bias,
    lang_table,
    ln_one_gain,
    ln_one_bias,
    w_qkv,
    q_bias,
    v_bias,
    w_out,
    out_bias,
    ln_two_gain,
    ln_two_bias,
    w_fc_one,
    fc_one_bias,
    w_fc_two,
    fc_two_bias,
    grad_out,
):
    slots, part, width = grad_out.shape
    heads = width // HEAD_DIM
    mels = mel.shape[2]
    rows = slots * part
    j = lax.axis_index("chan")
    x, c = j // 2, j % 2
    live = (x < clip_count[lax.axis_index("dp")]).astype(F32)

    def to_clip(block):
        same = send(pick(block, c, 0), SAME)
        other = send(pick(block, 1 - c, 0), OTHER)
        return ordered(x == 0, same, other)

    def from_clip(block):
        half = block.shape[0] // 2
        first, second = block[:half], block[half:]
        same = send(jnp.where(x == 0, first, second), SAME_BACK)
        other = send(jnp.where(x == 0, second, first), OTHER_BACK)
        return ordered(c == 0, same, other, stack=True)

    mel_pairs = mel.reshape(slots, part, 2 * mels)
    edge = send(jnp.where(j == 1, mel_pairs[1, -1], mel_pairs[0, 0]), [(1, 3), (2, 0)])
    edge = jnp.where(j == 1, mel_pairs[0, -1], jnp.where(j == 2, mel_pairs[1, 0], edge))
    zero_edge = jnp.zeros_like(edge)
    mel_own = jnp.concatenate(
        [
            jnp.where(c == 1, edge, zero_edge)[None],
            to_clip(mel_pairs),
            jnp.where(c == 0, edge, zero_edge)[None],
        ]
    )
    bias_full = gather_rows(conv_one_bias, x, c)
    one_full = gather_rows(conv_one, x, c, axis=1)
    two_full = gather_rows(conv_two, x, c, axis=1).reshape(-1, width)
    qkv_full = gather_rows(w_qkv, x, c)
    out_full = gather_rows(w_out, x, c)
    up_full = gather_rows(w_fc_one, x, c)
    down_full = gather_rows(w_fc_two, x, c)
    cotangent = to_clip(grad_out)

    even, odd = mel_own[:, :mels], mel_own[:, mels:]
    cols_even = jnp.concatenate(
        [odd[0:rows], even[1 : rows + 1], odd[1 : rows + 1]], axis=1
    )
    cols_odd = jnp.concatenate(
        [even[1 : rows + 1], odd[1 : rows + 1], even[2 : rows + 2]], axis=1
    )
    cols_edge = jnp.concatenate([even[0:1], odd[0:1], even[1:2]], axis=1)
    shift = bias_full.astype(F32)
    hid_even, slope_even = gelu_both(mm(cols_even, one_full) + shift)
    hid_odd, slope_odd = gelu_both(mm(cols_odd, one_full) + shift)
    hid_edge, _ = gelu_both(mm(cols_edge, one_full) + shift)
    hid_edge = jnp.where(c == 1, hid_edge, 0.0)
    hid_even, hid_odd, hid_edge = hid_even.astype(BF16), hid_odd.astype(BF16), hid_edge.astype(BF16)
    slope_even, slope_odd = slope_even.astype(BF16), slope_odd.astype(BF16)
    hid_prev = jnp.concatenate([hid_edge, hid_odd[:-1]])
    hid_taps = jnp.concatenate([hid_prev, hid_even, hid_odd], axis=1)
    stem_act, slope_two = gelu_both(mm(hid_taps, two_full) + conv_two_bias.astype(F32))
    slope_two = slope_two.astype(BF16)
    group = pick(lang_group, x, 0)
    stem = stem_act + positions(rows, width, c * rows) + pick(lang_table, group, 0).astype(F32)[None]

    gain_one, gain_two = ln_one_gain.astype(F32), ln_two_gain.astype(F32)
    stats_one = norm_stats(stem)
    normed = (
        (stem - stats_one[0]) * stats_one[1] * gain_one + ln_one_bias.astype(F32)
    ).astype(BF16)
    kv_shift = jnp.concatenate([jnp.zeros((width,), F32), v_bias.astype(F32)])
    kv_own = (mm(normed, qkv_full[:, width:]) + kv_shift).astype(BF16)
    kv_oth = send(kv_own, CORE)
    queries = (mm(normed, qkv_full[:, :width]) + q_bias.astype(F32)).astype(BF16)
    attended, lse = attend(queries, kv_own, kv_oth, heads)
    residual = stem + mm(attended, out_full) + out_bias.astype(F32)

    stats_two = norm_stats(residual)
    normed_two = (
        (residual - stats_two[0]) * stats_two[1] * gain_two + ln_two_bias.astype(F32)
    ).astype(BF16)
    active, slope_up = gelu_both(mm(normed_two, up_full) + fc_one_bias.astype(F32))
    active, slope_up = active.astype(BF16), slope_up.astype(BF16)
    encoded = (residual + mm(active, down_full) + fc_two_bias.astype(F32)) * live
    encoded = from_clip(encoded.astype(BF16))

    def weight_grad(left, right):
        split = left.reshape(left.shape[0], 2, 2, left.shape[1] // 4)

        def make(core):
            half = pick(split, core, 2).reshape(left.shape[0], -1)
            return mm_tn(half, right).reshape(2, -1, right.shape[1])

        return share_rows(make, x, c)

    grad_mlp = (cotangent.astype(F32) * live).astype(BF16)
    grad_rows = grad_mlp.astype(F32)
    down_share = weight_grad(active, grad_mlp)
    down_shift = jnp.sum(grad_rows, axis=0)
    grad_upper = (mm_nt(grad_mlp, down_full) * slope_up.astype(F32)).astype(BF16)
    up_share = weight_grad(normed_two, grad_upper)
    up_shift = jnp.sum(grad_upper.astype(F32), axis=0)
    grad_norm, grad_gain_two, grad_shift_two = norm_back(
        residual, stats_two, gain_two, mm_nt(grad_upper, up_full)
    )
    grad_residual = grad_rows + grad_norm
    grad_branch = grad_residual.astype(BF16)
    out_share = weight_grad(attended, grad_branch)
    out_shift = jnp.sum(grad_branch.astype(F32), axis=0)
    grad_att = mm_nt(grad_branch, out_full).astype(BF16)
    grad_q, dk_own, dk_oth, dv_own, dv_oth = attend_back(
        queries, kv_own, kv_oth, lse, grad_att, heads
    )
    grad_k = round_sum(dk_own, send(dk_oth, CORE))
    grad_v = round_sum(dv_own, send(dv_oth, CORE))
    grad_packed = jnp.concatenate([grad_q, grad_k, grad_v], axis=1)
    qkv_share = weight_grad(normed, grad_packed)
    q_shift = jnp.sum(grad_q.astype(F32), axis=0)
    v_shift = jnp.sum(grad_v.astype(F32), axis=0)
    grad_norm, grad_gain_one, grad_shift_one = norm_back(
        stem, stats_one, gain_one, mm_nt(grad_packed, qkv_full)
    )
    grad_stem = grad_residual + grad_norm
    group_hot = (jnp.arange(lang_table.shape[0]) == group).astype(F32)
    grad_lang = group_hot[:, None] * jnp.sum(grad_stem, axis=0)[None]
    grad_two = (grad_stem * slope_two.astype(F32)).astype(BF16)
    two_shift = jnp.sum(grad_two.astype(F32), axis=0)
    follow = send(grad_two[0:1], [(1, 0), (3, 2)])
    grad_next = jnp.concatenate([grad_two[1:], follow])

    taps = hid_taps.reshape(rows, 3, 2, 2, width // 4)

    def make_two(core):
        half = pick(taps, core, 3).reshape(rows, -1)
        grads = mm_tn(half, grad_two).reshape(3, 2, width // 4, width)
        return jnp.moveaxis(grads, 1, 0)

    two_share = share_rows(make_two, x, c).reshape(-1, width)
    hid_grad_even = mm_nt(grad_two, two_full[width : 2 * width])
    hid_grad_odd = mm_nt(grad_two, two_full[2 * width :]) + mm_nt(grad_next, two_full[:width])
    grad_even = (hid_grad_even * slope_even.astype(F32)).astype(BF16)
    grad_odd = (hid_grad_odd * slope_odd.astype(F32)).astype(BF16)
    one_shift = jnp.sum(grad_even.astype(F32), axis=0) + jnp.sum(grad_odd.astype(F32), axis=0)

    split_even = grad_even.reshape(rows, 2, 2, width // 4)
    split_odd = grad_odd.reshape(rows, 2, 2, width // 4)

    def make_one(core):
        half_even = pick(split_even, core, 2).reshape(rows, -1)
        half_odd = pick(split_odd, core, 2).reshape(rows, -1)
        grads = mm_tn(half_even, cols_even) + mm_tn(half_odd, cols_odd)
        return grads.reshape(2, width // 4, 3 * mels)

    one_share = share_rows(make_one, x, c)
    terms_even = mm_nt(grad_even, one_full)
    terms_odd = mm_nt(grad_odd, one_full)
    before, mid_e, after = terms_even[:, :mels], terms_even[:, mels : 2 * mels], terms_even[:, 2 * mels :]
    first_o, mid_o, last_o = terms_odd[:, :mels], terms_odd[:, mels : 2 * mels], terms_odd[:, 2 * mels :]
    spill = send(jnp.where(c == 0, last_o[-1:], before[0:1]), CORE)
    zero_spill = jnp.zeros_like(spill)
    last_prev = jnp.concatenate([jnp.where(c == 1, spill, zero_spill), last_o[:-1]])
    before_next = jnp.concatenate([before[1:], jnp.where(c == 0, spill, zero_spill)])
    mel_grad = jnp.concatenate([mid_e + first_o + last_prev, after + mid_o + before_next], axis=1)
    mel_grad = from_clip(mel_grad.astype(BF16)).astype(F32).reshape(slots, 2 * part, mels)

    down_sum = sum_dp(down_share)
    up_sum = sum_dp(up_share)
    out_sum = sum_dp(out_share)
    qkv_sum = sum_dp(qkv_share)
    two_sum = sum_dp(two_share)
    one_sum = sum_dp(one_share)
    early = lax.psum(
        jnp.concatenate([down_shift, up_shift, grad_gain_two, grad_shift_two, out_shift]),
        ("dp", "chan"),
    )
    late = lax.psum(
        jnp.concatenate(
            [
                q_shift, v_shift, grad_gain_one, grad_shift_one, two_shift, one_shift,
                grad_lang.reshape(-1),
            ]
        ),
        ("dp", "chan"),
    )
    up_end = width + up_shift.shape[0]
    vec = lambda packed, start: packed[start : start + width]
    return (
        encoded,
        mel_grad,
        one_sum.astype(F32).T,
        lax.dynamic_slice_in_dim(vec(late, 5 * width), j * (width // 4), width // 4),
        two_sum.astype(F32).reshape(conv_two.shape),
        vec(late, 4 * width),
        late[6 * width :].reshape(lang_table.shape),
        vec(late, 2 * width),
        vec(late, 3 * width),
        qkv_sum.astype(F32),
        vec(late, 0),
        vec(late, width),
        out_sum.astype(F32),
        vec(early, up_end + 2 * width),
        vec(early, up_end),
        vec(early, up_end + width),
        up_sum.astype(F32),
        early[width:up_end],
        down_sum.astype(F32),
        vec(early, 0),
    )


def solution(mesh):
    in_specs = (
        P("dp", "chan", None),
        P("dp"),
        P(),
        P(None, "chan"),
        P("chan"),
        P(None, "chan", None),
        P(),
        P(),
        P(),
        P(),
        P("chan", None),
        P(),
        P(),
        P("chan", None),
        P(),
        P(),
        P(),
        P("chan", None),
        P(),
        P("chan", None),
        P(),
        P("dp", "chan", None),
    )
    out_specs = (
        P("dp", "chan", None),
        P("dp", "chan", None),
        P(None, "chan"),
        P("chan"),
        P(None, "chan", None),
        P(),
        P(),
        P(),
        P(),
        P("chan", None),
        P(),
        P(),
        P("chan", None),
        P(),
        P(),
        P(),
        P("chan", None),
        P(),
        P("chan", None),
        P(),
    )
    return jax.shard_map(
        on_device, mesh=mesh, in_specs=in_specs, out_specs=out_specs, check_vma=False
    )
```

```python
import math

import jax
import jax.numpy as jnp
from jax import lax
from jax.experimental import pallas as pl
from jax.experimental.pallas import tpu as pltpu
from jax.sharding import PartitionSpec as P

HEAD_DIM = 64
PAIR = 2 * HEAD_DIM
SCALE = HEAD_DIM ** (-0.5)
BF16 = jnp.bfloat16
F32 = jnp.float32

CORE = [(j, j ^ 1) for j in range(4)]
CROSS = [(j, j ^ 2) for j in range(4)]
SAME = [(2 * x + c, 2 * c + x) for x in range(2) for c in range(2)]
OTHER = [(2 * x + c, 2 * (1 - c) + x) for x in range(2) for c in range(2)]
SAME_BACK = [(b, a) for a, b in SAME]
OTHER_BACK = [(b, a) for a, b in OTHER]


def send(block, perm):
    return lax.ppermute(block, "chan", perm)


def ordered(first_is_own, own, other, axis=0, stack=False):
    join = jnp.stack if stack else jnp.concatenate
    return jnp.where(first_is_own, join([own, other], axis), join([other, own], axis))


def pick(block, index, axis):
    return lax.dynamic_index_in_dim(block, index, axis, keepdims=False)


def gelu_both(inputs):
    cdf = 0.5 * (1.0 + lax.erf(inputs * math.sqrt(0.5)))
    pdf = jnp.exp(-0.5 * inputs * inputs) * (1.0 / math.sqrt(2.0 * math.pi))
    return inputs * cdf, cdf + inputs * pdf


def norm_stats(inputs):
    row_mean = jnp.mean(inputs, axis=-1, keepdims=True)
    centered = inputs - row_mean
    variance = jnp.mean(centered * centered, axis=-1, keepdims=True)
    return row_mean, lax.rsqrt(variance + 1e-05)


def norm_back(inputs, stats, gain_vec, cotangent):
    row_mean, inverse = stats
    unit = (inputs - row_mean) * inverse
    scaled = cotangent * gain_vec
    mean_one = jnp.mean(scaled, axis=-1, keepdims=True)
    mean_two = jnp.mean(scaled * unit, axis=-1, keepdims=True)
    grad = inverse * (scaled - mean_one - unit * mean_two)
    return grad, jnp.sum(cotangent * unit, axis=0), jnp.sum(cotangent, axis=0)


def positions(frame_count, model_width, first_frame):
    increment = math.log(10000.0) / (model_width // 2 - 1)
    inverse = jnp.exp(-increment * jnp.arange(model_width // 2, dtype=jnp.float32))
    angles = (first_frame + jnp.arange(frame_count)).astype(jnp.float32)[:, None] * inverse[None, :]
    return jnp.concatenate([jnp.sin(angles), jnp.cos(angles)], axis=1)


def mm(left, right):
    return jnp.dot(left, right, preferred_element_type=F32)


def mm_nt(left, right):
    return lax.dot_general(left, right, (((1,), (1,)), ((), ())), preferred_element_type=F32)


def mm_tn(left, right):
    return lax.dot_general(left, right, (((0,), (0,)), ((), ())), preferred_element_type=F32)


def head_stack(block):
    lane = lax.broadcasted_iota(jnp.int32, block.shape, 1)
    zero = jnp.zeros_like(block)
    return jnp.concatenate(
        [jnp.where(lane < HEAD_DIM, block, zero), jnp.where(lane < HEAD_DIM, zero, block)], axis=0
    )


def head_join(stacked):
    rows = stacked.shape[0] // 2
    lane = lax.broadcasted_iota(jnp.int32, (rows, stacked.shape[1]), 1)
    return jnp.where(lane < HEAD_DIM, stacked[:rows], stacked[rows:])


def attend_kernel(chunk, q_ref, k_own, k_oth, v_own, v_oth, *refs):
    att_ref, lse_ref, k_all, v_all = refs[-4:]
    rows = q_ref.shape[0]
    k_all[0:rows] = k_own[...]
    k_all[rows:] = k_oth[...]
    v_all[0:rows] = v_own[...]
    v_all[rows:] = v_oth[...]

    @pl.loop(0, rows // chunk)
    def _(step):
        at = pl.ds(pl.multiple_of(step * chunk, chunk), chunk)
        queries = head_stack(q_ref[at] * SCALE)
        scores = mm_nt(queries, k_all[...])
        top = jnp.max(scores, axis=1, keepdims=True)
        weights = jnp.exp(scores - top)
        total = jnp.sum(weights, axis=1, keepdims=True)
        out = mm(weights.astype(BF16), v_all[...]) / total
        att_ref[at] = head_join(out).astype(BF16)
        lse_ref[at] = head_join(jnp.broadcast_to(top + jnp.log(total), out.shape))


def attend(q, kv_own, kv_oth, first, count, pairs, earlier=()):
    rows = q.shape[0]
    chunk = 176
    spec = lambda shift: pl.BlockSpec((rows, PAIR), lambda p: (0, p + shift))
    return pl.pallas_call(
        lambda *refs: attend_kernel(chunk, *refs),
        grid=(count,),
        in_specs=[spec(first), spec(first), spec(first), spec(first + pairs), spec(first + pairs)]
        + [pl.BlockSpec(memory_space=pl.ANY)] * len(earlier),
        out_specs=[spec(first)] * 2,
        out_shape=[
            jax.ShapeDtypeStruct((rows, pairs * PAIR), BF16),
            jax.ShapeDtypeStruct((rows, pairs * PAIR), F32),
        ],
        input_output_aliases={5 + i: i for i in range(len(earlier))},
        scratch_shapes=[pltpu.VMEM((2 * rows, PAIR), BF16)] * 2,
        compiler_params=pltpu.CompilerParams(vmem_limit_bytes=40 * 1024 * 1024),
        cost_estimate=pl.CostEstimate(
            flops=count * 32 * rows * rows * PAIR,
            bytes_accessed=count * PAIR * rows * 16,
            transcendentals=4 * count * rows * rows,
        ),
        name="attend",
    )(q, kv_own, kv_oth, kv_own, kv_oth, *earlier)


def attend_back_kernel(chunk, q_ref, k_own, k_oth, v_own, v_oth, lse_ref, g_ref, *refs):
    dq_ref, own_ref, oth_ref, k_all, v_all, q_all, g_all, p_all, s_all = refs[-9:]
    rows = q_ref.shape[0]
    k_all[0:rows] = k_own[...]
    k_all[rows:] = k_oth[...]
    v_all[0:rows] = v_own[...]
    v_all[rows:] = v_oth[...]

    @pl.loop(0, rows // chunk)
    def _(step):
        at = pl.ds(pl.multiple_of(step * chunk, chunk), chunk)
        both = pl.ds(pl.multiple_of(2 * step * chunk, 2 * chunk), 2 * chunk)
        queries = head_stack(q_ref[at] * SCALE)
        grads = head_stack(g_ref[at])
        q_all[both] = queries
        g_all[both] = grads
        lse = jnp.concatenate([lse_ref[at, 0:1], lse_ref[at, HEAD_DIM : HEAD_DIM + 1]], axis=0)
        probs = jnp.exp(mm_nt(queries, k_all[...]) - lse)
        grad_probs = mm_nt(grads, v_all[...])
        inner = jnp.sum(probs * grad_probs, axis=1, keepdims=True)
        grad_scores = (probs * (grad_probs - inner)).astype(BF16)
        p_all[both] = probs.astype(BF16)
        s_all[both] = grad_scores
        dq_ref[at] = (head_join(mm(grad_scores, k_all[...])) * SCALE).astype(BF16)

    dk = mm_tn(q_all[...], s_all[...]).T.astype(BF16)
    own_ref[0] = dk[0:rows]
    oth_ref[0] = dk[rows:]
    dv = mm_tn(g_all[...], p_all[...]).T.astype(BF16)
    own_ref[1] = dv[0:rows]
    oth_ref[1] = dv[rows:]


def attend_back(q, kv_own, kv_oth, lse, grad_att, first, count, pairs, earlier=()):
    rows = q.shape[0]
    chunk = 176
    spec = lambda shift: pl.BlockSpec((rows, PAIR), lambda p: (0, p + shift))
    two = pl.BlockSpec((2, rows, PAIR), lambda p: (0, 0, p + first))
    both = jax.ShapeDtypeStruct((2, rows, pairs * PAIR), BF16)
    return pl.pallas_call(
        lambda *refs: attend_back_kernel(chunk, *refs),
        grid=(count,),
        in_specs=[spec(first), spec(first), spec(first), spec(first + pairs), spec(first + pairs)]
        + [spec(first)] * 2
        + [pl.BlockSpec(memory_space=pl.ANY)] * len(earlier),
        out_specs=[spec(first), two, two],
        out_shape=[jax.ShapeDtypeStruct((rows, pairs * PAIR), BF16), both, both],
        input_output_aliases={7 + i: i for i in range(len(earlier))},
        scratch_shapes=[pltpu.VMEM((2 * rows, PAIR), BF16)] * 4
        + [pltpu.VMEM((2 * rows, 2 * rows), BF16)] * 2,
        compiler_params=pltpu.CompilerParams(vmem_limit_bytes=40 * 1024 * 1024),
        cost_estimate=pl.CostEstimate(
            flops=count * 80 * rows * rows * PAIR,
            bytes_accessed=count * PAIR * rows * 26,
            transcendentals=4 * count * rows * rows,
        ),
        name="attend_back",
    )(q, kv_own, kv_oth, kv_own, kv_oth, lse, grad_att, *earlier)


def join(*values):
    return lax.optimization_barrier(values)


def after(value, *others):
    return lax.optimization_barrier((value,) + others)[0]


def place_kernel(moves, index_ref, *refs):
    whole, sems = refs[-2:]
    j = index_ref[0]
    x, c = j // 2, j % 2
    owners = [2 * x + c, 2 * (1 - x) + c, 2 * x + 1 - c, 2 * (1 - x) + 1 - c]
    copies = []
    for part, owner in zip(refs[:4], owners):
        for source, target in moves:
            copies.append(
                pltpu.make_async_copy(source(part), target(whole, owner), sems.at[len(copies)])
            )
    for copy in copies:
        copy.start()
    for copy in copies:
        copy.wait()


def place(j, parts, moves, shape):
    anywhere = pl.BlockSpec(memory_space=pl.ANY)
    return pl.pallas_call(
        lambda *refs: place_kernel(moves, *refs),
        in_specs=[pl.BlockSpec(memory_space=pltpu.SMEM)] + [anywhere] * 4,
        out_specs=pl.BlockSpec(memory_space=pltpu.VMEM),
        out_shape=jax.ShapeDtypeStruct(shape, BF16),
        scratch_shapes=[pltpu.SemaphoreType.DMA((4 * len(moves),))],
        compiler_params=pltpu.CompilerParams(vmem_limit_bytes=16 * 1024 * 1024),
        cost_estimate=pl.CostEstimate(
            flops=0, bytes_accessed=4 * math.prod(shape), transcendentals=0
        ),
        name="place",
    )(j.reshape(1), *parts)


def row_moves(first, rows):
    def target(whole, owner):
        return whole.at[pl.ds(pl.multiple_of(owner * rows, rows), rows)]

    return [(lambda part: part.at[pl.ds(first, rows)], target)]


def block_moves(first, rows, blocks, width):
    moves = []
    for block in range(blocks):

        def source(part, block=block):
            return part.at[pl.ds(first + block * rows, rows)]

        def target(whole, owner, block=block):
            at = pl.ds(pl.multiple_of(owner * rows, rows), rows)
            return whole.at[at, pl.ds(block * width, width)]

        moves.append((source, target))
    return moves


def tap_moves(rows):
    def target(whole, owner):
        return whole.at[:, pl.ds(pl.multiple_of(owner * rows, rows), rows)]

    return [(lambda part: part, target)]


def round_sum(*terms):
    return sum(term.astype(F32) for term in terms).astype(BF16)


def dp_step(share, bit):
    count = lax.axis_size("dp")
    side = (lax.axis_index("dp") // bit) % 2
    halves = share.reshape((2, share.shape[0] // 2) + share.shape[1:])
    perm = [(d, d ^ bit) for d in range(count)]
    arrived = lax.ppermute(pick(halves, 1 - side, 0), "dp", perm)
    return round_sum(pick(halves, side, 0), arrived)


def dp_back(share, bit):
    count = lax.axis_size("dp")
    side = (lax.axis_index("dp") // bit) % 2
    arrived = lax.ppermute(share, "dp", [(d, d ^ bit) for d in range(count)])
    return ordered(side == 0, share, arrived)


def dp_bits():
    bits = [1]
    while 2 * bits[-1] < lax.axis_size("dp"):
        bits.append(2 * bits[-1])
    return bits


def dp_moves():
    bits = dp_bits()
    steps = [lambda v, bit=bit: dp_step(v, bit) for bit in bits]
    return steps + [lambda v, bit=bit: dp_back(v, bit) for bit in reversed(bits)]


def total_moves():
    def over(axis, perm):
        return lambda v: v + lax.ppermute(v, axis, perm)

    count = lax.axis_size("dp")
    return [over("chan", CORE), over("chan", CROSS)] + [
        over("dp", [(d, d ^ bit) for d in range(count)]) for bit in dp_bits()
    ]


class Chain:
    def __init__(self, value, moves):
        self.value, self.moves = value, list(moves)

    def step(self):
        if self.moves:
            self.value = self.moves.pop(0)(self.value)


def slot(chains, steps, *main):
    joined = join(*[chain.value for chain in chains], *main)
    for chain, value in zip(chains, joined):
        chain.value = value
    for chain in steps:
        chain.step()
    main = joined[len(chains) :]
    return main[0] if len(main) == 1 else main


def on_device(
    mel,
    lang_group,
    clip_count,
    conv_one,
    conv_one_bias,
    conv_two,
    conv_two_bias,
    lang_table,
    ln_one_gain,
    ln_one_bias,
    w_qkv,
    q_bias,
    v_bias,
    w_out,
    out_bias,
    ln_two_gain,
    ln_two_bias,
    w_fc_one,
    fc_one_bias,
    w_fc_two,
    fc_two_bias,
    grad_out,
):
    slots, part, width = grad_out.shape
    hidden = w_fc_one.shape[1]
    pairs = width // PAIR
    quarter = width // 4
    mels = mel.shape[2]
    rows = slots * part
    j = lax.axis_index("chan")
    x, c = j // 2, j % 2
    live = (x < clip_count[lax.axis_index("dp")]).astype(F32)

    def to_clip(block):
        same = send(pick(block, c, 0), SAME)
        other = send(pick(block, 1 - c, 0), OTHER)
        return ordered(x == 0, same, other)

    def from_clip(block):
        half = block.shape[0] // 2
        first, second = block[:half], block[half:]
        same = send(jnp.where(x == 0, first, second), SAME_BACK)
        other = send(jnp.where(x == 0, second, first), OTHER_BACK)
        return ordered(c == 0, same, other, stack=True)

    mel_pairs = mel.reshape(slots, part, 2 * mels)
    edge = send(jnp.where(j == 1, mel_pairs[1, -1], mel_pairs[0, 0]), [(1, 3), (2, 0)])
    edge = jnp.where(j == 1, mel_pairs[0, -1], jnp.where(j == 2, mel_pairs[1, 0], edge))
    zero_edge = jnp.zeros_like(edge)
    mel_own = jnp.concatenate(
        [
            jnp.where(c == 1, edge, zero_edge)[None],
            to_clip(mel_pairs),
            jnp.where(c == 0, edge, zero_edge)[None],
        ]
    )

    one_part = jnp.concatenate([conv_one, conv_one_bias[None]])
    one_across = send(one_part, CROSS)
    one_column = ordered(x == 0, one_part, one_across, 1, stack=True)
    one_whole = ordered(c == 0, one_column, send(one_column, CORE), 2, stack=True)
    one_whole = one_whole.reshape(one_part.shape[0], width)
    one_full, one_bias = one_whole[: 3 * mels], one_whole[3 * mels].astype(F32)

    blocks = hidden // width
    up_part = jnp.concatenate(
        [w_out] + [w_fc_one[:, k * width : (k + 1) * width] for k in range(blocks)]
    )
    two_across = send(conv_two, CROSS)
    qkv_across = send(after(w_qkv, two_across), CROSS)
    up_across = send(after(up_part, qkv_across), CROSS)
    down_across = send(after(w_fc_two, up_across), CROSS)

    def parts_of(own, across):
        return own, across, send(own, CORE), send(across, CORE)

    two_full = place(
        j, parts_of(conv_two, two_across), tap_moves(quarter), (3, width, width)
    ).reshape(-1, width)
    qkv_full = place(
        j, parts_of(w_qkv, qkv_across), row_moves(0, quarter), (width, 3 * width)
    )

    even, odd = mel_own[:, :mels], mel_own[:, mels:]
    cols_even = jnp.concatenate([odd[0:rows], even[1 : rows + 1], odd[1 : rows + 1]], axis=1)
    cols_odd = jnp.concatenate(
        [even[1 : rows + 1], odd[1 : rows + 1], even[2 : rows + 2]], axis=1
    )
    cols_edge = jnp.concatenate([even[0:1], odd[0:1], even[1:2]], axis=1)
    hid_even, slope_even = gelu_both(mm(cols_even, one_full) + one_bias)
    hid_odd, slope_odd = gelu_both(mm(cols_odd, one_full) + one_bias)
    hid_edge, _ = gelu_both(mm(cols_edge, one_full) + one_bias)
    hid_edge = jnp.where(c == 1, hid_edge, 0.0)
    hid_even, hid_odd, hid_edge = hid_even.astype(BF16), hid_odd.astype(BF16), hid_edge.astype(BF16)
    slope_even, slope_odd = slope_even.astype(BF16), slope_odd.astype(BF16)
    hid_prev = jnp.concatenate([hid_edge, hid_odd[:-1]])
    hid_taps = jnp.concatenate([hid_prev, hid_even, hid_odd], axis=1)
    stem_act, slope_two = gelu_both(mm(hid_taps, two_full) + conv_two_bias.astype(F32))
    slope_two = slope_two.astype(BF16)
    group = pick(lang_group, x, 0)
    stem = stem_act + positions(rows, width, c * rows) + pick(lang_table, group, 0).astype(F32)[None]

    gain_one, gain_two = ln_one_gain.astype(F32), ln_two_gain.astype(F32)
    stats_one = norm_stats(stem)
    normed = (
        (stem - stats_one[0]) * stats_one[1] * gain_one + ln_one_bias.astype(F32)
    ).astype(BF16)
    kv_shift = jnp.concatenate([jnp.zeros((width,), F32), v_bias.astype(F32)])
    kv_own = (mm(normed, qkv_full[:, width:]) + kv_shift).astype(BF16)
    kv_oth = send(kv_own, CORE)
    queries = (mm(normed, qkv_full[:, :width]) + q_bias.astype(F32)).astype(BF16)
    half = pairs // 2
    partial = attend(queries, kv_own, kv_oth, 0, half, pairs)
    partial = join(*partial, up_across)
    up_across = partial[2]
    cotangent = to_clip(after(grad_out, partial[0]))
    attended, lse = attend(queries, kv_own, kv_oth, half, pairs - half, pairs, partial[:2])
    up_parts = parts_of(up_part, up_across)
    out_full = place(j, up_parts, row_moves(0, quarter), (width, width))
    up_full = place(
        j, up_parts, block_moves(quarter, quarter, blocks, width), (width, hidden)
    )
    down_full = place(
        j, parts_of(w_fc_two, down_across), row_moves(0, hidden // 4), (hidden, width)
    )
    residual = stem + mm(attended, out_full) + out_bias.astype(F32)

    stats_two = norm_stats(residual)
    normed_two = (
        (residual - stats_two[0]) * stats_two[1] * gain_two + ln_two_bias.astype(F32)
    ).astype(BF16)
    active, slope_up = gelu_both(mm(normed_two, up_full) + fc_one_bias.astype(F32))
    active, slope_up = active.astype(BF16), slope_up.astype(BF16)

    def core_moves():
        def over_core(grads):
            beside = send(pick(grads, 1 - c, 1), CORE)
            return round_sum(pick(grads, c, 1), beside)

        def over_x(grads):
            across = send(pick(grads, 1 - x, 0), CROSS)
            return round_sum(pick(grads, x, 0), across)

        return [over_core, over_x]

    def by_owner(grads):
        return grads.astype(BF16).reshape(2, 2, -1, grads.shape[1])

    grad_mlp = (cotangent.astype(F32) * live).astype(BF16)
    grad_rows = grad_mlp.astype(F32)
    down = Chain(by_owner(mm_tn(active, grad_mlp)), core_moves())
    down_shift = jnp.sum(grad_rows, axis=0)

    active, slope_up = slot([down], [down], active, slope_up)
    encoded = (residual + mm(active, down_full) + fc_two_bias.astype(F32)) * live
    encoded = encoded.astype(BF16)
    encoded, grad_mlp = slot([down], [down], encoded, grad_mlp)
    grad_upper = (mm_nt(grad_mlp, down_full) * slope_up.astype(F32)).astype(BF16)
    up = Chain(by_owner(mm_tn(normed_two, grad_upper)), core_moves() + dp_moves())
    up_shift = jnp.sum(grad_upper.astype(F32), axis=0)
    grad_upper = slot([up], [up], grad_upper)
    grad_norm, grad_gain_two, grad_shift_two = norm_back(
        residual, stats_two, gain_two, mm_nt(grad_upper, up_full)
    )
    grad_residual = grad_rows + grad_norm
    grad_branch = grad_residual.astype(BF16)
    out = Chain(by_owner(mm_tn(attended, grad_branch)), core_moves())
    out_shift = jnp.sum(grad_branch.astype(F32), axis=0)
    grad_branch = slot([up, out], [out], grad_branch)
    grad_att = mm_nt(grad_branch, out_full).astype(BF16)

    third = -(-pairs // 3)
    grad_att = slot([up, out], [out], grad_att)
    partial = attend_back(queries, kv_own, kv_oth, lse, grad_att, 0, third, pairs)
    partial = slot([up, out, down], [up], *partial)
    ffn = Chain(jnp.concatenate([down.value, out.value]), dp_moves())
    ffn.step()
    partial = attend_back(queries, kv_own, kv_oth, lse, grad_att, third, third, pairs, partial)
    partial = slot([ffn], [ffn], *partial)
    grad_q, own_kv, oth_kv = attend_back(
        queries, kv_own, kv_oth, lse, grad_att, 2 * third, pairs - 2 * third, pairs, partial
    )
    grad_q, own_kv, oth_kv = slot([ffn, up], [ffn, up], grad_q, own_kv, oth_kv)
    grad_kv = round_sum(own_kv, send(oth_kv, CORE))
    grad_packed = jnp.concatenate([grad_q, grad_kv[0], grad_kv[1]], axis=1)
    qkv = Chain(by_owner(mm_tn(normed, grad_packed)), core_moves() + dp_moves())
    q_shift = jnp.sum(grad_q.astype(F32), axis=0)
    v_shift = jnp.sum(grad_kv[1].astype(F32), axis=0)
    grad_packed = slot([ffn, up, qkv], [ffn, up, qkv], grad_packed)
    grad_norm, grad_gain_one, grad_shift_one = norm_back(
        stem, stats_one, gain_one, mm_nt(grad_packed, qkv_full)
    )
    grad_stem = grad_residual + grad_norm
    group_hot = (jnp.arange(lang_table.shape[0]) == group).astype(F32)
    grad_lang = group_hot[:, None] * jnp.sum(grad_stem, axis=0)[None]
    grad_two = (grad_stem * slope_two.astype(F32)).astype(BF16)
    two_shift = jnp.sum(grad_two.astype(F32), axis=0)
    grad_two = slot([ffn, up, qkv], [ffn, up, qkv], grad_two)
    follow = send(grad_two[0:1], [(1, 0), (3, 2)])
    two_grads = mm_tn(hid_taps, grad_two).astype(BF16).reshape(3, 2, 2, quarter, width)
    two = Chain(two_grads.transpose(1, 2, 0, 3, 4), core_moves())
    grad_two = slot([two], [two], grad_two)
    grad_next = jnp.concatenate([grad_two[1:], follow])
    hid_grad_even = mm_nt(grad_two, two_full[width : 2 * width])
    hid_grad_odd = mm_nt(grad_two, two_full[2 * width :]) + mm_nt(grad_next, two_full[:width])
    grad_even = (hid_grad_even * slope_even.astype(F32)).astype(BF16)
    grad_odd = (hid_grad_odd * slope_odd.astype(F32)).astype(BF16)
    one_shift = jnp.sum(grad_even.astype(F32), axis=0) + jnp.sum(grad_odd.astype(F32), axis=0)
    grad_even, grad_odd = slot(
        [ffn, up, qkv, two], [ffn, up, qkv, two], grad_even, grad_odd
    )
    one = Chain(by_owner(mm_tn(grad_even, cols_even) + mm_tn(grad_odd, cols_odd)), core_moves())
    vectors = Chain(
        jnp.concatenate(
            [
                q_shift, v_shift, grad_gain_one, grad_shift_one, two_shift, one_shift,
                down_shift, grad_gain_two, grad_shift_two, out_shift, up_shift,
                grad_lang.reshape(-1),
            ]
        ).reshape(-1, 128),
        total_moves(),
    )
    one.step()
    vectors.step()
    terms_even = mm_nt(grad_even, one_full)
    terms_odd = mm_nt(grad_odd, one_full)
    before, mid_e, late = (terms_even[:, k * mels : (k + 1) * mels] for k in range(3))
    early, mid_o, last = (terms_odd[:, k * mels : (k + 1) * mels] for k in range(3))
    spill = send(jnp.where(c == 0, last[-1:], before[0:1]), CORE)
    zero_spill = jnp.zeros_like(spill)
    last_prev = jnp.concatenate([jnp.where(c == 1, spill, zero_spill), last[:-1]])
    before_next = jnp.concatenate([before[1:], jnp.where(c == 0, spill, zero_spill)])
    mel_grad = jnp.concatenate(
        [mid_e + early + last_prev, late + mid_o + before_next], axis=1
    ).astype(BF16)
    mel_grad = slot([one, vectors], [one, vectors], mel_grad)
    back = from_clip(jnp.concatenate([encoded, mel_grad], axis=1))
    encoded = back[:, :, :width]
    mel_grad = back[:, :, width:].astype(F32).reshape(slots, 2 * part, mels)

    one_rows = width // 4
    spare = width // 3 - 3 * mels
    flat = jnp.pad(one.value, ((0, 0), (0, spare)))
    flat = jnp.concatenate([flat[k * one_rows // 3 : (k + 1) * one_rows // 3] for k in range(3)], axis=1)
    conv = Chain(jnp.concatenate([two.value.reshape(-1, width), flat]), dp_moves())
    chains = [ffn, up, qkv, conv, vectors]
    while any(chain.moves for chain in chains):
        slot(chains, chains)

    down_sum, out_sum = ffn.value[: hidden // 4], ffn.value[hidden // 4 :]
    two_sum, flat = conv.value[: 3 * quarter], conv.value[3 * quarter :]
    one_sum = jnp.concatenate([flat[:, k * width // 3 : (k + 1) * width // 3] for k in range(3)])
    one_sum = one_sum[:, : 3 * mels]
    sums = vectors.value.reshape(-1)
    vec = lambda k: sums[k * width : (k + 1) * width]
    return (
        encoded,
        mel_grad,
        one_sum.astype(F32).T,
        lax.dynamic_slice_in_dim(vec(5), j * quarter, quarter),
        two_sum.astype(F32).reshape(conv_two.shape),
        vec(4),
        sums[10 * width + hidden :].reshape(lang_table.shape),
        vec(2),
        vec(3),
        qkv.value.astype(F32),
        vec(0),
        vec(1),
        out_sum.astype(F32),
        vec(9),
        vec(7),
        vec(8),
        up.value.astype(F32),
        sums[10 * width : 10 * width + hidden],
        down_sum.astype(F32),
        vec(6),
    )


def solution(mesh):
    in_specs = (
        P("dp", "chan", None),
        P("dp"),
        P(),
        P(None, "chan"),
        P("chan"),
        P(None, "chan", None),
        P(),
        P(),
        P(),
        P(),
        P("chan", None),
        P(),
        P(),
        P("chan", None),
        P(),
        P(),
        P(),
        P("chan", None),
        P(),
        P("chan", None),
        P(),
        P("dp", "chan", None),
    )
    out_specs = (
        P("dp", "chan", None),
        P("dp", "chan", None),
        P(None, "chan"),
        P("chan"),
        P(None, "chan", None),
        P(),
        P(),
        P(),
        P(),
        P("chan", None),
        P(),
        P(),
        P("chan", None),
        P(),
        P(),
        P(),
        P("chan", None),
        P(),
        P("chan", None),
        P(),
    )
    return jax.shard_map(
        on_device, mesh=mesh, in_specs=in_specs, out_specs=out_specs, check_vma=False
    )
```

```python
import math

import jax
import jax.numpy as jnp
from jax import lax
from jax.experimental import pallas as pl
from jax.experimental.pallas import tpu as pltpu
from jax.sharding import PartitionSpec as P

HEAD_DIM = 64
PAIR = 2 * HEAD_DIM
SCALE = HEAD_DIM ** (-0.5)
BF16 = jnp.bfloat16
F32 = jnp.float32

CORE = [(j, j ^ 1) for j in range(4)]
CROSS = [(j, j ^ 2) for j in range(4)]
SAME = [(2 * x + c, 2 * c + x) for x in range(2) for c in range(2)]
OTHER = [(2 * x + c, 2 * (1 - c) + x) for x in range(2) for c in range(2)]
SAME_BACK = [(b, a) for a, b in SAME]
OTHER_BACK = [(b, a) for a, b in OTHER]


def send(block, perm):
    return lax.ppermute(block, "chan", perm)


def ordered(first_is_own, own, other, axis=0, stack=False):
    join = jnp.stack if stack else jnp.concatenate
    return jnp.where(first_is_own, join([own, other], axis), join([other, own], axis))


def pick(block, index, axis):
    return lax.dynamic_index_in_dim(block, index, axis, keepdims=False)


def gelu_both(inputs):
    cdf = 0.5 * (1.0 + lax.erf(inputs * math.sqrt(0.5)))
    pdf = jnp.exp(-0.5 * inputs * inputs) * (1.0 / math.sqrt(2.0 * math.pi))
    return inputs * cdf, cdf + inputs * pdf


def norm_stats(inputs):
    row_mean = jnp.mean(inputs, axis=-1, keepdims=True)
    centered = inputs - row_mean
    variance = jnp.mean(centered * centered, axis=-1, keepdims=True)
    return row_mean, lax.rsqrt(variance + 1e-05)


def norm_back(inputs, stats, gain_vec, cotangent):
    row_mean, inverse = stats
    unit = (inputs - row_mean) * inverse
    scaled = cotangent * gain_vec
    mean_one = jnp.mean(scaled, axis=-1, keepdims=True)
    mean_two = jnp.mean(scaled * unit, axis=-1, keepdims=True)
    grad = inverse * (scaled - mean_one - unit * mean_two)
    return grad, jnp.sum(cotangent * unit, axis=0), jnp.sum(cotangent, axis=0)


def positions(frame_count, model_width, first_frame):
    increment = math.log(10000.0) / (model_width // 2 - 1)
    inverse = jnp.exp(-increment * jnp.arange(model_width // 2, dtype=jnp.float32))
    angles = (first_frame + jnp.arange(frame_count)).astype(jnp.float32)[:, None] * inverse[None, :]
    return jnp.concatenate([jnp.sin(angles), jnp.cos(angles)], axis=1)


def mm(left, right):
    return jnp.dot(left, right, preferred_element_type=F32)


def mm_nt(left, right):
    return lax.dot_general(left, right, (((1,), (1,)), ((), ())), preferred_element_type=F32)


def mm_tn(left, right):
    return lax.dot_general(left, right, (((0,), (0,)), ((), ())), preferred_element_type=F32)


def head_stack(block):
    lane = lax.broadcasted_iota(jnp.int32, block.shape, 1)
    zero = jnp.zeros_like(block)
    return jnp.concatenate(
        [jnp.where(lane < HEAD_DIM, block, zero), jnp.where(lane < HEAD_DIM, zero, block)], axis=0
    )


def head_join(stacked):
    rows = stacked.shape[0] // 2
    lane = lax.broadcasted_iota(jnp.int32, (rows, stacked.shape[1]), 1)
    return jnp.where(lane < HEAD_DIM, stacked[:rows], stacked[rows:])


def attend_kernel(chunk, q_ref, k_own, k_oth, v_own, v_oth, *refs):
    att_ref, lse_ref, k_all, v_all = refs[-4:]
    rows = q_ref.shape[0]
    k_all[0:rows] = k_own[...]
    k_all[rows:] = k_oth[...]
    v_all[0:rows, 0:PAIR] = v_own[...]
    v_all[rows:, 0:PAIR] = v_oth[...]
    v_all[:, PAIR:] = jnp.ones((2 * rows, PAIR), BF16)
    for start in range(0, rows, chunk):
        at = pl.ds(start, chunk)
        queries = head_stack(q_ref[at] * SCALE)
        scores = mm_nt(queries, k_all[...])
        top = jnp.max(scores, axis=1, keepdims=True)
        both = mm(jnp.exp(scores - top).astype(BF16), v_all[...])
        total = both[:, PAIR:]
        att_ref[at] = head_join(both[:, :PAIR] / total).astype(BF16)
        lse_ref[at] = head_join(top + jnp.log(total))


def attend(q, kv_own, kv_oth, first, count, pairs, earlier=()):
    rows = q.shape[0]
    chunk = 176
    spec = lambda shift: pl.BlockSpec((rows, PAIR), lambda p: (0, p + shift))
    return pl.pallas_call(
        lambda *refs: attend_kernel(chunk, *refs),
        grid=(count,),
        in_specs=[spec(first), spec(first), spec(first), spec(first + pairs), spec(first + pairs)]
        + [pl.BlockSpec(memory_space=pl.ANY)] * len(earlier),
        out_specs=[spec(first)] * 2,
        out_shape=[
            jax.ShapeDtypeStruct((rows, pairs * PAIR), BF16),
            jax.ShapeDtypeStruct((rows, pairs * PAIR), F32),
        ],
        input_output_aliases={5 + i: i for i in range(len(earlier))},
        scratch_shapes=[
            pltpu.VMEM((2 * rows, PAIR), BF16),
            pltpu.VMEM((2 * rows, 2 * PAIR), BF16),
        ],
        compiler_params=pltpu.CompilerParams(vmem_limit_bytes=56 * 1024 * 1024),
        cost_estimate=pl.CostEstimate(
            flops=count * 32 * rows * rows * PAIR,
            bytes_accessed=count * PAIR * rows * 16,
            transcendentals=4 * count * rows * rows,
        ),
        name="attend",
    )(q, kv_own, kv_oth, kv_own, kv_oth, *earlier)


def attend_back_kernel(chunk, q_ref, k_own, k_oth, v_own, v_oth, lse_ref, g_ref, *refs):
    dq_ref, own_ref, oth_ref, k_all, v_all, q_all, g_all, p_all, s_all = refs[-9:]
    rows = q_ref.shape[0]
    k_all[0:rows] = k_own[...]
    k_all[rows:] = k_oth[...]
    v_all[0:rows] = v_own[...]
    v_all[rows:] = v_oth[...]
    for start in range(0, rows, chunk):
        at = pl.ds(start, chunk)
        both = pl.ds(2 * start, 2 * chunk)
        queries = head_stack(q_ref[at] * SCALE)
        grads = head_stack(g_ref[at])
        q_all[both] = queries
        g_all[both] = grads
        lse = jnp.concatenate([lse_ref[at, 0:1], lse_ref[at, HEAD_DIM : HEAD_DIM + 1]], axis=0)
        probs = jnp.exp(mm_nt(queries, k_all[...]) - lse)
        grad_probs = mm_nt(grads, v_all[...])
        inner = jnp.sum(probs * grad_probs, axis=1, keepdims=True)
        grad_scores = (probs * (grad_probs - inner)).astype(BF16)
        p_all[both] = probs.astype(BF16)
        s_all[both] = grad_scores
        dq_ref[at] = (head_join(mm(grad_scores, k_all[...])) * SCALE).astype(BF16)

    dk = mm_tn(q_all[...], s_all[...]).T.astype(BF16)
    own_ref[0] = dk[0:rows]
    oth_ref[0] = dk[rows:]
    dv = mm_tn(g_all[...], p_all[...]).T.astype(BF16)
    own_ref[1] = dv[0:rows]
    oth_ref[1] = dv[rows:]


def attend_back(q, kv_own, kv_oth, lse, grad_att, first, count, pairs, earlier=()):
    rows = q.shape[0]
    chunk = 176
    spec = lambda shift: pl.BlockSpec((rows, PAIR), lambda p: (0, p + shift))
    two = pl.BlockSpec((2, rows, PAIR), lambda p: (0, 0, p + first))
    both = jax.ShapeDtypeStruct((2, rows, pairs * PAIR), BF16)
    return pl.pallas_call(
        lambda *refs: attend_back_kernel(chunk, *refs),
        grid=(count,),
        in_specs=[spec(first), spec(first), spec(first), spec(first + pairs), spec(first + pairs)]
        + [spec(first)] * 2
        + [pl.BlockSpec(memory_space=pl.ANY)] * len(earlier),
        out_specs=[spec(first), two, two],
        out_shape=[jax.ShapeDtypeStruct((rows, pairs * PAIR), BF16), both, both],
        input_output_aliases={7 + i: i for i in range(len(earlier))},
        scratch_shapes=[pltpu.VMEM((2 * rows, PAIR), BF16)] * 4
        + [pltpu.VMEM((2 * rows, 2 * rows), BF16)] * 2,
        compiler_params=pltpu.CompilerParams(vmem_limit_bytes=56 * 1024 * 1024),
        cost_estimate=pl.CostEstimate(
            flops=count * 80 * rows * rows * PAIR,
            bytes_accessed=count * PAIR * rows * 26,
            transcendentals=4 * count * rows * rows,
        ),
        name="attend_back",
    )(q, kv_own, kv_oth, kv_own, kv_oth, lse, grad_att, *earlier)


def join(*values):
    return lax.optimization_barrier(values)


def after(value, *others):
    return lax.optimization_barrier((value,) + others)[0]


def place_kernel(moves, index_ref, own, near, far_a, far_b, near_far, *refs):
    wholes, sems = refs[:-1], refs[-1]
    j, y = index_ref[0], index_ref[1]
    x, c = j // 2, j % 2
    rows = own.shape[1]
    half = rows // 2
    across = rows * (2 * (1 - x) + c)
    beside = rows * (2 * (1 - x) + 1 - c)
    pieces = [
        (own, rows * j),
        (near, rows * (2 * x + 1 - c)),
        (far_a, across + half * y),
        (far_b, across + half * (1 - y)),
        (near_far.at[0], beside + half * y),
        (near_far.at[1], beside + half * (1 - y)),
    ]
    copies = []
    for piece, row in pieces:
        at = pl.ds(pl.multiple_of(row, half), piece.shape[1])
        for move in moves:
            source, target = move(piece, wholes, at)
            copies.append(pltpu.make_async_copy(source, target, sems.at[len(copies)]))
    for copy in copies:
        copy.start()
    for copy in copies:
        copy.wait()


def place(index, parts, moves, *shapes):
    anywhere = pl.BlockSpec(memory_space=pl.ANY)
    return pl.pallas_call(
        lambda *refs: place_kernel(moves, *refs),
        in_specs=[pl.BlockSpec(memory_space=pltpu.SMEM)] + [anywhere] * 5,
        out_specs=[pl.BlockSpec(memory_space=pltpu.VMEM)] * len(shapes),
        out_shape=[jax.ShapeDtypeStruct(shape, BF16) for shape in shapes],
        scratch_shapes=[pltpu.SemaphoreType.DMA((6 * len(moves),))],
        compiler_params=pltpu.CompilerParams(vmem_limit_bytes=16 * 1024 * 1024),
        cost_estimate=pl.CostEstimate(
            flops=0, bytes_accessed=sum(4 * math.prod(shape) for shape in shapes), transcendentals=0
        ),
        name="place",
    )(index, *parts)


ROW_MOVES = [lambda piece, wholes, at: (piece.at[0], wholes[0].at[at])]
TAP_MOVES = [lambda piece, wholes, at: (piece, wholes[0].at[:, at])]


def block_moves(blocks, width):
    def move(block):
        columns = pl.ds(block * width, width)
        return lambda piece, wholes, at: (piece.at[1 + block], wholes[1].at[at, columns])

    return ROW_MOVES + [move(block) for block in range(blocks)]


def round_sum(*terms):
    return sum(term.astype(F32) for term in terms).astype(BF16)


def dp_step(share, bit, axis=0):
    count = lax.axis_size("dp")
    side = (lax.axis_index("dp") // bit) % 2
    shape = share.shape
    halves = share.reshape(shape[:axis] + (2, shape[axis] // 2) + shape[axis + 1 :])
    perm = [(d, d ^ bit) for d in range(count)]
    arrived = lax.ppermute(pick(halves, 1 - side, axis), "dp", perm)
    return round_sum(pick(halves, side, axis), arrived)


def dp_back(share, bit, axis=0):
    count = lax.axis_size("dp")
    side = (lax.axis_index("dp") // bit) % 2
    arrived = lax.ppermute(share, "dp", [(d, d ^ bit) for d in range(count)])
    return ordered(side == 0, share, arrived, axis)


def dp_bits():
    bits = [1]
    while 2 * bits[-1] < lax.axis_size("dp"):
        bits.append(2 * bits[-1])
    return bits


def quad_sides(bits):
    index = lax.axis_index("dp")
    return [(index // bit) % 2 for bit in bits]


def quad_send(block, bits, other):
    flip = bits[0] * (other // 2) + bits[1] * (other % 2)
    return lax.ppermute(block, "dp", [(d, d ^ flip) for d in range(lax.axis_size("dp"))])


def quad_step(share, bits):
    high, low = quad_sides(bits)
    shape = share.shape
    parts = share.reshape(shape[0], 2, 2, shape[1] // 4, shape[2])

    def part(other):
        place = (0, (high + other // 2) % 2, (low + other) % 2, 0, 0)
        size = (shape[0], 1, 1, shape[1] // 4, shape[2])
        return lax.dynamic_slice(parts, place, size).reshape(shape[0], -1, shape[2])

    return round_sum(part(0), *[quad_send(part(other), bits, other) for other in (1, 2, 3)])


def quad_back(share, bits):
    high, low = quad_sides(bits)
    near, far, last = (quad_send(share, bits, other) for other in (1, 2, 3))
    own_pair = ordered(low == 0, share, near, 1)
    far_pair = ordered(low == 0, far, last, 1)
    return ordered(high == 0, own_pair, far_pair, 1)


def rest_moves(quads):
    bits = dp_bits()[1:]
    groups = [tuple(bits[k : k + 2]) for k in range(0, len(bits), 2)] if quads else [
        (bit,) for bit in bits
    ]
    there = [
        (lambda v, g=group: quad_step(v, g)) if len(group) == 2
        else (lambda v, g=group: dp_step(v, g[0], axis=1))
        for group in groups
    ]
    back = [
        (lambda v, g=group: quad_back(v, g)) if len(group) == 2
        else (lambda v, g=group: dp_back(v, g[0], axis=1))
        for group in reversed(groups)
    ]
    return there + back


def total_moves():
    def over(axis, perm):
        return lambda v: v + lax.ppermute(v, axis, perm)

    count = lax.axis_size("dp")
    return [over("chan", CORE), over("chan", CROSS)] + [
        over("dp", [(d, d ^ bit) for d in range(count)]) for bit in dp_bits()
    ]


class Chain:
    def __init__(self, value, moves):
        self.value, self.moves = value, list(moves)

    def step(self):
        if self.moves:
            self.value = self.moves.pop(0)(self.value)


def slot(chains, *main):
    joined = join(*[chain.value for chain in chains], *main)
    for chain, value in zip(chains, joined):
        chain.value = value
        chain.step()
    main = joined[len(chains) :]
    return main[0] if len(main) == 1 else main


def on_device(
    mel,
    lang_group,
    clip_count,
    conv_one,
    conv_one_bias,
    conv_two,
    conv_two_bias,
    lang_table,
    ln_one_gain,
    ln_one_bias,
    w_qkv,
    q_bias,
    v_bias,
    w_out,
    out_bias,
    ln_two_gain,
    ln_two_bias,
    w_fc_one,
    fc_one_bias,
    w_fc_two,
    fc_two_bias,
    grad_out,
):
    slots, part, width = grad_out.shape
    hidden = w_fc_one.shape[1]
    pairs = width // PAIR
    quarter = width // 4
    mels = mel.shape[2]
    rows = slots * part
    j = lax.axis_index("chan")
    x, c = j // 2, j % 2
    live = (x < clip_count[lax.axis_index("dp")]).astype(F32)

    def to_clip(block):
        same = send(pick(block, c, 0), SAME)
        other = send(pick(block, 1 - c, 0), OTHER)
        return ordered(x == 0, same, other)

    def from_clip(block):
        half = block.shape[0] // 2
        first, second = block[:half], block[half:]
        same = send(jnp.where(x == 0, first, second), SAME_BACK)
        other = send(jnp.where(x == 0, second, first), OTHER_BACK)
        return ordered(c == 0, same, other, stack=True)

    mel_pairs = mel.reshape(slots, part, 2 * mels)
    edge = send(jnp.where(j == 1, mel_pairs[1, -1], mel_pairs[0, 0]), [(1, 3), (2, 0)])
    edge = jnp.where(j == 1, mel_pairs[0, -1], jnp.where(j == 2, mel_pairs[1, 0], edge))
    zero_edge = jnp.zeros_like(edge)
    mel_own = jnp.concatenate(
        [
            jnp.where(c == 1, edge, zero_edge)[None],
            to_clip(mel_pairs),
            jnp.where(c == 0, edge, zero_edge)[None],
        ]
    )

    y = lax.axis_index("dp") % 2
    index = jnp.stack([j, y])
    dp_count = lax.axis_size("dp")
    over_y = [(d, d ^ 1) for d in range(dp_count)]
    one_part = jnp.concatenate([conv_one.T, conv_one_bias[:, None]], axis=1)
    one_across = send(one_part, CROSS)
    one_column = ordered(x == 0, one_part, one_across, stack=True)
    one_whole = ordered(c == 0, one_column, send(one_column, CORE), 1, stack=True)
    one_whole = one_whole.reshape(width, -1)

    def cross_half(own):
        half = own.shape[1] // 2
        return send(lax.dynamic_slice_in_dim(own, y * half, half, 1), CROSS)

    def cross_rest(far):
        return lax.ppermute(far, "dp", over_y)

    def beside(far, rest):
        return send(jnp.stack([far, rest]), CORE)

    blocks = hidden // width
    early_part = jnp.stack([w_out, w_fc_one[:, :width]])
    later_part = jnp.stack([w_fc_one[:, k * width : (k + 1) * width] for k in range(1, blocks)])
    qkv_part, down_part = w_qkv[None], w_fc_two[None]
    two_far = cross_half(conv_two)
    two_near = send(conv_two, CORE)
    two_far, early_part, later_part = join(two_far, early_part, later_part)
    two_rest = cross_rest(two_far)
    qkv_far = cross_half(after(qkv_part, two_far))

    even, odd = mel_own[:, :mels], mel_own[:, mels:]
    ones = jnp.ones((rows, 1), BF16)
    cols_even = jnp.concatenate([odd[0:rows], even[1 : rows + 1], odd[1 : rows + 1], ones], axis=1)
    cols_odd = jnp.concatenate(
        [even[1 : rows + 1], odd[1 : rows + 1], even[2 : rows + 2], ones], axis=1
    )
    cols_edge = jnp.concatenate([even[0:1], odd[0:1], even[1:2], ones[0:1]], axis=1)
    hid_even, slope_even = gelu_both(mm_nt(cols_even, one_whole))
    hid_odd, slope_odd = gelu_both(mm_nt(cols_odd, one_whole))
    hid_edge, _ = gelu_both(mm_nt(cols_edge, one_whole))
    hid_edge = jnp.where(c == 1, hid_edge, 0.0)
    hid_even, hid_odd, hid_edge = hid_even.astype(BF16), hid_odd.astype(BF16), hid_edge.astype(BF16)
    slope_even, slope_odd = slope_even.astype(BF16), slope_odd.astype(BF16)
    hid_even, hid_odd, hid_edge, slope_even, slope_odd, two_rest, qkv_far = join(
        hid_even, hid_odd, hid_edge, slope_even, slope_odd, two_rest, qkv_far
    )
    two_beside = beside(two_far, two_rest)
    qkv_rest, qkv_near = cross_rest(qkv_far), send(after(qkv_part, qkv_far), CORE)
    early_far = cross_half(after(early_part, qkv_far))
    hid_prev = jnp.concatenate([hid_edge, hid_odd[:-1]])
    hid_taps = jnp.concatenate([hid_prev, hid_even, hid_odd], axis=1)
    group = pick(lang_group, x, 0)
    place_rows = positions(rows, width, after(c * rows, qkv_far))
    place_rows += pick(lang_table, group, 0).astype(F32)[None]
    place_rows, hid_taps, two_beside, early_far, qkv_rest = join(
        place_rows, hid_taps, two_beside, early_far, qkv_rest
    )
    qkv_beside = beside(qkv_far, qkv_rest)
    early_rest = cross_rest(early_far)
    later_far = cross_half(after(later_part, early_far))
    (two_full,) = place(
        index, (conv_two, two_near, two_far, two_rest, two_beside), TAP_MOVES, (3, width, width)
    )
    two_full = two_full.reshape(-1, width)
    stem_act, slope_two = gelu_both(mm(hid_taps, two_full) + conv_two_bias.astype(F32))
    slope_two = slope_two.astype(BF16)
    stem = stem_act + place_rows

    gain_one, gain_two = ln_one_gain.astype(F32), ln_two_gain.astype(F32)
    stats_one = norm_stats(stem)
    normed = (
        (stem - stats_one[0]) * stats_one[1] * gain_one + ln_one_bias.astype(F32)
    ).astype(BF16)
    normed, slope_two, qkv_beside = join(normed, slope_two, qkv_beside)
    (qkv_full,) = place(
        index, (qkv_part, qkv_near, qkv_far, qkv_rest, qkv_beside), ROW_MOVES, (width, 3 * width)
    )
    kv_shift = jnp.concatenate([jnp.zeros((width,), F32), v_bias.astype(F32)])
    kv_own = (mm(normed, qkv_full[:, width:]) + kv_shift).astype(BF16)
    kv_oth = send(kv_own, CORE)
    queries = (mm(normed, qkv_full[:, :width]) + q_bias.astype(F32)).astype(BF16)
    queries, kv_oth, early_rest, later_far = join(queries, kv_oth, early_rest, later_far)
    later_rest = cross_rest(later_far)
    up_part = jnp.concatenate([early_part, later_part])
    up_near = send(after(up_part, later_far), CORE)
    down_far = cross_half(after(down_part, later_far))
    half = pairs // 2
    partial = attend(queries, kv_own, kv_oth, 0, half, pairs)
    *partial, later_rest, up_near, down_far = join(*partial, later_rest, up_near, down_far)
    up_far = jnp.concatenate([early_far, later_far])
    up_rest = jnp.concatenate([early_rest, later_rest])
    up_beside = beside(up_far, up_rest)
    down_rest = cross_rest(down_far)
    cotangent = to_clip(after(grad_out, down_far))
    attended, lse = attend(queries, kv_own, kv_oth, half, pairs - half, pairs, partial)
    attended, up_beside, down_rest, cotangent = join(attended, up_beside, down_rest, cotangent)
    down_near, down_beside = send(after(down_part, down_rest), CORE), beside(down_far, down_rest)
    out_full, up_full = place(
        index,
        (up_part, up_near, up_far, up_rest, up_beside),
        block_moves(blocks, width),
        (width, width),
        (width, hidden),
    )
    residual = stem + mm(attended, out_full) + out_bias.astype(F32)

    stats_two = norm_stats(residual)
    normed_two = (
        (residual - stats_two[0]) * stats_two[1] * gain_two + ln_two_bias.astype(F32)
    ).astype(BF16)
    active, slope_up = gelu_both(mm(normed_two, up_full) + fc_one_bias.astype(F32))
    active, slope_up = active.astype(BF16), slope_up.astype(BF16)

    def by_owner(grads):
        return grads.astype(BF16).reshape(2, 2, -1, grads.shape[1])

    def over_core(grads):
        beside = send(pick(grads, 1 - c, 1), CORE)
        return round_sum(pick(grads, c, 1), beside)

    def over_x(grads):
        across = send(pick(grads, 1 - x, 0), CROSS)
        return round_sum(pick(grads, x, 0), across)

    def first_hop(grads):
        middle = grads.shape[2] // 2
        return over_x(grads[..., :middle]), dp_step(grads[..., middle:], 1, axis=1)

    def second_hop(sides):
        return jnp.stack([dp_step(sides[0], 1), over_x(sides[1])])

    def back_y(v):
        return dp_back(v, 1, axis=1)

    def back_left(v):
        return dp_back(v[0], 1), v[1]

    def back_right(v):
        return v[0], dp_back(v[1], 1)

    start_moves = [over_core, first_hop, second_hop]
    down_moves = start_moves + rest_moves(True) + [back_left, back_right]
    up_moves = start_moves + rest_moves(False) + [back_left, back_right]
    qkv_moves = start_moves + rest_moves(True) + [back_y]
    conv_moves = rest_moves(True) + [back_y]

    def columns(sides):
        return jnp.concatenate([sides[0], sides[1]], axis=1).astype(F32)

    active, slope_up, down_near, down_beside = join(active, slope_up, down_near, down_beside)
    down_parts = (down_part, down_near, down_far, down_rest, down_beside)
    (down_full,) = place(index, down_parts, ROW_MOVES, (hidden, width))
    grad_mlp = (cotangent.astype(F32) * live).astype(BF16)
    grad_rows = grad_mlp.astype(F32)
    down = Chain(by_owner(mm_tn(active, grad_mlp)), down_moves)
    down_shift = jnp.sum(grad_rows, axis=0)
    grad_mlp = slot([down], grad_mlp)
    grad_upper = (mm_nt(grad_mlp, down_full) * slope_up.astype(F32)).astype(BF16)
    up_shift = jnp.sum(grad_upper.astype(F32), axis=0)
    grad_upper, down_sides = join(grad_upper, down.value)
    down_moves_left = down.moves
    middle = down_sides.shape[1] // 2
    down = Chain(down_sides[:, :middle], [first_hop])
    later = Chain(down_sides[:, middle:], [first_hop])
    down.step()
    grad_norm, grad_gain_two, grad_shift_two = norm_back(
        residual, stats_two, gain_two, mm_nt(grad_upper, up_full)
    )
    grad_residual = grad_rows + grad_norm
    grad_branch = grad_residual.astype(BF16)
    out_shift = jnp.sum(grad_branch.astype(F32), axis=0)
    grad_branch, grad_residual, down.value, later.value = join(
        grad_branch, grad_residual, down.value, later.value
    )
    later.step()
    out_grads = mm_tn(attended, grad_branch).astype(BF16)
    grad_att = mm_nt(grad_branch, out_full).astype(BF16)
    up_grads = mm_tn(normed_two, after(grad_upper, grad_att, out_grads)).astype(BF16)
    grad_att, up_grads, later.value = join(grad_att, up_grads, later.value)
    down = Chain(
        (
            jnp.concatenate([down.value[0], later.value[0]]),
            jnp.concatenate([down.value[1], later.value[1]], axis=1),
        ),
        down_moves_left[1:],
    )
    up = Chain(by_owner(jnp.concatenate([up_grads, out_grads], axis=1)), up_moves)

    third = -(-pairs // 3)
    operands = (queries, kv_own, kv_oth, lse)
    grad_att = slot([down, up], grad_att)
    partial = attend_back(*operands, grad_att, 0, third, pairs)
    partial = slot([down, up], *partial)
    partial = attend_back(*operands, grad_att, third, third, pairs, partial)
    partial = slot([down, up], *partial)
    grad_q, own_kv, oth_kv = attend_back(
        *operands, grad_att, 2 * third, pairs - 2 * third, pairs, partial
    )
    grad_q, own_kv, oth_kv, active = slot([down, up], grad_q, own_kv, oth_kv, active)
    oth_kv = send(oth_kv, CORE)
    encoded = (residual + mm(active, down_full) + fc_two_bias.astype(F32)) * live
    encoded, own_kv, oth_kv, down.value, up.value = join(
        encoded.astype(BF16), own_kv, oth_kv, down.value, up.value
    )
    grad_kv = round_sum(own_kv, oth_kv)
    grad_packed = jnp.concatenate([grad_q, grad_kv[0], grad_kv[1]], axis=1)
    qkv = Chain(by_owner(mm_tn(normed, grad_packed)), qkv_moves)
    q_shift = jnp.sum(grad_q.astype(F32), axis=0)
    v_shift = jnp.sum(grad_kv[1].astype(F32), axis=0)
    grad_packed = slot([down, up, qkv], grad_packed)
    grad_norm, grad_gain_one, grad_shift_one = norm_back(
        stem, stats_one, gain_one, mm_nt(grad_packed, qkv_full)
    )
    grad_stem = grad_residual + grad_norm
    group_hot = (jnp.arange(lang_table.shape[0]) == group).astype(F32)
    grad_lang = group_hot[:, None] * jnp.sum(grad_stem, axis=0)[None]
    grad_two = (grad_stem * slope_two.astype(F32)).astype(BF16)
    two_shift = jnp.sum(grad_two.astype(F32), axis=0)
    two_grads = mm_tn(hid_taps, grad_two).astype(BF16).reshape(3, 2, 2, quarter, width)
    two = Chain(
        two_grads.transpose(1, 2, 0, 3, 4).reshape(2, 2, 3 * quarter, width), start_moves
    )
    grad_two, down.value = slot([two, qkv, up], grad_two, down.value)
    follow = send(grad_two[0:1], [(1, 0), (3, 2)])
    hid_grad_even = mm_nt(grad_two, two_full[width : 2 * width])
    hid_grad_last = mm_nt(grad_two, two_full[2 * width :])
    grad_next = jnp.concatenate([grad_two[1:], follow])
    hid_grad_odd = hid_grad_last + mm_nt(grad_next, two_full[:width])
    grad_even = (hid_grad_even * slope_even.astype(F32)).astype(BF16)
    grad_odd = (hid_grad_odd * slope_odd.astype(F32)).astype(BF16)
    one_grads = mm_tn(grad_even, cols_even) + mm_tn(grad_odd, cols_odd)
    spare = width // 3 - one_grads.shape[1]
    one = Chain(
        by_owner(jnp.pad(one_grads, ((0, 0), (0, spare)))),
        [over_core, over_x, lambda v: dp_step(v, 1)],
    )
    vectors = Chain(
        jnp.concatenate(
            [
                jnp.stack(
                    [
                        q_shift, v_shift, grad_gain_one, grad_shift_one, two_shift,
                        down_shift, grad_gain_two, grad_shift_two, out_shift,
                    ]
                ),
                up_shift.reshape(-1, width),
                grad_lang,
            ]
        ),
        total_moves(),
    )
    grad_even, grad_odd = slot([two, qkv, one, vectors, up], grad_even, grad_odd)
    terms_even = mm(grad_even, one_whole)
    terms_odd = mm(grad_odd, one_whole)
    before, mid_e, late = (terms_even[:, k * mels : (k + 1) * mels] for k in range(3))
    early, mid_o, last = (terms_odd[:, k * mels : (k + 1) * mels] for k in range(3))
    spill = send(jnp.where(c == 0, last[-1:], before[0:1]), CORE)
    zero_spill = jnp.zeros_like(spill)
    last_prev = jnp.concatenate([jnp.where(c == 1, spill, zero_spill), last[:-1]])
    before_next = jnp.concatenate([before[1:], jnp.where(c == 0, spill, zero_spill)])
    mel_grad = jnp.concatenate(
        [mid_e + early + last_prev, late + mid_o + before_next], axis=1
    ).astype(BF16)
    mel_grad = slot([two, one, vectors, qkv, up], mel_grad)
    mel_grad = slot([one, vectors, qkv], from_clip(mel_grad), two.value)
    mel_grad, two.value = mel_grad
    one_rows = one.value.shape[0] // 3
    flat = jnp.concatenate([one.value[k * one_rows : (k + 1) * one_rows] for k in range(3)], axis=1)
    flat = flat.reshape(one_rows, 2, width // 2).transpose(1, 0, 2)
    conv = Chain(jnp.concatenate([two.value, flat], axis=1), conv_moves)
    encoded, mel_grad = slot([conv, qkv, vectors, up], encoded, mel_grad)
    mel_grad = mel_grad.astype(F32).reshape(slots, 2 * part, mels)
    encoded = from_clip(encoded)
    chains = [conv, qkv, vectors, up, down]
    while any(chain.moves for chain in chains):
        slot(chains)

    up_out = columns(up.value)
    down_left, down_right = down.value
    down_right = down_right.reshape(2, 2, -1, down_right.shape[1]).swapaxes(0, 1)
    down_sum = columns((down_left, down_right.reshape(down_left.shape)))
    conv_rows = columns(conv.value)
    taken, gap = 3 * quarter // 2, one_rows
    conv_halves = conv_rows.reshape(2, -1, width)
    two_sum = conv_halves[:, :taken].reshape(conv_two.shape)
    one_halves = conv_halves[:, taken:]
    one_sum = jnp.concatenate(
        [
            one_halves[h, :, k * width // 3 : (k + 1) * width // 3]
            for h in range(2)
            for k in range(3)
        ]
    )
    sums = vectors.value
    vec = lambda k: sums[k]
    return (
        encoded,
        mel_grad,
        one_sum[:, : 3 * mels].T,
        one_sum[:, 3 * mels],
        two_sum,
        vec(4),
        sums[9 + blocks :],
        vec(2),
        vec(3),
        columns(qkv.value),
        vec(0),
        vec(1),
        up_out[:, hidden:],
        vec(8),
        vec(6),
        vec(7),
        up_out[:, :hidden],
        sums[9 : 9 + blocks].reshape(-1),
        down_sum,
        vec(5),
    )


def solution(mesh):
    in_specs = (
        P("dp", "chan", None),
        P("dp"),
        P(),
        P(None, "chan"),
        P("chan"),
        P(None, "chan", None),
        P(),
        P(),
        P(),
        P(),
        P("chan", None),
        P(),
        P(),
        P("chan", None),
        P(),
        P(),
        P(),
        P("chan", None),
        P(),
        P("chan", None),
        P(),
        P("dp", "chan", None),
    )
    out_specs = (
        P("dp", "chan", None),
        P("dp", "chan", None),
        P(None, "chan"),
        P("chan"),
        P(None, "chan", None),
        P(),
        P(),
        P(),
        P(),
        P("chan", None),
        P(),
        P(),
        P("chan", None),
        P(),
        P(),
        P(),
        P("chan", None),
        P(),
        P("chan", None),
        P(),
    )
    return jax.shard_map(
        on_device, mesh=mesh, in_specs=in_specs, out_specs=out_specs, check_vma=False
    )
```

```python
import math

import jax
import jax.numpy as jnp
from jax import lax
from jax.experimental import pallas as pl
from jax.experimental.pallas import tpu as pltpu
from jax.sharding import PartitionSpec as P

HEAD_DIM = 64
PAIR = 2 * HEAD_DIM
SCALE = HEAD_DIM ** (-0.5)
BF16 = jnp.bfloat16
F32 = jnp.float32

CORE = [(j, j ^ 1) for j in range(4)]
CROSS = [(j, j ^ 2) for j in range(4)]
SAME = [(2 * x + c, 2 * c + x) for x in range(2) for c in range(2)]
OTHER = [(2 * x + c, 2 * (1 - c) + x) for x in range(2) for c in range(2)]
SAME_BACK = [(b, a) for a, b in SAME]
OTHER_BACK = [(b, a) for a, b in OTHER]


def send(block, perm):
    return lax.ppermute(block, "chan", perm)


def ordered(first_is_own, own, other, axis=0, stack=False):
    join = jnp.stack if stack else jnp.concatenate
    return jnp.where(first_is_own, join([own, other], axis), join([other, own], axis))


def pick(block, index, axis):
    return lax.dynamic_index_in_dim(block, index, axis, keepdims=False)


def gelu_both(inputs):
    cdf = 0.5 * (1.0 + lax.erf(inputs * math.sqrt(0.5)))
    pdf = jnp.exp(-0.5 * inputs * inputs) * (1.0 / math.sqrt(2.0 * math.pi))
    return inputs * cdf, cdf + inputs * pdf


def norm_stats(inputs):
    row_mean = jnp.mean(inputs, axis=-1, keepdims=True)
    centered = inputs - row_mean
    variance = jnp.mean(centered * centered, axis=-1, keepdims=True)
    return row_mean, lax.rsqrt(variance + 1e-05)


def norm_back(inputs, stats, gain_vec, cotangent):
    row_mean, inverse = stats
    unit = (inputs - row_mean) * inverse
    scaled = cotangent * gain_vec
    mean_one = jnp.mean(scaled, axis=-1, keepdims=True)
    mean_two = jnp.mean(scaled * unit, axis=-1, keepdims=True)
    grad = inverse * (scaled - mean_one - unit * mean_two)
    return grad, jnp.sum(cotangent * unit, axis=0), jnp.sum(cotangent, axis=0)


def positions(frame_count, model_width, first_frame):
    increment = math.log(10000.0) / (model_width // 2 - 1)
    inverse = jnp.exp(-increment * jnp.arange(model_width // 2, dtype=jnp.float32))
    angles = (first_frame + jnp.arange(frame_count)).astype(jnp.float32)[:, None] * inverse[None, :]
    return jnp.concatenate([jnp.sin(angles), jnp.cos(angles)], axis=1)


def mm(left, right):
    return jnp.dot(left, right, preferred_element_type=F32)


def mm_nt(left, right):
    return lax.dot_general(left, right, (((1,), (1,)), ((), ())), preferred_element_type=F32)


def mm_tn(left, right):
    return lax.dot_general(left, right, (((0,), (0,)), ((), ())), preferred_element_type=F32)


def head_stack(block):
    lane = lax.broadcasted_iota(jnp.int32, block.shape, 1)
    zero = jnp.zeros_like(block)
    return jnp.concatenate(
        [jnp.where(lane < HEAD_DIM, block, zero), jnp.where(lane < HEAD_DIM, zero, block)], axis=0
    )


def head_join(stacked):
    rows = stacked.shape[0] // 2
    lane = lax.broadcasted_iota(jnp.int32, (rows, stacked.shape[1]), 1)
    return jnp.where(lane < HEAD_DIM, stacked[:rows], stacked[rows:])


def attend_kernel(chunk, q_ref, k_own, k_oth, v_own, v_oth, *refs):
    att_ref, lse_ref, k_all, v_all = refs[-4:]
    rows = q_ref.shape[0]
    k_all[0:rows] = k_own[...]
    k_all[rows:] = k_oth[...]
    v_all[0:rows, 0:PAIR] = v_own[...]
    v_all[rows:, 0:PAIR] = v_oth[...]
    v_all[:, PAIR:] = jnp.ones((2 * rows, PAIR), BF16)
    for start in range(0, rows, chunk):
        at = pl.ds(start, chunk)
        queries = head_stack(q_ref[at] * SCALE)
        scores = mm_nt(queries, k_all[...])
        top = jnp.max(scores, axis=1, keepdims=True)
        both = mm(jnp.exp(scores - top).astype(BF16), v_all[...])
        total = both[:, PAIR:]
        att_ref[at] = head_join(both[:, :PAIR] / total).astype(BF16)
        lse_ref[at] = head_join(top + jnp.log(total))


def attend(q, kv_own, kv_oth, first, count, pairs, earlier=()):
    rows = q.shape[0]
    chunk = 176
    spec = lambda shift: pl.BlockSpec((rows, PAIR), lambda p: (0, p + shift))
    return pl.pallas_call(
        lambda *refs: attend_kernel(chunk, *refs),
        grid=(count,),
        in_specs=[spec(first), spec(first), spec(first), spec(first + pairs), spec(first + pairs)]
        + [pl.BlockSpec(memory_space=pl.ANY)] * len(earlier),
        out_specs=[spec(first)] * 2,
        out_shape=[
            jax.ShapeDtypeStruct((rows, pairs * PAIR), BF16),
            jax.ShapeDtypeStruct((rows, pairs * PAIR), F32),
        ],
        input_output_aliases={5 + i: i for i in range(len(earlier))},
        scratch_shapes=[
            pltpu.VMEM((2 * rows, PAIR), BF16),
            pltpu.VMEM((2 * rows, 2 * PAIR), BF16),
        ],
        compiler_params=pltpu.CompilerParams(vmem_limit_bytes=56 * 1024 * 1024),
        cost_estimate=pl.CostEstimate(
            flops=count * 16 * rows * rows * PAIR,
            bytes_accessed=count * PAIR * rows * 16,
            transcendentals=4 * count * rows * rows,
        ),
        name="attend",
    )(q, kv_own, kv_oth, kv_own, kv_oth, *earlier)


def attend_back_kernel(chunk, q_ref, k_own, k_oth, v_own, v_oth, lse_ref, g_ref, *refs):
    dq_ref, own_ref, oth_ref, k_all, v_all, q_all, g_all, p_all, s_all = refs[-9:]
    rows = q_ref.shape[0]
    k_all[0:rows] = k_own[...]
    k_all[rows:] = k_oth[...]
    v_all[0:rows] = v_own[...]
    v_all[rows:] = v_oth[...]
    for start in range(0, rows, chunk):
        at = pl.ds(start, chunk)
        both = pl.ds(2 * start, 2 * chunk)
        queries = head_stack(q_ref[at] * SCALE)
        grads = head_stack(g_ref[at])
        q_all[both] = queries
        g_all[both] = grads
        lse = jnp.concatenate([lse_ref[at, 0:1], lse_ref[at, HEAD_DIM : HEAD_DIM + 1]], axis=0)
        probs = jnp.exp(mm_nt(queries, k_all[...]) - lse)
        grad_probs = mm_nt(grads, v_all[...])
        inner = jnp.sum(probs * grad_probs, axis=1, keepdims=True)
        grad_scores = (probs * (grad_probs - inner)).astype(BF16)
        p_all[both] = probs.astype(BF16)
        s_all[both] = grad_scores
        dq_ref[at] = (head_join(mm(grad_scores, k_all[...])) * SCALE).astype(BF16)

    dk = mm_tn(q_all[...], s_all[...]).T.astype(BF16)
    own_ref[0] = dk[0:rows]
    oth_ref[0] = dk[rows:]
    dv = mm_tn(g_all[...], p_all[...]).T.astype(BF16)
    own_ref[1] = dv[0:rows]
    oth_ref[1] = dv[rows:]


def attend_back(q, kv_own, kv_oth, lse, grad_att, first, count, pairs, earlier=()):
    rows = q.shape[0]
    chunk = 176
    spec = lambda shift: pl.BlockSpec((rows, PAIR), lambda p: (0, p + shift))
    two = pl.BlockSpec((2, rows, PAIR), lambda p: (0, 0, p + first))
    both = jax.ShapeDtypeStruct((2, rows, pairs * PAIR), BF16)
    return pl.pallas_call(
        lambda *refs: attend_back_kernel(chunk, *refs),
        grid=(count,),
        in_specs=[spec(first), spec(first), spec(first), spec(first + pairs), spec(first + pairs)]
        + [spec(first)] * 2
        + [pl.BlockSpec(memory_space=pl.ANY)] * len(earlier),
        out_specs=[spec(first), two, two],
        out_shape=[jax.ShapeDtypeStruct((rows, pairs * PAIR), BF16), both, both],
        input_output_aliases={7 + i: i for i in range(len(earlier))},
        scratch_shapes=[pltpu.VMEM((2 * rows, PAIR), BF16)] * 4
        + [pltpu.VMEM((2 * rows, 2 * rows), BF16)] * 2,
        compiler_params=pltpu.CompilerParams(vmem_limit_bytes=56 * 1024 * 1024),
        cost_estimate=pl.CostEstimate(
            flops=count * 40 * rows * rows * PAIR,
            bytes_accessed=count * PAIR * rows * 26,
            transcendentals=4 * count * rows * rows,
        ),
        name="attend_back",
    )(q, kv_own, kv_oth, kv_own, kv_oth, lse, grad_att, *earlier)


def join(*values):
    return lax.optimization_barrier(values)


def after(value, *others):
    return lax.optimization_barrier((value,) + others)[0]


def place_kernel(moves, halved, index_ref, own, near, *refs):
    outs = len(refs) - (3 if halved else 2) - 1
    fars, wholes, sems = refs[: -outs - 1], refs[-outs - 1 : -1], refs[-1]
    j, y = index_ref[0], index_ref[1]
    x, c = j // 2, j % 2
    rows = own.shape[1]
    across = rows * (2 * (1 - x) + c)
    beside = rows * (2 * (1 - x) + 1 - c)
    pieces = [(own, rows * j), (near, rows * (2 * x + 1 - c))]
    if halved:
        half = rows // 2
        pieces += [
            (fars[0], across + half * y),
            (fars[1], across + half * (1 - y)),
            (fars[2].at[0], beside + half * y),
            (fars[2].at[1], beside + half * (1 - y)),
        ]
    else:
        half = rows
        pieces += [(fars[0], across), (fars[1], beside)]
    copies = []
    for piece, row in pieces:
        at = pl.ds(pl.multiple_of(row, half), piece.shape[1])
        for move in moves:
            source, target = move(piece, wholes, at)
            copies.append(pltpu.make_async_copy(source, target, sems.at[len(copies)]))
    for copy in copies:
        copy.start()
    for copy in copies:
        copy.wait()


def place(index, parts, moves, *shapes):
    anywhere = pl.BlockSpec(memory_space=pl.ANY)
    halved = len(parts) == 5
    return pl.pallas_call(
        lambda *refs: place_kernel(moves, halved, *refs),
        in_specs=[pl.BlockSpec(memory_space=pltpu.SMEM)] + [anywhere] * len(parts),
        out_specs=[pl.BlockSpec(memory_space=pltpu.VMEM)] * len(shapes),
        out_shape=[jax.ShapeDtypeStruct(shape, BF16) for shape in shapes],
        scratch_shapes=[pltpu.SemaphoreType.DMA(((6 if halved else 4) * len(moves),))],
        compiler_params=pltpu.CompilerParams(vmem_limit_bytes=16 * 1024 * 1024),
        cost_estimate=pl.CostEstimate(
            flops=0, bytes_accessed=sum(4 * math.prod(shape) for shape in shapes), transcendentals=0
        ),
        name="place",
    )(index, *parts)


ROW_MOVES = [lambda piece, wholes, at: (piece.at[0], wholes[0].at[at])]
TAP_MOVES = [lambda piece, wholes, at: (piece, wholes[0].at[:, at])]


def block_moves(blocks, width):
    def move(block):
        columns = pl.ds(block * width, width)
        return lambda piece, wholes, at: (piece.at[1 + block], wholes[1].at[at, columns])

    return ROW_MOVES + [move(block) for block in range(blocks)]


def round_sum(*terms):
    return sum(term.astype(F32) for term in terms).astype(BF16)


def dp_bits():
    bits = [1]
    while 2 * bits[-1] < lax.axis_size("dp"):
        bits.append(2 * bits[-1])
    return bits


def over_dp(block, bit):
    return lax.ppermute(block, "dp", [(d, d ^ bit) for d in range(lax.axis_size("dp"))])


def dp_side(bit):
    return (lax.axis_index("dp") // bit) % 2


class Terms:
    def __init__(self, array, names):
        self.terms, self.fixed = [(array, tuple(names))], {}

    def view(self, chosen):
        def cut(array, names):
            axis = 0
            for name in names:
                if name in chosen:
                    array = pick(array, chosen[name], axis)
                else:
                    axis += 1
            return array

        return round_sum(*[cut(array, names) for array, names in self.terms])

    def hop(self, name, side, ship):
        block = self.view({**self.fixed, name: 1 - side})
        names = tuple(n for n in self.terms[0][1] if n not in self.fixed and n != name)
        self.fixed[name] = side
        self.terms.append((ship(block), names))

    def dp_hop(self, bit):
        self.hop(bit, dp_side(bit), lambda block: over_dp(block, bit))

    def quad_hop(self, pair):
        sides = [dp_side(bit) for bit in pair]
        names = tuple(n for n in self.terms[0][1] if n not in self.fixed and n not in pair)
        arrived = []
        for other in (1, 2, 3):
            place = {pair[0]: (sides[0] + other // 2) % 2, pair[1]: (sides[1] + other) % 2}
            arrived.append(quad_send(self.view({**self.fixed, **place}), pair, other))
        self.fixed.update(zip(pair, sides))
        self.terms += [(block, names) for block in arrived]

    def rest_hops(self):
        for group in rest_groups():
            if len(group) == 2:
                self.quad_hop(group)
            else:
                self.dp_hop(group[0])

    def total(self):
        return self.view(self.fixed)

    @property
    def arrays(self):
        return [array for array, _ in self.terms]

    @arrays.setter
    def arrays(self, arrays):
        self.terms = [(array, names) for array, (_, names) in zip(arrays, self.terms)]


def tie(sums, *main):
    lists, main = lax.optimization_barrier(([t.arrays for t in sums], main))
    for t, arrays in zip(sums, lists):
        t.arrays = arrays
    return main[0] if len(main) == 1 else main


class Gather:
    def __init__(self, share, axis=0):
        self.share, self.axis, self.group, self.arrived = share, axis, (), []

    def settle(self):
        sides = [dp_side(bit) == 0 for bit in self.group]
        if len(sides) == 1:
            self.share = ordered(sides[0], self.share, self.arrived[0], self.axis)
        elif len(sides) == 2:
            near, far, last = self.arrived
            own_pair = ordered(sides[1], self.share, near, self.axis)
            far_pair = ordered(sides[1], far, last, self.axis)
            self.share = ordered(sides[0], own_pair, far_pair, self.axis)
        self.group, self.arrived = (), []
        return self.share

    def hop(self, group):
        share = self.settle()
        self.group = group
        if len(group) == 1:
            self.arrived = [over_dp(share, group[0])]
        else:
            self.arrived = [quad_send(share, group, other) for other in (1, 2, 3)]

    def rest_hops(self):
        for group in reversed(rest_groups()):
            self.hop(group)

    @property
    def arrays(self):
        return [self.share] + self.arrived

    @arrays.setter
    def arrays(self, arrays):
        self.share, self.arrived = arrays[0], list(arrays[1:])


def rest_groups():
    bits = dp_bits()[1:]
    return [tuple(bits[k : k + 2]) for k in range(0, len(bits), 2)]


def quad_send(block, pair, other):
    flip = pair[0] * (other // 2) + pair[1] * (other % 2)
    return lax.ppermute(block, "dp", [(d, d ^ flip) for d in range(lax.axis_size("dp"))])


def on_device(
    mel,
    lang_group,
    clip_count,
    conv_one,
    conv_one_bias,
    conv_two,
    conv_two_bias,
    lang_table,
    ln_one_gain,
    ln_one_bias,
    w_qkv,
    q_bias,
    v_bias,
    w_out,
    out_bias,
    ln_two_gain,
    ln_two_bias,
    w_fc_one,
    fc_one_bias,
    w_fc_two,
    fc_two_bias,
    grad_out,
):
    slots, part, width = grad_out.shape
    hidden = w_fc_one.shape[1]
    pairs = width // PAIR
    quarter = width // 4
    mels = mel.shape[2]
    rows = slots * part
    j = lax.axis_index("chan")
    x, c = j // 2, j % 2
    live = (x < clip_count[lax.axis_index("dp")]).astype(F32)

    def to_clip(block):
        same = send(pick(block, c, 0), SAME)
        other = send(pick(block, 1 - c, 0), OTHER)
        return ordered(x == 0, same, other)

    def send_back(block):
        half = block.shape[0] // 2
        first, second = block[:half], block[half:]
        same = send(jnp.where(x == 0, first, second), SAME_BACK)
        return same, send(jnp.where(x == 0, second, first), OTHER_BACK)

    def take_back(same, other):
        return ordered(c == 0, same, other, stack=True)

    mel_pairs = mel.reshape(slots, part, 2 * mels)
    edge = send(jnp.where(j == 1, mel_pairs[1, -1], mel_pairs[0, 0]), [(1, 3), (2, 0)])
    edge = jnp.where(j == 1, mel_pairs[0, -1], jnp.where(j == 2, mel_pairs[1, 0], edge))
    zero_edge = jnp.zeros_like(edge)
    mel_own = jnp.concatenate(
        [
            jnp.where(c == 1, edge, zero_edge)[None],
            to_clip(mel_pairs),
            jnp.where(c == 0, edge, zero_edge)[None],
        ]
    )

    y = lax.axis_index("dp") % 2
    index = jnp.stack([j, y])
    one_part = jnp.concatenate([conv_one.T, conv_one_bias[:, None]], axis=1)
    one_across = send(one_part, CROSS)
    one_column = ordered(x == 0, one_part, one_across, stack=True)
    one_whole = ordered(c == 0, one_column, send(one_column, CORE), 1, stack=True)
    one_whole = one_whole.reshape(width, -1)

    def cross_half(own):
        half = own.shape[1] // 2
        return send(lax.dynamic_slice_in_dim(own, y * half, half, 1), CROSS)

    def cross_rest(far):
        return over_dp(far, 1)

    def beside(far, rest):
        return send(jnp.stack([far, rest]), CORE)

    blocks = hidden // width
    up_part = jnp.stack(
        [w_out] + [w_fc_one[:, k * width : (k + 1) * width] for k in range(blocks)]
    )
    qkv_part, down_part = w_qkv[None], w_fc_two[None]
    two_across = send(conv_two, CROSS)
    two_near = send(conv_two, CORE)

    even, odd = mel_own[:, :mels], mel_own[:, mels:]
    ones = jnp.ones((rows, 1), BF16)
    cols_even = jnp.concatenate([odd[0:rows], even[1 : rows + 1], odd[1 : rows + 1], ones], axis=1)
    cols_odd = jnp.concatenate(
        [even[1 : rows + 1], odd[1 : rows + 1], even[2 : rows + 2], ones], axis=1
    )
    cols_edge = jnp.concatenate([even[0:1], odd[0:1], even[1:2], ones[0:1]], axis=1)
    hid_even, slope_even = gelu_both(mm_nt(cols_even, one_whole))
    hid_odd, slope_odd = gelu_both(mm_nt(cols_odd, one_whole))
    hid_edge, _ = gelu_both(mm_nt(cols_edge, one_whole))
    hid_edge = jnp.where(c == 1, hid_edge, 0.0)
    hid_even, hid_odd, hid_edge = hid_even.astype(BF16), hid_odd.astype(BF16), hid_edge.astype(BF16)
    slope_even, slope_odd = slope_even.astype(BF16), slope_odd.astype(BF16)
    hid_even, hid_odd, hid_edge, slope_even, slope_odd, two_across, up_part = join(
        hid_even, hid_odd, hid_edge, slope_even, slope_odd, two_across, up_part
    )
    two_beside = send(two_across, CORE)
    qkv_across = send(after(qkv_part, two_across), CROSS)
    hid_prev = jnp.concatenate([hid_edge, hid_odd[:-1]])
    hid_taps = jnp.concatenate([hid_prev, hid_even, hid_odd], axis=1)
    group = pick(lang_group, x, 0)
    place_rows = positions(rows, width, after(c * rows, two_across))
    place_rows += pick(lang_table, group, 0).astype(F32)[None]
    place_rows, hid_taps, two_beside = join(place_rows, hid_taps, two_beside)
    (two_full,) = place(
        index, (conv_two, two_near, two_across, two_beside), TAP_MOVES, (3, width, width)
    )
    two_full = two_full.reshape(-1, width)
    stem_act, slope_two = gelu_both(mm(hid_taps, two_full) + conv_two_bias.astype(F32))
    slope_two = slope_two.astype(BF16)
    stem = stem_act + place_rows

    gain_one, gain_two = ln_one_gain.astype(F32), ln_two_gain.astype(F32)
    stats_one = norm_stats(stem)
    normed = (
        (stem - stats_one[0]) * stats_one[1] * gain_one + ln_one_bias.astype(F32)
    ).astype(BF16)
    normed, slope_two, qkv_across = join(normed, slope_two, qkv_across)
    qkv_near = send(after(qkv_part, two_across), CORE)
    qkv_beside = send(qkv_across, CORE)
    up_far = cross_half(after(up_part, qkv_across))
    (qkv_full,) = place(
        index, (qkv_part, qkv_near, qkv_across, qkv_beside), ROW_MOVES, (width, 3 * width)
    )
    kv_shift = jnp.concatenate([jnp.zeros((width,), F32), v_bias.astype(F32)])
    kv_own = (mm(normed, qkv_full[:, width:]) + kv_shift).astype(BF16)
    kv_oth = send(kv_own, CORE)
    queries = (mm(normed, qkv_full[:, :width]) + q_bias.astype(F32)).astype(BF16)
    queries, kv_oth = join(queries, kv_oth)
    half = pairs // 2
    partial = attend(queries, kv_own, kv_oth, 0, half, pairs)
    *partial, up_far = join(*partial, up_far)
    up_near = send(after(up_part, up_far), CORE)
    up_rest = cross_rest(up_far)
    down_far = cross_half(after(down_part, up_far))
    attended, lse = attend(queries, kv_own, kv_oth, half, pairs - half, pairs, partial)
    attended, up_near, up_rest, down_far = join(attended, up_near, up_rest, down_far)
    up_beside = beside(up_far, up_rest)
    down_rest = cross_rest(down_far)
    grad_part = after(grad_out, down_far)
    grad_same = send(pick(grad_part, c, 0), SAME)
    grad_other = send(pick(grad_part, 1 - c, 0), OTHER)
    out_full, up_full = place(
        index,
        (up_part, up_near, up_far, up_rest, up_beside),
        block_moves(blocks, width),
        (width, width),
        (width, hidden),
    )
    residual = stem + mm(attended, out_full) + out_bias.astype(F32)

    stats_two = norm_stats(residual)
    normed_two = (
        (residual - stats_two[0]) * stats_two[1] * gain_two + ln_two_bias.astype(F32)
    ).astype(BF16)
    active, slope_up = gelu_both(mm(normed_two, up_full) + fc_one_bias.astype(F32))
    active, slope_up = active.astype(BF16), slope_up.astype(BF16)

    def owner_terms(grads):
        return Terms(grads.astype(BF16).reshape(2, 2, -1, grads.shape[1]), ["x", "core"])

    def core_hop(terms):
        terms.hop("core", c, lambda block: send(block, CORE))

    def x_hop(terms):
        terms.hop("x", x, lambda block: send(block, CROSS))

    def first_hops(sides):
        x_hop(sides[0])
        sides[1].dp_hop(1)

    def second_hops(sides):
        sides[0].dp_hop(1)
        x_hop(sides[1])

    active, slope_up, down_rest, grad_same, grad_other = join(
        active, slope_up, down_rest, grad_same, grad_other
    )
    cotangent = ordered(x == 0, grad_same, grad_other)
    down_near = send(after(down_part, down_rest), CORE)
    down_parts = (down_part, down_near, down_far, down_rest, beside(down_far, down_rest))
    (down_full,) = place(index, down_parts, ROW_MOVES, (hidden, width))
    grad_mlp = (cotangent.astype(F32) * live).astype(BF16)
    grad_rows = grad_mlp.astype(F32)
    down = owner_terms(mm_tn(active, grad_mlp))
    down_shift = jnp.sum(grad_rows, axis=0)
    grad_mlp = tie([down], grad_mlp)
    core_hop(down)
    grad_upper = (mm_nt(grad_mlp, down_full) * slope_up.astype(F32)).astype(BF16)
    up_shift = jnp.sum(grad_upper.astype(F32), axis=0)
    grad_upper = tie([down], grad_upper)
    x_hop(down)
    up = owner_terms(mm_tn(normed_two, grad_upper))
    grad_upper = tie([up], grad_upper)
    core_hop(up)
    grad_norm, grad_gain_two, grad_shift_two = norm_back(
        residual, stats_two, gain_two, mm_nt(grad_upper, up_full)
    )
    grad_residual = grad_rows + grad_norm
    grad_branch = grad_residual.astype(BF16)
    out_shift = jnp.sum(grad_branch.astype(F32), axis=0)
    out_grads = mm_tn(attended, grad_branch).astype(BF16)
    grad_att = mm_nt(grad_branch, out_full).astype(BF16)
    grad_att, out_grads = tie([up], grad_att, out_grads)

    third = -(-pairs // 3)
    operands = (queries, kv_own, kv_oth, lse)
    bits = dp_bits()
    partial = attend_back(*operands, grad_att, 0, third, pairs)
    partial = tie([down, up], *partial)
    x_hop(up)
    partial = attend_back(*operands, grad_att, third, third, pairs, partial)
    grad_q, own_kv, oth_kv = attend_back(
        *operands, grad_att, 2 * third, pairs - 2 * third, pairs, partial
    )
    grad_q, own_kv, oth_kv = tie([up], grad_q, own_kv, oth_kv)
    oth_kv = send(oth_kv, CORE)
    up_share = up.total()
    ffn = jnp.concatenate(
        [down.total()] + [up_share[:, k * width : (k + 1) * width] for k in range(blocks)]
    )
    ffn = Terms(ffn.reshape((2,) * len(bits) + (-1, width)), bits)
    ffn.dp_hop(1)
    encoded = (residual + mm(after(active, grad_q), down_full) + fc_two_bias.astype(F32)) * live
    encoded, own_kv, oth_kv = join(encoded.astype(BF16), own_kv, oth_kv)
    q_shift = jnp.sum(grad_q.astype(F32), axis=0)
    grad_kv = round_sum(own_kv, oth_kv)
    grad_packed = jnp.concatenate([grad_q, grad_kv[0], grad_kv[1]], axis=1)
    qkv_grads = jnp.concatenate([mm_tn(normed, grad_packed).astype(BF16), out_grads], axis=1)
    v_shift = jnp.sum(grad_kv[1].astype(F32), axis=0)
    qkv = owner_terms(qkv_grads)
    grad_packed = tie([qkv], grad_packed)
    core_hop(qkv)
    encoded = send_back(encoded)
    grad_normed = tie([qkv], mm_nt(grad_packed, qkv_full))

    def split_rows(terms):
        middle = terms.arrays[0].shape[-1] // 2
        sides = []
        for cut in (slice(0, middle), slice(middle, None)):
            side = Terms(None, ())
            side.terms = []
            for array, names in terms.terms:
                part = array[..., cut]
                shape = part.shape[: len(names)] + (2,) * len(bits)
                part = part.reshape(shape + (part.shape[-2] // 2 ** len(bits), middle))
                side.terms.append((part, names + tuple(bits)))
            side.fixed = dict(terms.fixed)
            sides.append(side)
        return sides

    qkv = split_rows(qkv)
    first_hops(qkv)
    grad_norm, grad_gain_one, grad_shift_one = norm_back(stem, stats_one, gain_one, grad_normed)
    grad_stem = grad_residual + grad_norm
    group_hot = (jnp.arange(lang_table.shape[0]) == group).astype(F32)
    grad_lang = group_hot[:, None] * jnp.sum(grad_stem, axis=0)[None]
    grad_two = (grad_stem * slope_two.astype(F32)).astype(BF16)
    two_shift = jnp.sum(grad_two.astype(F32), axis=0)
    grad_two, encoded = join(grad_two, encoded)
    encoded = take_back(*encoded)
    two_grads = mm_tn(hid_taps, grad_two).astype(BF16).reshape(3, 2, 2, quarter, width)
    two = Terms(
        two_grads.transpose(1, 2, 0, 3, 4).reshape(2, 2, 3 * quarter, width), ["x", "core"]
    )
    grad_two = tie([two, ffn], grad_two)
    core_hop(two)
    for bit in bits[1:2]:
        ffn.dp_hop(bit)
    follow = send(grad_two[0:1], [(1, 0), (3, 2)])
    vectors = jnp.concatenate(
        [
            jnp.stack(
                [
                    q_shift, v_shift, grad_gain_one, grad_shift_one, two_shift,
                    down_shift, grad_gain_two, grad_shift_two, out_shift,
                ]
            ),
            up_shift.reshape(-1, width),
            grad_lang,
        ]
    )
    hid_grad_even = mm_nt(grad_two, two_full[width : 2 * width])
    grad_even = (hid_grad_even * slope_even.astype(F32)).astype(BF16)
    grad_even, grad_two, follow, vectors = tie([two, ffn], grad_even, grad_two, follow, vectors)
    two = split_rows(two)
    first_hops(two)
    for bit in bits[2:]:
        ffn.dp_hop(bit)
    vectors += send(vectors, CORE)
    hid_grad_last = mm_nt(grad_two, two_full[2 * width :])
    grad_next = jnp.concatenate([grad_two[1:], follow])
    hid_grad_odd = hid_grad_last + mm_nt(grad_next, two_full[:width])
    grad_odd = (hid_grad_odd * slope_odd.astype(F32)).astype(BF16)
    grad_odd, vectors = tie(qkv + [ffn], grad_odd, vectors)
    second_hops(qkv)
    backs = list(reversed(bits))
    ffn = Gather(ffn.total())
    ffn.hop((backs[0],))
    vectors += send(vectors, CROSS)
    one_grads = mm_tn(grad_even, cols_even) + mm_tn(grad_odd, cols_odd)
    spare = width // 3 - one_grads.shape[1]
    one = owner_terms(jnp.pad(one_grads, ((0, 0), (0, spare))))
    grad_even, grad_odd, vectors = tie([one] + two, grad_even, grad_odd, vectors)
    second_hops(two)
    core_hop(one)
    vectors += over_dp(vectors, 1)
    terms_even = mm(grad_even, one_whole)
    terms_odd = mm(grad_odd, one_whole)
    before, mid_e, late = (terms_even[:, k * mels : (k + 1) * mels] for k in range(3))
    early, mid_o, last = (terms_odd[:, k * mels : (k + 1) * mels] for k in range(3))
    spill = send(jnp.where(c == 0, last[-1:], before[0:1]), CORE)
    zero_spill = jnp.zeros_like(spill)
    last_prev = jnp.concatenate([jnp.where(c == 1, spill, zero_spill), last[:-1]])
    before_next = jnp.concatenate([before[1:], jnp.where(c == 0, spill, zero_spill)])
    mel_grad = jnp.concatenate(
        [mid_e + early + last_prev, late + mid_o + before_next], axis=1
    ).astype(BF16)
    mel_grad, vectors = tie([one, ffn] + qkv, mel_grad, vectors)
    x_hop(one)
    for bit in backs[1:-1]:
        ffn.hop((bit,))
    for side in qkv:
        side.terms, side.fixed = [(side.total(), tuple(bits[1:]))], {}
    qkv = Terms(jnp.stack([side.arrays[0] for side in qkv], axis=len(bits) - 1), bits[1:])
    qkv.rest_hops()
    mel_grad, vectors = tie([one], mel_grad, vectors)
    one_share = one.total()
    one_rows = one_share.shape[0] // 3
    flat = jnp.concatenate([one_share[k * one_rows : (k + 1) * one_rows] for k in range(3)], axis=1)
    flat = Terms(
        jnp.stack([flat[:, : width // 2], flat[:, width // 2 :]]).swapaxes(0, 1).reshape(
            (2,) * len(bits) + (one_rows // 2 ** len(bits), 2, width // 2)
        ).swapaxes(-3, -2),
        bits,
    )
    flat.dp_hop(1)
    mel_grad = send_back(mel_grad)
    mel_grad, vectors = tie([flat, ffn] + two, mel_grad, vectors)
    conv = jnp.stack([side.total() for side in two], axis=len(bits) - 1)
    conv = Terms(jnp.concatenate([conv, flat.total()], axis=-2), bits[1:])
    conv.rest_hops()
    ffn.hop((1,))
    vectors = tie([qkv, conv], vectors)
    qkv = Gather(qkv.total(), 1)
    qkv.rest_hops()
    conv = Gather(conv.total(), 1)
    conv.rest_hops()
    for bit in bits[1:2]:
        vectors += over_dp(vectors, bit)
    mel_grad = take_back(*mel_grad).astype(F32).reshape(slots, 2 * part, mels)
    mel_grad, vectors = tie([qkv, conv, ffn], mel_grad, vectors)
    qkv.hop((1,))
    conv.hop((1,))
    for bit in bits[2:]:
        vectors += over_dp(vectors, bit)
    tie([qkv])
    qkv_share = qkv.settle()
    vectors = tie([conv], vectors)
    conv = conv.settle()
    ffn = ffn.settle().astype(F32)
    down_sum = ffn[: hidden // 4]
    up_sum = jnp.concatenate(
        [ffn[hidden // 4 + k * quarter : hidden // 4 + (k + 1) * quarter] for k in range(blocks)],
        axis=1,
    )

    def columns(sides):
        return jnp.concatenate([sides[0], sides[1]], axis=1).astype(F32)

    qkv_out = columns(qkv_share)
    pieces = 2 ** len(bits)
    conv_pieces = columns(conv).reshape(pieces, -1, width)
    taken = 3 * quarter // pieces
    two_sum = conv_pieces[:, :taken].reshape(conv_two.shape)
    one_flat = conv_pieces[:, taken:].reshape(one_rows, width)
    one_sum = jnp.concatenate(
        [one_flat[:, k * width // 3 : (k + 1) * width // 3] for k in range(3)]
    )
    vec = lambda k: vectors[k]
    return (
        encoded,
        mel_grad,
        one_sum[:, : 3 * mels].T,
        one_sum[:, 3 * mels],
        two_sum,
        vec(4),
        vectors[9 + blocks :],
        vec(2),
        vec(3),
        qkv_out[:, : 3 * width],
        vec(0),
        vec(1),
        qkv_out[:, 3 * width :],
        vec(8),
        vec(6),
        vec(7),
        up_sum,
        vectors[9 : 9 + blocks].reshape(-1),
        down_sum,
        vec(5),
    )


def solution(mesh):
    in_specs = (
        P("dp", "chan", None),
        P("dp"),
        P(),
        P(None, "chan"),
        P("chan"),
        P(None, "chan", None),
        P(),
        P(),
        P(),
        P(),
        P("chan", None),
        P(),
        P(),
        P("chan", None),
        P(),
        P(),
        P(),
        P("chan", None),
        P(),
        P("chan", None),
        P(),
        P("dp", "chan", None),
    )
    out_specs = (
        P("dp", "chan", None),
        P("dp", "chan", None),
        P(None, "chan"),
        P("chan"),
        P(None, "chan", None),
        P(),
        P(),
        P(),
        P(),
        P("chan", None),
        P(),
        P(),
        P("chan", None),
        P(),
        P(),
        P(),
        P("chan", None),
        P(),
        P("chan", None),
        P(),
    )
    return jax.shard_map(
        on_device, mesh=mesh, in_specs=in_specs, out_specs=out_specs, check_vma=False
    )
```

```python
import math

import jax
import jax.numpy as jnp
from jax import lax
from jax.experimental import pallas as pl
from jax.experimental.pallas import tpu as pltpu
from jax.sharding import PartitionSpec as P

HEAD_DIM = 64
PAIR = 2 * HEAD_DIM
SCALE = HEAD_DIM ** (-0.5)
BF16 = jnp.bfloat16
F32 = jnp.float32

CORE = [(j, j ^ 1) for j in range(4)]
CROSS = [(j, j ^ 2) for j in range(4)]
SAME = [(2 * x + c, 2 * c + x) for x in range(2) for c in range(2)]
OTHER = [(2 * x + c, 2 * (1 - c) + x) for x in range(2) for c in range(2)]
SAME_BACK = [(b, a) for a, b in SAME]
OTHER_BACK = [(b, a) for a, b in OTHER]


def send(block, perm):
    return lax.ppermute(block, "chan", perm)


def ordered(first_is_own, own, other, axis=0, stack=False):
    join = jnp.stack if stack else jnp.concatenate
    return jnp.where(first_is_own, join([own, other], axis), join([other, own], axis))


def pick(block, index, axis):
    return lax.dynamic_index_in_dim(block, index, axis, keepdims=False)


def gelu_both(inputs):
    cdf = 0.5 * (1.0 + lax.erf(inputs * math.sqrt(0.5)))
    pdf = jnp.exp(-0.5 * inputs * inputs) * (1.0 / math.sqrt(2.0 * math.pi))
    return inputs * cdf, cdf + inputs * pdf


def norm_stats(inputs):
    row_mean = jnp.mean(inputs, axis=-1, keepdims=True)
    centered = inputs - row_mean
    variance = jnp.mean(centered * centered, axis=-1, keepdims=True)
    return row_mean, lax.rsqrt(variance + 1e-05)


def norm_back(inputs, stats, gain_vec, cotangent):
    row_mean, inverse = stats
    unit = (inputs - row_mean) * inverse
    scaled = cotangent * gain_vec
    mean_one = jnp.mean(scaled, axis=-1, keepdims=True)
    mean_two = jnp.mean(scaled * unit, axis=-1, keepdims=True)
    grad = inverse * (scaled - mean_one - unit * mean_two)
    return grad, jnp.sum(cotangent * unit, axis=0), jnp.sum(cotangent, axis=0)


def positions(frame_count, model_width, first_frame):
    increment = math.log(10000.0) / (model_width // 2 - 1)
    inverse = jnp.exp(-increment * jnp.arange(model_width // 2, dtype=jnp.float32))
    angles = (first_frame + jnp.arange(frame_count)).astype(jnp.float32)[:, None] * inverse[None, :]
    return jnp.concatenate([jnp.sin(angles), jnp.cos(angles)], axis=1)


def mm(left, right):
    return jnp.dot(left, right, preferred_element_type=F32)


def mm_nt(left, right):
    return lax.dot_general(left, right, (((1,), (1,)), ((), ())), preferred_element_type=F32)


def mm_tn(left, right):
    return lax.dot_general(left, right, (((0,), (0,)), ((), ())), preferred_element_type=F32)


def head_stack(block):
    lane = lax.broadcasted_iota(jnp.int32, block.shape, 1)
    zero = jnp.zeros_like(block)
    return jnp.concatenate(
        [jnp.where(lane < HEAD_DIM, block, zero), jnp.where(lane < HEAD_DIM, zero, block)], axis=0
    )


def head_join(stacked):
    rows = stacked.shape[0] // 2
    lane = lax.broadcasted_iota(jnp.int32, (rows, stacked.shape[1]), 1)
    return jnp.where(lane < HEAD_DIM, stacked[:rows], stacked[rows:])


def attend_kernel(chunk, q_ref, k_own, k_oth, v_own, v_oth, *refs):
    att_ref, lse_ref, k_all, v_all = refs[-4:]
    rows = q_ref.shape[0]
    k_all[0:rows] = k_own[...]
    k_all[rows:] = k_oth[...]
    v_all[0:rows, 0:PAIR] = v_own[...]
    v_all[rows:, 0:PAIR] = v_oth[...]
    v_all[:, PAIR:] = jnp.ones((2 * rows, PAIR), BF16)
    for start in range(0, rows, chunk):
        at = pl.ds(start, chunk)
        queries = head_stack(q_ref[at] * SCALE)
        scores = mm_nt(queries, k_all[...])
        top = jnp.max(scores, axis=1, keepdims=True)
        both = mm(jnp.exp(scores - top).astype(BF16), v_all[...])
        total = both[:, PAIR:]
        att_ref[at] = head_join(both[:, :PAIR] / total).astype(BF16)
        lse_ref[at] = head_join(top + jnp.log(total))


def attend(q, kv_own, kv_oth, first, count, pairs, earlier=()):
    rows = q.shape[0]
    chunk = 176
    spec = lambda shift: pl.BlockSpec((rows, PAIR), lambda p: (0, p + shift))
    return pl.pallas_call(
        lambda *refs: attend_kernel(chunk, *refs),
        grid=(count,),
        in_specs=[spec(first), spec(first), spec(first), spec(first + pairs), spec(first + pairs)]
        + [pl.BlockSpec(memory_space=pl.ANY)] * len(earlier),
        out_specs=[spec(first)] * 2,
        out_shape=[
            jax.ShapeDtypeStruct((rows, pairs * PAIR), BF16),
            jax.ShapeDtypeStruct((rows, pairs * PAIR), F32),
        ],
        input_output_aliases={5 + i: i for i in range(len(earlier))},
        scratch_shapes=[
            pltpu.VMEM((2 * rows, PAIR), BF16),
            pltpu.VMEM((2 * rows, 2 * PAIR), BF16),
        ],
        compiler_params=pltpu.CompilerParams(vmem_limit_bytes=56 * 1024 * 1024),
        cost_estimate=pl.CostEstimate(
            flops=count * 16 * rows * rows * PAIR,
            bytes_accessed=count * PAIR * rows * 16,
            transcendentals=4 * count * rows * rows,
        ),
        name="attend",
    )(q, kv_own, kv_oth, kv_own, kv_oth, *earlier)


def attend_back_kernel(chunk, q_ref, k_own, k_oth, v_own, v_oth, lse_ref, g_ref, *refs):
    dq_ref, own_ref, oth_ref, k_all, v_all, q_all, g_all, p_all, s_all = refs[-9:]
    rows = q_ref.shape[0]
    k_all[0:rows] = k_own[...]
    k_all[rows:] = k_oth[...]
    v_all[0:rows] = v_own[...]
    v_all[rows:] = v_oth[...]
    for start in range(0, rows, chunk):
        at = pl.ds(start, chunk)
        both = pl.ds(2 * start, 2 * chunk)
        queries = head_stack(q_ref[at] * SCALE)
        grads = head_stack(g_ref[at])
        q_all[both] = queries
        g_all[both] = grads
        lse = jnp.concatenate([lse_ref[at, 0:1], lse_ref[at, HEAD_DIM : HEAD_DIM + 1]], axis=0)
        probs = jnp.exp(mm_nt(queries, k_all[...]) - lse)
        grad_probs = mm_nt(grads, v_all[...])
        inner = jnp.sum(probs * grad_probs, axis=1, keepdims=True)
        grad_scores = (probs * (grad_probs - inner)).astype(BF16)
        p_all[both] = probs.astype(BF16)
        s_all[both] = grad_scores
        dq_ref[at] = (head_join(mm(grad_scores, k_all[...])) * SCALE).astype(BF16)

    dk = mm_tn(q_all[...], s_all[...]).T.astype(BF16)
    own_ref[0] = dk[0:rows]
    oth_ref[0] = dk[rows:]
    dv = mm_tn(g_all[...], p_all[...]).T.astype(BF16)
    own_ref[1] = dv[0:rows]
    oth_ref[1] = dv[rows:]


def attend_back(q, kv_own, kv_oth, lse, grad_att, first, count, pairs, earlier=()):
    rows = q.shape[0]
    chunk = 176
    spec = lambda shift: pl.BlockSpec((rows, PAIR), lambda p: (0, p + shift))
    two = pl.BlockSpec((2, rows, PAIR), lambda p: (0, 0, p + first))
    both = jax.ShapeDtypeStruct((2, rows, pairs * PAIR), BF16)
    return pl.pallas_call(
        lambda *refs: attend_back_kernel(chunk, *refs),
        grid=(count,),
        in_specs=[spec(first), spec(first), spec(first), spec(first + pairs), spec(first + pairs)]
        + [spec(first)] * 2
        + [pl.BlockSpec(memory_space=pl.ANY)] * len(earlier),
        out_specs=[spec(first), two, two],
        out_shape=[jax.ShapeDtypeStruct((rows, pairs * PAIR), BF16), both, both],
        input_output_aliases={7 + i: i for i in range(len(earlier))},
        scratch_shapes=[pltpu.VMEM((2 * rows, PAIR), BF16)] * 4
        + [pltpu.VMEM((2 * rows, 2 * rows), BF16)] * 2,
        compiler_params=pltpu.CompilerParams(vmem_limit_bytes=56 * 1024 * 1024),
        cost_estimate=pl.CostEstimate(
            flops=count * 40 * rows * rows * PAIR,
            bytes_accessed=count * PAIR * rows * 26,
            transcendentals=4 * count * rows * rows,
        ),
        name="attend_back",
    )(q, kv_own, kv_oth, kv_own, kv_oth, lse, grad_att, *earlier)


def join(*values):
    return lax.optimization_barrier(values)


def after(value, *others):
    return lax.optimization_barrier((value,) + others)[0]


def place_kernel(moves, halved, index_ref, own, near, *refs):
    outs = len(refs) - (3 if halved else 2) - 1
    fars, wholes, sems = refs[: -outs - 1], refs[-outs - 1 : -1], refs[-1]
    j, y = index_ref[0], index_ref[1]
    x, c = j // 2, j % 2
    rows = own.shape[1]
    across = rows * (2 * (1 - x) + c)
    beside = rows * (2 * (1 - x) + 1 - c)
    pieces = [(own, rows * j), (near, rows * (2 * x + 1 - c))]
    if halved:
        half = rows // 2
        pieces += [
            (fars[0], across + half * y),
            (fars[1], across + half * (1 - y)),
            (fars[2].at[0], beside + half * y),
            (fars[2].at[1], beside + half * (1 - y)),
        ]
    else:
        half = rows
        pieces += [(fars[0], across), (fars[1], beside)]
    copies = []
    for piece, row in pieces:
        at = pl.ds(pl.multiple_of(row, half), piece.shape[1])
        for move in moves:
            source, target = move(piece, wholes, at)
            copies.append(pltpu.make_async_copy(source, target, sems.at[len(copies)]))
    for copy in copies:
        copy.start()
    for copy in copies:
        copy.wait()


def place(index, parts, moves, *shapes):
    anywhere = pl.BlockSpec(memory_space=pl.ANY)
    halved = len(parts) == 5
    return pl.pallas_call(
        lambda *refs: place_kernel(moves, halved, *refs),
        in_specs=[pl.BlockSpec(memory_space=pltpu.SMEM)] + [anywhere] * len(parts),
        out_specs=[pl.BlockSpec(memory_space=pltpu.VMEM)] * len(shapes),
        out_shape=[jax.ShapeDtypeStruct(shape, BF16) for shape in shapes],
        scratch_shapes=[pltpu.SemaphoreType.DMA(((6 if halved else 4) * len(moves),))],
        compiler_params=pltpu.CompilerParams(vmem_limit_bytes=16 * 1024 * 1024),
        cost_estimate=pl.CostEstimate(
            flops=0, bytes_accessed=sum(4 * math.prod(shape) for shape in shapes), transcendentals=0
        ),
        name="place",
    )(index, *parts)


ROW_MOVES = [lambda piece, wholes, at: (piece.at[0], wholes[0].at[at])]
TAP_MOVES = [lambda piece, wholes, at: (piece, wholes[0].at[:, at])]


def block_moves(blocks, width):
    def move(block):
        columns = pl.ds(block * width, width)
        return lambda piece, wholes, at: (piece.at[1 + block], wholes[1].at[at, columns])

    return ROW_MOVES + [move(block) for block in range(blocks)]


def round_sum(*terms):
    return sum(term.astype(F32) for term in terms).astype(BF16)


def dp_bits():
    bits = [1]
    while 2 * bits[-1] < lax.axis_size("dp"):
        bits.append(2 * bits[-1])
    return bits


def over_dp(block, bit):
    return lax.ppermute(block, "dp", [(d, d ^ bit) for d in range(lax.axis_size("dp"))])


def dp_side(bit):
    return (lax.axis_index("dp") // bit) % 2


class Terms:
    def __init__(self, array, names):
        self.terms, self.fixed = [(array, tuple(names))], {}

    def view(self, chosen):
        def cut(array, names):
            axis = 0
            for name in names:
                if name in chosen:
                    array = pick(array, chosen[name], axis)
                else:
                    axis += 1
            return array

        return round_sum(*[cut(array, names) for array, names in self.terms])

    def hop(self, name, side, ship):
        block = self.view({**self.fixed, name: 1 - side})
        names = tuple(n for n in self.terms[0][1] if n not in self.fixed and n != name)
        self.fixed[name] = side
        self.terms.append((ship(block), names))

    def dp_hop(self, bit):
        self.hop(bit, dp_side(bit), lambda block: over_dp(block, bit))

    def quad_hop(self, pair):
        sides = [dp_side(bit) for bit in pair]
        names = tuple(n for n in self.terms[0][1] if n not in self.fixed and n not in pair)
        arrived = []
        for other in (1, 2, 3):
            place = {pair[0]: (sides[0] + other // 2) % 2, pair[1]: (sides[1] + other) % 2}
            arrived.append(quad_send(self.view({**self.fixed, **place}), pair, other))
        self.fixed.update(zip(pair, sides))
        self.terms += [(block, names) for block in arrived]

    def rest_hops(self):
        for group in rest_groups():
            if len(group) == 2:
                self.quad_hop(group)
            else:
                self.dp_hop(group[0])

    def total(self):
        return self.view(self.fixed)

    @property
    def arrays(self):
        return [array for array, _ in self.terms]

    @arrays.setter
    def arrays(self, arrays):
        self.terms = [(array, names) for array, (_, names) in zip(arrays, self.terms)]


def tie(sums, *main):
    lists, main = lax.optimization_barrier(([t.arrays for t in sums], main))
    for t, arrays in zip(sums, lists):
        t.arrays = arrays
    return main[0] if len(main) == 1 else main


class Gather:
    def __init__(self, share, axis=0):
        self.share, self.axis, self.group, self.arrived = share, axis, (), []

    def settle(self):
        sides = [dp_side(bit) == 0 for bit in self.group]
        if len(sides) == 1:
            self.share = ordered(sides[0], self.share, self.arrived[0], self.axis)
        elif len(sides) == 2:
            near, far, last = self.arrived
            own_pair = ordered(sides[1], self.share, near, self.axis)
            far_pair = ordered(sides[1], far, last, self.axis)
            self.share = ordered(sides[0], own_pair, far_pair, self.axis)
        self.group, self.arrived = (), []
        return self.share

    def hop(self, group):
        share = self.settle()
        self.group = group
        if len(group) == 1:
            self.arrived = [over_dp(share, group[0])]
        else:
            self.arrived = [quad_send(share, group, other) for other in (1, 2, 3)]

    def rest_hops(self):
        for group in reversed(rest_groups()):
            self.hop(group)

    @property
    def arrays(self):
        return [self.share] + self.arrived

    @arrays.setter
    def arrays(self, arrays):
        self.share, self.arrived = arrays[0], list(arrays[1:])


def rest_groups():
    bits = dp_bits()[1:]
    return [tuple(bits[k : k + 2]) for k in range(0, len(bits), 2)]


def quad_send(block, pair, other):
    flip = pair[0] * (other // 2) + pair[1] * (other % 2)
    return lax.ppermute(block, "dp", [(d, d ^ flip) for d in range(lax.axis_size("dp"))])


def on_device(
    mel,
    lang_group,
    clip_count,
    conv_one,
    conv_one_bias,
    conv_two,
    conv_two_bias,
    lang_table,
    ln_one_gain,
    ln_one_bias,
    w_qkv,
    q_bias,
    v_bias,
    w_out,
    out_bias,
    ln_two_gain,
    ln_two_bias,
    w_fc_one,
    fc_one_bias,
    w_fc_two,
    fc_two_bias,
    grad_out,
):
    slots, part, width = grad_out.shape
    hidden = w_fc_one.shape[1]
    pairs = width // PAIR
    quarter = width // 4
    mels = mel.shape[2]
    rows = slots * part
    j = lax.axis_index("chan")
    x, c = j // 2, j % 2
    live = (x < clip_count[lax.axis_index("dp")]).astype(F32)

    def to_clip(block):
        same = send(pick(block, c, 0), SAME)
        other = send(pick(block, 1 - c, 0), OTHER)
        return ordered(x == 0, same, other)

    def send_back(block):
        half = block.shape[0] // 2
        first, second = block[:half], block[half:]
        same = send(jnp.where(x == 0, first, second), SAME_BACK)
        return same, send(jnp.where(x == 0, second, first), OTHER_BACK)

    def take_back(same, other):
        return ordered(c == 0, same, other, stack=True)

    mel_pairs = mel.reshape(slots, part, 2 * mels)
    edge = send(jnp.where(j == 1, mel_pairs[1, -1], mel_pairs[0, 0]), [(1, 3), (2, 0)])
    edge = jnp.where(j == 1, mel_pairs[0, -1], jnp.where(j == 2, mel_pairs[1, 0], edge))
    zero_edge = jnp.zeros_like(edge)
    mel_own = jnp.concatenate(
        [
            jnp.where(c == 1, edge, zero_edge)[None],
            to_clip(mel_pairs),
            jnp.where(c == 0, edge, zero_edge)[None],
        ]
    )

    y = lax.axis_index("dp") % 2
    index = jnp.stack([j, y])
    one_part = jnp.concatenate([conv_one.T, conv_one_bias[:, None]], axis=1)
    blocks = hidden // width
    up_part = jnp.stack(
        [w_out] + [w_fc_one[:, k * width : (k + 1) * width] for k in range(blocks)]
    )
    one_across = send(one_part, CROSS)
    qkv_part, down_part = w_qkv[None], w_fc_two[None]
    two_across = send(conv_two, CROSS)
    one_across, up_part, two_across = join(one_across, up_part, two_across)
    one_column = ordered(x == 0, one_part, one_across, stack=True)
    one_whole = ordered(c == 0, one_column, send(one_column, CORE), 1, stack=True)
    one_whole = one_whole.reshape(width, -1)

    def cross_half(own, side=y):
        half = own.shape[1] // 2
        return send(lax.dynamic_slice_in_dim(own, side * half, half, 1), CROSS)

    def cross_rest(far):
        return over_dp(far, 1)

    def beside(far, rest):
        return send(jnp.stack([far, rest]), CORE)

    two_near = send(conv_two, CORE)
    qkv_far = cross_half(after(qkv_part, two_across))

    mel_own, one_whole, qkv_far = join(mel_own, one_whole, qkv_far)
    two_beside = send(two_across, CORE)
    qkv_rest = cross_half(after(qkv_part, qkv_far), 1 - y)
    even, odd = mel_own[:, :mels], mel_own[:, mels:]
    ones = jnp.ones((rows, 1), BF16)
    cols_even = jnp.concatenate([odd[0:rows], even[1 : rows + 1], odd[1 : rows + 1], ones], axis=1)
    cols_odd = jnp.concatenate(
        [even[1 : rows + 1], odd[1 : rows + 1], even[2 : rows + 2], ones], axis=1
    )
    cols_edge = jnp.concatenate([even[0:1], odd[0:1], even[1:2], ones[0:1]], axis=1)
    hid_even, slope_even = gelu_both(mm_nt(cols_even, one_whole))
    hid_odd, slope_odd = gelu_both(mm_nt(cols_odd, one_whole))
    hid_edge, _ = gelu_both(mm_nt(cols_edge, one_whole))
    hid_edge = jnp.where(c == 1, hid_edge, 0.0)
    hid_even, hid_odd, hid_edge = hid_even.astype(BF16), hid_odd.astype(BF16), hid_edge.astype(BF16)
    slope_even, slope_odd = slope_even.astype(BF16), slope_odd.astype(BF16)
    hid_even, hid_odd, hid_edge, slope_even, slope_odd, two_beside = join(
        hid_even, hid_odd, hid_edge, slope_even, slope_odd, two_beside
    )
    hid_prev = jnp.concatenate([hid_edge, hid_odd[:-1]])
    hid_taps = jnp.concatenate([hid_prev, hid_even, hid_odd], axis=1)
    group = pick(lang_group, x, 0)
    place_rows = positions(rows, width, after(c * rows, hid_edge))
    place_rows += pick(lang_table, group, 0).astype(F32)[None]
    place_rows, hid_taps, qkv_rest = join(place_rows, hid_taps, qkv_rest)
    qkv_near = send(after(qkv_part, qkv_rest), CORE)
    qkv_beside = beside(qkv_far, qkv_rest)
    (two_full,) = place(
        index, (conv_two, two_near, two_across, two_beside), TAP_MOVES, (3, width, width)
    )
    two_full = two_full.reshape(-1, width)
    stem_act, slope_two = gelu_both(mm(hid_taps, two_full) + conv_two_bias.astype(F32))
    slope_two = slope_two.astype(BF16)
    stem = stem_act + place_rows

    gain_one, gain_two = ln_one_gain.astype(F32), ln_two_gain.astype(F32)
    stats_one = norm_stats(stem)
    normed = (
        (stem - stats_one[0]) * stats_one[1] * gain_one + ln_one_bias.astype(F32)
    ).astype(BF16)
    normed, slope_two, qkv_near, qkv_beside = join(normed, slope_two, qkv_near, qkv_beside)
    up_far = cross_half(after(up_part, qkv_rest))
    (qkv_full,) = place(
        index, (qkv_part, qkv_near, qkv_far, qkv_rest, qkv_beside), ROW_MOVES, (width, 3 * width)
    )
    kv_shift = jnp.concatenate([jnp.zeros((width,), F32), v_bias.astype(F32)])
    kv_own = (mm(normed, qkv_full[:, width:]) + kv_shift).astype(BF16)
    kv_oth = send(kv_own, CORE)
    queries = (mm(normed, qkv_full[:, :width]) + q_bias.astype(F32)).astype(BF16)
    queries, kv_oth = join(queries, kv_oth)
    half = pairs // 2
    partial = attend(queries, kv_own, kv_oth, 0, half, pairs)
    *partial, up_far = join(*partial, up_far)
    up_near = send(after(up_part, up_far), CORE)
    up_rest = cross_rest(up_far)
    down_far = cross_half(after(down_part, up_far))
    down_near = send(after(down_part, up_far), CORE)
    attended, lse = attend(queries, kv_own, kv_oth, half, pairs - half, pairs, partial)
    attended, up_near, up_rest, down_far, down_near = join(
        attended, up_near, up_rest, down_far, down_near
    )
    up_beside = beside(up_far, up_rest)
    down_rest = cross_rest(down_far)
    grad_part = after(grad_out, down_far)
    grad_same = send(pick(grad_part, c, 0), SAME)
    grad_other = send(pick(grad_part, 1 - c, 0), OTHER)
    out_full, up_full = place(
        index,
        (up_part, up_near, up_far, up_rest, up_beside),
        block_moves(blocks, width),
        (width, width),
        (width, hidden),
    )
    residual = stem + mm(attended, out_full) + out_bias.astype(F32)

    stats_two = norm_stats(residual)
    normed_two = (
        (residual - stats_two[0]) * stats_two[1] * gain_two + ln_two_bias.astype(F32)
    ).astype(BF16)
    active, slope_up = gelu_both(mm(normed_two, up_full) + fc_one_bias.astype(F32))
    active, slope_up = active.astype(BF16), slope_up.astype(BF16)

    def owner_terms(grads):
        return Terms(grads.astype(BF16).reshape(2, 2, -1, grads.shape[1]), ["x", "core"])

    def core_hop(terms):
        terms.hop("core", c, lambda block: send(block, CORE))

    def x_hop(terms):
        terms.hop("x", x, lambda block: send(block, CROSS))

    def first_hops(sides):
        x_hop(sides[0])
        sides[1].dp_hop(1)

    def second_hops(sides):
        sides[0].dp_hop(1)
        x_hop(sides[1])

    active, slope_up, down_rest, grad_same, grad_other = join(
        active, slope_up, down_rest, grad_same, grad_other
    )
    cotangent = ordered(x == 0, grad_same, grad_other)
    down_parts = (down_part, down_near, down_far, down_rest, beside(down_far, down_rest))
    (down_full,) = place(index, down_parts, ROW_MOVES, (hidden, width))
    grad_mlp = (cotangent.astype(F32) * live).astype(BF16)
    grad_rows = grad_mlp.astype(F32)
    down = owner_terms(mm_tn(active, grad_mlp))
    down_shift = jnp.sum(grad_rows, axis=0)
    grad_mlp = tie([down], grad_mlp)
    core_hop(down)
    grad_upper = (mm_nt(grad_mlp, down_full) * slope_up.astype(F32)).astype(BF16)
    up_shift = jnp.sum(grad_upper.astype(F32), axis=0)
    grad_upper = tie([down], grad_upper)
    x_hop(down)
    up = owner_terms(mm_tn(normed_two, grad_upper))
    grad_upper = tie([up], grad_upper)
    core_hop(up)
    grad_norm, grad_gain_two, grad_shift_two = norm_back(
        residual, stats_two, gain_two, mm_nt(grad_upper, up_full)
    )
    grad_residual = grad_rows + grad_norm
    grad_branch = grad_residual.astype(BF16)
    out_shift = jnp.sum(grad_branch.astype(F32), axis=0)
    out_grads = mm_tn(attended, grad_branch).astype(BF16)
    grad_att = mm_nt(grad_branch, out_full).astype(BF16)
    grad_att, out_grads = tie([up], grad_att, out_grads)

    third = -(-pairs // 3)
    operands = (queries, kv_own, kv_oth, lse)
    bits = dp_bits()
    partial = attend_back(*operands, grad_att, 0, third, pairs)
    partial = tie([down, up], *partial)
    x_hop(up)
    partial = attend_back(*operands, grad_att, third, third, pairs, partial)
    grad_q, own_kv, oth_kv = attend_back(
        *operands, grad_att, 2 * third, pairs - 2 * third, pairs, partial
    )
    grad_q, own_kv, oth_kv = tie([up], grad_q, own_kv, oth_kv)
    oth_kv = send(oth_kv, CORE)
    up_share = up.total()
    ffn = jnp.concatenate(
        [down.total()] + [up_share[:, k * width : (k + 1) * width] for k in range(blocks)]
    )
    ffn = Terms(ffn.reshape((2,) * len(bits) + (-1, width)), bits)
    ffn.dp_hop(1)
    encoded = (residual + mm(after(active, grad_q), down_full) + fc_two_bias.astype(F32)) * live
    encoded, own_kv, oth_kv = join(encoded.astype(BF16), own_kv, oth_kv)
    q_shift = jnp.sum(grad_q.astype(F32), axis=0)
    grad_kv = round_sum(own_kv, oth_kv)
    grad_packed = jnp.concatenate([grad_q, grad_kv[0], grad_kv[1]], axis=1)
    qkv_grads = jnp.concatenate([mm_tn(normed, grad_packed).astype(BF16), out_grads], axis=1)
    v_shift = jnp.sum(grad_kv[1].astype(F32), axis=0)
    qkv = owner_terms(qkv_grads)
    grad_packed = tie([qkv], grad_packed)
    core_hop(qkv)
    encoded = send_back(encoded)
    grad_normed = tie([qkv], mm_nt(grad_packed, qkv_full))

    def split_rows(terms):
        middle = terms.arrays[0].shape[-1] // 2
        sides = []
        for cut in (slice(0, middle), slice(middle, None)):
            side = Terms(None, ())
            side.terms = []
            for array, names in terms.terms:
                part = array[..., cut]
                shape = part.shape[: len(names)] + (2,) * len(bits)
                part = part.reshape(shape + (part.shape[-2] // 2 ** len(bits), middle))
                side.terms.append((part, names + tuple(bits)))
            side.fixed = dict(terms.fixed)
            sides.append(side)
        return sides

    qkv = split_rows(qkv)
    first_hops(qkv)
    grad_norm, grad_gain_one, grad_shift_one = norm_back(stem, stats_one, gain_one, grad_normed)
    grad_stem = grad_residual + grad_norm
    group_hot = (jnp.arange(lang_table.shape[0]) == group).astype(F32)
    grad_lang = group_hot[:, None] * jnp.sum(grad_stem, axis=0)[None]
    grad_two = (grad_stem * slope_two.astype(F32)).astype(BF16)
    two_shift = jnp.sum(grad_two.astype(F32), axis=0)
    two_grads = mm_tn(hid_taps, grad_two).astype(BF16).reshape(3, 2, 2, quarter, width)
    two = Terms(
        two_grads.transpose(1, 2, 0, 3, 4).reshape(2, 2, 3 * quarter, width), ["x", "core"]
    )
    grad_two, encoded = tie([two, ffn], grad_two, encoded)
    encoded = take_back(*encoded)
    core_hop(two)
    for bit in bits[1:2]:
        ffn.dp_hop(bit)
    follow = send(grad_two[0:1], [(1, 0), (3, 2)])
    vectors = jnp.concatenate(
        [
            jnp.stack(
                [
                    q_shift, v_shift, grad_gain_one, grad_shift_one, two_shift,
                    down_shift, grad_gain_two, grad_shift_two, out_shift,
                ]
            ),
            up_shift.reshape(-1, width),
            grad_lang,
        ]
    )
    hid_grad_even = mm_nt(grad_two, two_full[width : 2 * width])
    grad_even = (hid_grad_even * slope_even.astype(F32)).astype(BF16)
    grad_even, grad_two, follow, vectors = tie([two, ffn], grad_even, grad_two, follow, vectors)
    two = split_rows(two)
    first_hops(two)
    for bit in bits[2:]:
        ffn.dp_hop(bit)
    vectors += send(vectors, CORE)
    hid_grad_last = mm_nt(grad_two, two_full[2 * width :])
    grad_next = jnp.concatenate([grad_two[1:], follow])
    hid_grad_odd = hid_grad_last + mm_nt(grad_next, two_full[:width])
    grad_odd = (hid_grad_odd * slope_odd.astype(F32)).astype(BF16)
    grad_odd, vectors = tie(qkv + [ffn], grad_odd, vectors)
    second_hops(qkv)
    backs = list(reversed(bits))
    ffn = Gather(ffn.total())
    ffn.hop((backs[0],))
    vectors += send(vectors, CROSS)
    one_grads = mm_tn(grad_even, cols_even) + mm_tn(grad_odd, cols_odd)
    spare = width // 3 - one_grads.shape[1]
    one = owner_terms(jnp.pad(one_grads, ((0, 0), (0, spare))))
    grad_even, grad_odd, vectors = tie([one] + two, grad_even, grad_odd, vectors)
    second_hops(two)
    core_hop(one)
    vectors += over_dp(vectors, 1)
    terms_even = mm(grad_even, one_whole)
    terms_odd = mm(grad_odd, one_whole)
    before, mid_e, late = (terms_even[:, k * mels : (k + 1) * mels] for k in range(3))
    early, mid_o, last = (terms_odd[:, k * mels : (k + 1) * mels] for k in range(3))
    spill = send(jnp.where(c == 0, last[-1:], before[0:1]), CORE)
    zero_spill = jnp.zeros_like(spill)
    last_prev = jnp.concatenate([jnp.where(c == 1, spill, zero_spill), last[:-1]])
    before_next = jnp.concatenate([before[1:], jnp.where(c == 0, spill, zero_spill)])
    mel_grad = jnp.concatenate(
        [mid_e + early + last_prev, late + mid_o + before_next], axis=1
    ).astype(BF16)
    mel_grad, vectors = tie([one, ffn] + qkv, mel_grad, vectors)
    x_hop(one)
    for bit in backs[1:-1]:
        ffn.hop((bit,))
    for side in qkv:
        side.terms, side.fixed = [(side.total(), tuple(bits[1:]))], {}
    qkv = Terms(jnp.stack([side.arrays[0] for side in qkv], axis=len(bits) - 1), bits[1:])
    qkv.rest_hops()
    mel_grad, vectors = tie([one], mel_grad, vectors)
    one_share = one.total()
    one_rows = one_share.shape[0] // 3
    flat = jnp.concatenate([one_share[k * one_rows : (k + 1) * one_rows] for k in range(3)], axis=1)
    flat = Terms(
        jnp.stack([flat[:, : width // 2], flat[:, width // 2 :]]).swapaxes(0, 1).reshape(
            (2,) * len(bits) + (one_rows // 2 ** len(bits), 2, width // 2)
        ).swapaxes(-3, -2),
        bits,
    )
    flat.dp_hop(1)
    mel_grad = send_back(mel_grad)
    mel_grad, vectors = tie([flat, ffn] + two, mel_grad, vectors)
    conv = jnp.stack([side.total() for side in two], axis=len(bits) - 1)
    conv = Terms(jnp.concatenate([conv, flat.total()], axis=-2), bits[1:])
    conv.rest_hops()
    ffn.hop((1,))
    vectors = tie([qkv, conv], vectors)
    qkv = Gather(qkv.total(), 1)
    qkv.rest_hops()
    conv = Gather(conv.total(), 1)
    conv.rest_hops()
    for bit in bits[1:2]:
        vectors += over_dp(vectors, bit)
    mel_grad = take_back(*mel_grad).astype(F32).reshape(slots, 2 * part, mels)
    mel_grad, vectors = tie([qkv, conv, ffn], mel_grad, vectors)
    qkv.hop((1,))
    conv.hop((1,))
    for bit in bits[2:]:
        vectors += over_dp(vectors, bit)
    tie([qkv])
    qkv_share = qkv.settle()
    vectors = tie([conv], vectors)
    conv = conv.settle()
    ffn = ffn.settle().astype(F32)
    down_sum = ffn[: hidden // 4]
    up_sum = jnp.concatenate(
        [ffn[hidden // 4 + k * quarter : hidden // 4 + (k + 1) * quarter] for k in range(blocks)],
        axis=1,
    )

    def columns(sides):
        return jnp.concatenate([sides[0], sides[1]], axis=1).astype(F32)

    qkv_out = columns(qkv_share)
    pieces = 2 ** len(bits)
    conv_pieces = columns(conv).reshape(pieces, -1, width)
    taken = 3 * quarter // pieces
    two_sum = conv_pieces[:, :taken].reshape(conv_two.shape)
    one_flat = conv_pieces[:, taken:].reshape(one_rows, width)
    one_sum = jnp.concatenate(
        [one_flat[:, k * width // 3 : (k + 1) * width // 3] for k in range(3)]
    )
    vec = lambda k: vectors[k]
    return (
        encoded,
        mel_grad,
        one_sum[:, : 3 * mels].T,
        one_sum[:, 3 * mels],
        two_sum,
        vec(4),
        vectors[9 + blocks :],
        vec(2),
        vec(3),
        qkv_out[:, : 3 * width],
        vec(0),
        vec(1),
        qkv_out[:, 3 * width :],
        vec(8),
        vec(6),
        vec(7),
        up_sum,
        vectors[9 : 9 + blocks].reshape(-1),
        down_sum,
        vec(5),
    )


def solution(mesh):
    in_specs = (
        P("dp", "chan", None),
        P("dp"),
        P(),
        P(None, "chan"),
        P("chan"),
        P(None, "chan", None),
        P(),
        P(),
        P(),
        P(),
        P("chan", None),
        P(),
        P(),
        P("chan", None),
        P(),
        P(),
        P(),
        P("chan", None),
        P(),
        P("chan", None),
        P(),
        P("dp", "chan", None),
    )
    out_specs = (
        P("dp", "chan", None),
        P("dp", "chan", None),
        P(None, "chan"),
        P("chan"),
        P(None, "chan", None),
        P(),
        P(),
        P(),
        P(),
        P("chan", None),
        P(),
        P(),
        P("chan", None),
        P(),
        P(),
        P(),
        P("chan", None),
        P(),
        P("chan", None),
        P(),
    )
    return jax.shard_map(
        on_device, mesh=mesh, in_specs=in_specs, out_specs=out_specs, check_vma=False
    )
```

```python
import math

import jax
import jax.numpy as jnp
from jax import lax
from jax.experimental import pallas as pl
from jax.experimental.pallas import tpu as pltpu
from jax.sharding import PartitionSpec as P

HEAD_DIM = 64
PAIR = 2 * HEAD_DIM
SCALE = HEAD_DIM ** (-0.5)
BF16 = jnp.bfloat16
F32 = jnp.float32

CORE = [(j, j ^ 1) for j in range(4)]
CROSS = [(j, j ^ 2) for j in range(4)]
SAME = [(2 * x + c, 2 * c + x) for x in range(2) for c in range(2)]
OTHER = [(2 * x + c, 2 * (1 - c) + x) for x in range(2) for c in range(2)]
SAME_BACK = [(b, a) for a, b in SAME]
OTHER_BACK = [(b, a) for a, b in OTHER]


def send(block, perm):
    return lax.ppermute(block, "chan", perm)


def ordered(first_is_own, own, other, axis=0, stack=False):
    join = jnp.stack if stack else jnp.concatenate
    return jnp.where(first_is_own, join([own, other], axis), join([other, own], axis))


def pick(block, index, axis):
    return lax.dynamic_index_in_dim(block, index, axis, keepdims=False)


def gelu_both(inputs):
    cdf = 0.5 * (1.0 + lax.erf(inputs * math.sqrt(0.5)))
    pdf = jnp.exp(-0.5 * inputs * inputs) * (1.0 / math.sqrt(2.0 * math.pi))
    return inputs * cdf, cdf + inputs * pdf


def norm_stats(inputs):
    row_mean = jnp.mean(inputs, axis=-1, keepdims=True)
    centered = inputs - row_mean
    variance = jnp.mean(centered * centered, axis=-1, keepdims=True)
    return row_mean, lax.rsqrt(variance + 1e-05)


def norm_back(inputs, stats, gain_vec, cotangent):
    row_mean, inverse = stats
    unit = (inputs - row_mean) * inverse
    scaled = cotangent * gain_vec
    mean_one = jnp.mean(scaled, axis=-1, keepdims=True)
    mean_two = jnp.mean(scaled * unit, axis=-1, keepdims=True)
    grad = inverse * (scaled - mean_one - unit * mean_two)
    return grad, jnp.sum(cotangent * unit, axis=0), jnp.sum(cotangent, axis=0)


def positions(frame_count, model_width, first_frame):
    increment = math.log(10000.0) / (model_width // 2 - 1)
    inverse = jnp.exp(-increment * jnp.arange(model_width // 2, dtype=jnp.float32))
    angles = (first_frame + jnp.arange(frame_count)).astype(jnp.float32)[:, None] * inverse[None, :]
    return jnp.concatenate([jnp.sin(angles), jnp.cos(angles)], axis=1)


def mm(left, right):
    return jnp.dot(left, right, preferred_element_type=F32)


def mm_nt(left, right):
    return lax.dot_general(left, right, (((1,), (1,)), ((), ())), preferred_element_type=F32)


def mm_tn(left, right):
    return lax.dot_general(left, right, (((0,), (0,)), ((), ())), preferred_element_type=F32)


def head_stack(block):
    lane = lax.broadcasted_iota(jnp.int32, block.shape, 1)
    zero = jnp.zeros_like(block)
    return jnp.concatenate(
        [jnp.where(lane < HEAD_DIM, block, zero), jnp.where(lane < HEAD_DIM, zero, block)], axis=0
    )


def head_join(stacked):
    rows = stacked.shape[0] // 2
    lane = lax.broadcasted_iota(jnp.int32, (rows, stacked.shape[1]), 1)
    return jnp.where(lane < HEAD_DIM, stacked[:rows], stacked[rows:])


def attend_kernel(chunk, q_ref, k_own, k_oth, v_own, v_oth, *refs):
    att_ref, lse_ref, k_all, v_all = refs[-4:]
    rows = q_ref.shape[0]
    k_all[0:rows] = k_own[...]
    k_all[rows:] = k_oth[...]
    v_all[0:rows, 0:PAIR] = v_own[...]
    v_all[rows:, 0:PAIR] = v_oth[...]
    v_all[:, PAIR:] = jnp.ones((2 * rows, PAIR), BF16)
    for start in range(0, rows, chunk):
        at = pl.ds(start, chunk)
        queries = head_stack(q_ref[at] * SCALE)
        scores = mm_nt(queries, k_all[...])
        top = jnp.max(scores, axis=1, keepdims=True)
        both = mm(jnp.exp(scores - top).astype(BF16), v_all[...])
        total = both[:, PAIR:]
        att_ref[at] = head_join(both[:, :PAIR] / total).astype(BF16)
        lse_ref[at] = head_join(top + jnp.log(total))


def attend(q, kv_own, kv_oth, first, count, pairs, earlier=()):
    rows = q.shape[0]
    chunk = 176
    spec = lambda shift: pl.BlockSpec((rows, PAIR), lambda p: (0, p + shift))
    return pl.pallas_call(
        lambda *refs: attend_kernel(chunk, *refs),
        grid=(count,),
        in_specs=[spec(first), spec(first), spec(first), spec(first + pairs), spec(first + pairs)]
        + [pl.BlockSpec(memory_space=pl.ANY)] * len(earlier),
        out_specs=[spec(first)] * 2,
        out_shape=[
            jax.ShapeDtypeStruct((rows, pairs * PAIR), BF16),
            jax.ShapeDtypeStruct((rows, pairs * PAIR), F32),
        ],
        input_output_aliases={5 + i: i for i in range(len(earlier))},
        scratch_shapes=[
            pltpu.VMEM((2 * rows, PAIR), BF16),
            pltpu.VMEM((2 * rows, 2 * PAIR), BF16),
        ],
        compiler_params=pltpu.CompilerParams(vmem_limit_bytes=56 * 1024 * 1024),
        cost_estimate=pl.CostEstimate(
            flops=count * 16 * rows * rows * PAIR,
            bytes_accessed=count * PAIR * rows * 16,
            transcendentals=4 * count * rows * rows,
        ),
        name="attend",
    )(q, kv_own, kv_oth, kv_own, kv_oth, *earlier)


def attend_back_kernel(chunk, q_ref, k_own, k_oth, v_own, v_oth, lse_ref, g_ref, *refs):
    dq_ref, own_ref, oth_ref, k_all, v_all, q_all, g_all, p_all, s_all = refs[-9:]
    rows = q_ref.shape[0]
    k_all[0:rows] = k_own[...]
    k_all[rows:] = k_oth[...]
    v_all[0:rows] = v_own[...]
    v_all[rows:] = v_oth[...]
    for start in range(0, rows, chunk):
        at = pl.ds(start, chunk)
        both = pl.ds(2 * start, 2 * chunk)
        queries = head_stack(q_ref[at] * SCALE)
        grads = head_stack(g_ref[at])
        q_all[both] = queries
        g_all[both] = grads
        lse = jnp.concatenate([lse_ref[at, 0:1], lse_ref[at, HEAD_DIM : HEAD_DIM + 1]], axis=0)
        probs = jnp.exp(mm_nt(queries, k_all[...]) - lse)
        grad_probs = mm_nt(grads, v_all[...])
        inner = jnp.sum(probs * grad_probs, axis=1, keepdims=True)
        grad_scores = (probs * (grad_probs - inner)).astype(BF16)
        p_all[both] = probs.astype(BF16)
        s_all[both] = grad_scores
        dq_ref[at] = (head_join(mm(grad_scores, k_all[...])) * SCALE).astype(BF16)

    dk = mm_tn(q_all[...], s_all[...]).T.astype(BF16)
    own_ref[0] = dk[0:rows]
    oth_ref[0] = dk[rows:]
    dv = mm_tn(g_all[...], p_all[...]).T.astype(BF16)
    own_ref[1] = dv[0:rows]
    oth_ref[1] = dv[rows:]


def attend_back(q, kv_own, kv_oth, lse, grad_att, first, count, pairs, earlier=()):
    rows = q.shape[0]
    chunk = 176
    spec = lambda shift: pl.BlockSpec((rows, PAIR), lambda p: (0, p + shift))
    two = pl.BlockSpec((2, rows, PAIR), lambda p: (0, 0, p + first))
    both = jax.ShapeDtypeStruct((2, rows, pairs * PAIR), BF16)
    return pl.pallas_call(
        lambda *refs: attend_back_kernel(chunk, *refs),
        grid=(count,),
        in_specs=[spec(first), spec(first), spec(first), spec(first + pairs), spec(first + pairs)]
        + [spec(first)] * 2
        + [pl.BlockSpec(memory_space=pl.ANY)] * len(earlier),
        out_specs=[spec(first), two, two],
        out_shape=[jax.ShapeDtypeStruct((rows, pairs * PAIR), BF16), both, both],
        input_output_aliases={7 + i: i for i in range(len(earlier))},
        scratch_shapes=[pltpu.VMEM((2 * rows, PAIR), BF16)] * 4
        + [pltpu.VMEM((2 * rows, 2 * rows), BF16)] * 2,
        compiler_params=pltpu.CompilerParams(vmem_limit_bytes=56 * 1024 * 1024),
        cost_estimate=pl.CostEstimate(
            flops=count * 40 * rows * rows * PAIR,
            bytes_accessed=count * PAIR * rows * 26,
            transcendentals=4 * count * rows * rows,
        ),
        name="attend_back",
    )(q, kv_own, kv_oth, kv_own, kv_oth, lse, grad_att, *earlier)


def join(*values):
    return lax.optimization_barrier(values)


def after(value, *others):
    return lax.optimization_barrier((value,) + others)[0]


def place_kernel(moves, halved, index_ref, own, near, *refs):
    outs = len(refs) - (3 if halved else 2) - 1
    fars, wholes, sems = refs[: -outs - 1], refs[-outs - 1 : -1], refs[-1]
    j, y = index_ref[0], index_ref[1]
    x, c = j // 2, j % 2
    rows = own.shape[1]
    across = rows * (2 * (1 - x) + c)
    beside = rows * (2 * (1 - x) + 1 - c)
    pieces = [(own, rows * j), (near, rows * (2 * x + 1 - c))]
    if halved:
        half = rows // 2
        pieces += [
            (fars[0], across + half * y),
            (fars[1], across + half * (1 - y)),
            (fars[2].at[0], beside + half * y),
            (fars[2].at[1], beside + half * (1 - y)),
        ]
    else:
        half = rows
        pieces += [(fars[0], across), (fars[1], beside)]
    copies = []
    for piece, row in pieces:
        at = pl.ds(pl.multiple_of(row, half), piece.shape[1])
        for move in moves:
            source, target = move(piece, wholes, at)
            copies.append(pltpu.make_async_copy(source, target, sems.at[len(copies)]))
    for copy in copies:
        copy.start()
    for copy in copies:
        copy.wait()


def place(index, parts, moves, *shapes):
    anywhere = pl.BlockSpec(memory_space=pl.ANY)
    halved = len(parts) == 5
    return pl.pallas_call(
        lambda *refs: place_kernel(moves, halved, *refs),
        in_specs=[pl.BlockSpec(memory_space=pltpu.SMEM)] + [anywhere] * len(parts),
        out_specs=[pl.BlockSpec(memory_space=pltpu.VMEM)] * len(shapes),
        out_shape=[jax.ShapeDtypeStruct(shape, BF16) for shape in shapes],
        scratch_shapes=[pltpu.SemaphoreType.DMA(((6 if halved else 4) * len(moves),))],
        compiler_params=pltpu.CompilerParams(vmem_limit_bytes=16 * 1024 * 1024),
        cost_estimate=pl.CostEstimate(
            flops=0, bytes_accessed=sum(4 * math.prod(shape) for shape in shapes), transcendentals=0
        ),
        name="place",
    )(index, *parts)


ROW_MOVES = [lambda piece, wholes, at: (piece.at[0], wholes[0].at[at])]
TAP_MOVES = [lambda piece, wholes, at: (piece, wholes[0].at[:, at])]


def block_moves(blocks, width):
    def move(block):
        columns = pl.ds(block * width, width)
        return lambda piece, wholes, at: (piece.at[1 + block], wholes[1].at[at, columns])

    return ROW_MOVES + [move(block) for block in range(blocks)]


def round_sum(*terms):
    return sum(term.astype(F32) for term in terms).astype(BF16)


def dp_bits():
    bits = [1]
    while 2 * bits[-1] < lax.axis_size("dp"):
        bits.append(2 * bits[-1])
    return bits


def over_dp(block, bit):
    return lax.ppermute(block, "dp", [(d, d ^ bit) for d in range(lax.axis_size("dp"))])


def dp_side(bit):
    return (lax.axis_index("dp") // bit) % 2


class Terms:
    def __init__(self, array, names):
        self.terms, self.fixed = [(array, tuple(names))], {}

    def view(self, chosen):
        def cut(array, names):
            axis = 0
            for name in names:
                if name in chosen:
                    array = pick(array, chosen[name], axis)
                else:
                    axis += 1
            return array

        return round_sum(*[cut(array, names) for array, names in self.terms])

    def hop(self, name, side, ship):
        block = self.view({**self.fixed, name: 1 - side})
        names = tuple(n for n in self.terms[0][1] if n not in self.fixed and n != name)
        self.fixed[name] = side
        self.terms.append((ship(block), names))

    def dp_hop(self, bit):
        self.hop(bit, dp_side(bit), lambda block: over_dp(block, bit))

    def quad_hop(self, pair):
        sides = [dp_side(bit) for bit in pair]
        names = tuple(n for n in self.terms[0][1] if n not in self.fixed and n not in pair)
        arrived = []
        for other in (1, 2, 3):
            place = {pair[0]: (sides[0] + other // 2) % 2, pair[1]: (sides[1] + other) % 2}
            arrived.append(quad_send(self.view({**self.fixed, **place}), pair, other))
        self.fixed.update(zip(pair, sides))
        self.terms += [(block, names) for block in arrived]

    def rest_hops(self):
        for group in rest_groups():
            if len(group) == 2:
                self.quad_hop(group)
            else:
                self.dp_hop(group[0])

    def total(self):
        return self.view(self.fixed)

    @property
    def arrays(self):
        return [array for array, _ in self.terms]

    @arrays.setter
    def arrays(self, arrays):
        self.terms = [(array, names) for array, (_, names) in zip(arrays, self.terms)]


def tie(sums, *main):
    lists, main = lax.optimization_barrier(([t.arrays for t in sums], main))
    for t, arrays in zip(sums, lists):
        t.arrays = arrays
    return main[0] if len(main) == 1 else main


class Gather:
    def __init__(self, share, axis=0):
        self.share, self.axis, self.group, self.arrived = share, axis, (), []

    def settle(self):
        sides = [dp_side(bit) == 0 for bit in self.group]
        if len(sides) == 1:
            self.share = ordered(sides[0], self.share, self.arrived[0], self.axis)
        elif len(sides) == 2:
            near, far, last = self.arrived
            own_pair = ordered(sides[1], self.share, near, self.axis)
            far_pair = ordered(sides[1], far, last, self.axis)
            self.share = ordered(sides[0], own_pair, far_pair, self.axis)
        self.group, self.arrived = (), []
        return self.share

    def hop(self, group):
        share = self.settle()
        self.group = group
        if len(group) == 1:
            self.arrived = [over_dp(share, group[0])]
        else:
            self.arrived = [quad_send(share, group, other) for other in (1, 2, 3)]

    def rest_hops(self):
        for group in reversed(rest_groups()):
            self.hop(group)

    @property
    def arrays(self):
        return [self.share] + self.arrived

    @arrays.setter
    def arrays(self, arrays):
        self.share, self.arrived = arrays[0], list(arrays[1:])


def rest_groups():
    bits = dp_bits()[1:]
    return [tuple(bits[k : k + 2]) for k in range(0, len(bits), 2)]


def quad_send(block, pair, other):
    flip = pair[0] * (other // 2) + pair[1] * (other % 2)
    return lax.ppermute(block, "dp", [(d, d ^ flip) for d in range(lax.axis_size("dp"))])


def on_device(
    mel,
    lang_group,
    clip_count,
    conv_one,
    conv_one_bias,
    conv_two,
    conv_two_bias,
    lang_table,
    ln_one_gain,
    ln_one_bias,
    w_qkv,
    q_bias,
    v_bias,
    w_out,
    out_bias,
    ln_two_gain,
    ln_two_bias,
    w_fc_one,
    fc_one_bias,
    w_fc_two,
    fc_two_bias,
    grad_out,
):
    slots, part, width = grad_out.shape
    hidden = w_fc_one.shape[1]
    pairs = width // PAIR
    quarter = width // 4
    mels = mel.shape[2]
    rows = slots * part
    j = lax.axis_index("chan")
    x, c = j // 2, j % 2
    live = (x < clip_count[lax.axis_index("dp")]).astype(F32)

    def to_clip(block):
        same = send(pick(block, c, 0), SAME)
        other = send(pick(block, 1 - c, 0), OTHER)
        return ordered(x == 0, same, other)

    def send_back(block):
        half = block.shape[0] // 2
        first, second = block[:half], block[half:]
        same = send(jnp.where(x == 0, first, second), SAME_BACK)
        return same, send(jnp.where(x == 0, second, first), OTHER_BACK)

    def take_back(same, other):
        return ordered(c == 0, same, other, stack=True)

    mel_pairs = mel.reshape(slots, part, 2 * mels)
    edge = send(jnp.where(j == 1, mel_pairs[1, -1], mel_pairs[0, 0]), [(1, 3), (2, 0)])
    edge = jnp.where(j == 1, mel_pairs[0, -1], jnp.where(j == 2, mel_pairs[1, 0], edge))
    zero_edge = jnp.zeros_like(edge)
    mel_own = jnp.concatenate(
        [
            jnp.where(c == 1, edge, zero_edge)[None],
            to_clip(mel_pairs),
            jnp.where(c == 0, edge, zero_edge)[None],
        ]
    )

    y = lax.axis_index("dp") % 2
    index = jnp.stack([j, y])
    one_part = jnp.concatenate([conv_one.T, conv_one_bias[:, None]], axis=1)
    blocks = hidden // width
    up_part = jnp.stack(
        [w_out] + [w_fc_one[:, k * width : (k + 1) * width] for k in range(blocks)]
    )
    one_across = send(one_part, CROSS)
    qkv_part, down_part = w_qkv[None], w_fc_two[None]
    two_across = send(conv_two, CROSS)
    one_across, up_part, two_across = join(one_across, up_part, two_across)
    one_column = ordered(x == 0, one_part, one_across, stack=True)
    one_whole = ordered(c == 0, one_column, send(one_column, CORE), 1, stack=True)
    one_whole = one_whole.reshape(width, -1)

    def cross_half(own, side=y):
        half = own.shape[1] // 2
        return send(lax.dynamic_slice_in_dim(own, side * half, half, 1), CROSS)

    def cross_rest(far):
        return over_dp(far, 1)

    def beside(far, rest):
        return send(jnp.stack([far, rest]), CORE)

    two_near = send(conv_two, CORE)
    qkv_far = cross_half(after(qkv_part, two_across))

    mel_own, one_whole, qkv_far = join(mel_own, one_whole, qkv_far)
    two_beside = send(two_across, CORE)
    qkv_rest = cross_half(after(qkv_part, qkv_far), 1 - y)
    even, odd = mel_own[:, :mels], mel_own[:, mels:]
    ones = jnp.ones((rows, 1), BF16)
    cols_even = jnp.concatenate([odd[0:rows], even[1 : rows + 1], odd[1 : rows + 1], ones], axis=1)
    cols_odd = jnp.concatenate(
        [even[1 : rows + 1], odd[1 : rows + 1], even[2 : rows + 2], ones], axis=1
    )
    cols_edge = jnp.concatenate([even[0:1], odd[0:1], even[1:2], ones[0:1]], axis=1)
    hid_even, slope_even = gelu_both(mm_nt(cols_even, one_whole))
    hid_odd, slope_odd = gelu_both(mm_nt(cols_odd, one_whole))
    hid_edge, _ = gelu_both(mm_nt(cols_edge, one_whole))
    hid_edge = jnp.where(c == 1, hid_edge, 0.0)
    hid_even, hid_odd, hid_edge = hid_even.astype(BF16), hid_odd.astype(BF16), hid_edge.astype(BF16)
    slope_even, slope_odd = slope_even.astype(BF16), slope_odd.astype(BF16)
    hid_even, hid_odd, hid_edge, slope_even, slope_odd, two_beside = join(
        hid_even, hid_odd, hid_edge, slope_even, slope_odd, two_beside
    )
    hid_prev = jnp.concatenate([hid_edge, hid_odd[:-1]])
    hid_taps = jnp.concatenate([hid_prev, hid_even, hid_odd], axis=1)
    group = pick(lang_group, x, 0)
    place_rows = positions(rows, width, after(c * rows, hid_edge))
    place_rows += pick(lang_table, group, 0).astype(F32)[None]
    place_rows, hid_taps, qkv_rest = join(place_rows, hid_taps, qkv_rest)
    qkv_near = send(after(qkv_part, qkv_rest), CORE)
    qkv_beside = beside(qkv_far, qkv_rest)
    (two_full,) = place(
        index, (conv_two, two_near, two_across, two_beside), TAP_MOVES, (3, width, width)
    )
    two_full = two_full.reshape(-1, width)
    stem_act, slope_two = gelu_both(mm(hid_taps, two_full) + conv_two_bias.astype(F32))
    slope_two = slope_two.astype(BF16)
    stem = stem_act + place_rows

    gain_one, gain_two = ln_one_gain.astype(F32), ln_two_gain.astype(F32)
    stats_one = norm_stats(stem)
    normed = (
        (stem - stats_one[0]) * stats_one[1] * gain_one + ln_one_bias.astype(F32)
    ).astype(BF16)
    normed, slope_two, qkv_near, qkv_beside = join(normed, slope_two, qkv_near, qkv_beside)
    up_far = cross_half(after(up_part, qkv_rest))
    (qkv_full,) = place(
        index, (qkv_part, qkv_near, qkv_far, qkv_rest, qkv_beside), ROW_MOVES, (width, 3 * width)
    )
    kv_shift = jnp.concatenate([jnp.zeros((width,), F32), v_bias.astype(F32)])
    kv_own = (mm(normed, qkv_full[:, width:]) + kv_shift).astype(BF16)
    kv_oth = send(kv_own, CORE)
    queries = (mm(normed, qkv_full[:, :width]) + q_bias.astype(F32)).astype(BF16)
    queries, kv_oth = join(queries, kv_oth)
    half = pairs // 2
    partial = attend(queries, kv_own, kv_oth, 0, half, pairs)
    *partial, up_far = join(*partial, up_far)
    up_near = send(after(up_part, up_far), CORE)
    up_rest = cross_rest(up_far)
    down_far = cross_half(after(down_part, up_far))
    down_near = send(after(down_part, up_far), CORE)
    attended, lse = attend(queries, kv_own, kv_oth, half, pairs - half, pairs, partial)
    attended, up_near, up_rest, down_far, down_near = join(
        attended, up_near, up_rest, down_far, down_near
    )
    up_beside = beside(up_far, up_rest)
    down_rest = cross_rest(down_far)
    grad_part = after(grad_out, down_far)
    grad_same = send(pick(grad_part, c, 0), SAME)
    grad_other = send(pick(grad_part, 1 - c, 0), OTHER)
    out_full, up_full = place(
        index,
        (up_part, up_near, up_far, up_rest, up_beside),
        block_moves(blocks, width),
        (width, width),
        (width, hidden),
    )
    residual = stem + mm(attended, out_full) + out_bias.astype(F32)

    stats_two = norm_stats(residual)
    normed_two = (
        (residual - stats_two[0]) * stats_two[1] * gain_two + ln_two_bias.astype(F32)
    ).astype(BF16)
    active, slope_up = gelu_both(mm(normed_two, up_full) + fc_one_bias.astype(F32))
    active, slope_up = active.astype(BF16), slope_up.astype(BF16)

    def owner_terms(grads):
        return Terms(grads.astype(BF16).reshape(2, 2, -1, grads.shape[1]), ["x", "core"])

    def core_hop(terms):
        terms.hop("core", c, lambda block: send(block, CORE))

    def x_hop(terms):
        terms.hop("x", x, lambda block: send(block, CROSS))

    def first_hops(sides):
        x_hop(sides[0])
        sides[1].dp_hop(1)

    def second_hops(sides):
        sides[0].dp_hop(1)
        x_hop(sides[1])

    active, slope_up, down_rest, grad_same, grad_other = join(
        active, slope_up, down_rest, grad_same, grad_other
    )
    cotangent = ordered(x == 0, grad_same, grad_other)
    down_parts = (down_part, down_near, down_far, down_rest, beside(down_far, down_rest))
    (down_full,) = place(index, down_parts, ROW_MOVES, (hidden, width))
    grad_mlp = (cotangent.astype(F32) * live).astype(BF16)
    grad_rows = grad_mlp.astype(F32)
    down = owner_terms(mm_tn(active, grad_mlp))
    down_shift = jnp.sum(grad_rows, axis=0)
    grad_mlp = tie([down], grad_mlp)
    core_hop(down)
    grad_upper = (mm_nt(grad_mlp, down_full) * slope_up.astype(F32)).astype(BF16)
    up_shift = jnp.sum(grad_upper.astype(F32), axis=0)
    grad_upper = tie([down], grad_upper)
    x_hop(down)
    up = owner_terms(mm_tn(normed_two, grad_upper))
    grad_upper = tie([up], grad_upper)
    core_hop(up)
    grad_norm, grad_gain_two, grad_shift_two = norm_back(
        residual, stats_two, gain_two, mm_nt(grad_upper, up_full)
    )
    grad_residual = grad_rows + grad_norm
    grad_branch = grad_residual.astype(BF16)
    out_shift = jnp.sum(grad_branch.astype(F32), axis=0)
    out_grads = mm_tn(attended, grad_branch).astype(BF16)
    grad_att = mm_nt(grad_branch, out_full).astype(BF16)
    grad_att, out_grads = tie([up], grad_att, out_grads)

    third = -(-pairs // 3)
    operands = (queries, kv_own, kv_oth, lse)
    bits = dp_bits()
    partial = attend_back(*operands, grad_att, 0, third, pairs)
    partial = tie([down, up], *partial)
    x_hop(up)
    grad_q, own_kv, oth_kv = attend_back(*operands, grad_att, third, pairs - third, pairs, partial)
    grad_q, own_kv, oth_kv = tie([up], grad_q, own_kv, oth_kv)
    oth_kv = send(oth_kv, CORE)
    up_share = up.total()
    ffn = jnp.concatenate(
        [down.total()] + [up_share[:, k * width : (k + 1) * width] for k in range(blocks)]
    )
    ffn = Terms(ffn.reshape((2,) * len(bits) + (-1, width)), bits)
    ffn.dp_hop(1)
    encoded = (residual + mm(after(active, grad_q), down_full) + fc_two_bias.astype(F32)) * live
    encoded, own_kv, oth_kv = join(encoded.astype(BF16), own_kv, oth_kv)
    q_shift = jnp.sum(grad_q.astype(F32), axis=0)
    grad_kv = round_sum(own_kv, oth_kv)
    grad_packed = jnp.concatenate([grad_q, grad_kv[0], grad_kv[1]], axis=1)
    qkv_grads = jnp.concatenate([mm_tn(normed, grad_packed).astype(BF16), out_grads], axis=1)
    v_shift = jnp.sum(grad_kv[1].astype(F32), axis=0)
    qkv = owner_terms(qkv_grads)
    grad_packed = tie([qkv], grad_packed)
    core_hop(qkv)
    encoded = send_back(encoded)
    grad_normed = tie([qkv], mm_nt(grad_packed, qkv_full))

    def split_rows(terms):
        middle = terms.arrays[0].shape[-1] // 2
        sides = []
        for cut in (slice(0, middle), slice(middle, None)):
            side = Terms(None, ())
            side.terms = []
            for array, names in terms.terms:
                part = array[..., cut]
                shape = part.shape[: len(names)] + (2,) * len(bits)
                part = part.reshape(shape + (part.shape[-2] // 2 ** len(bits), middle))
                side.terms.append((part, names + tuple(bits)))
            side.fixed = dict(terms.fixed)
            sides.append(side)
        return sides

    qkv = split_rows(qkv)
    first_hops(qkv)
    grad_norm, grad_gain_one, grad_shift_one = norm_back(stem, stats_one, gain_one, grad_normed)
    grad_stem = grad_residual + grad_norm
    group_hot = (jnp.arange(lang_table.shape[0]) == group).astype(F32)
    grad_lang = group_hot[:, None] * jnp.sum(grad_stem, axis=0)[None]
    grad_two = (grad_stem * slope_two.astype(F32)).astype(BF16)
    two_shift = jnp.sum(grad_two.astype(F32), axis=0)
    two_grads = mm_tn(hid_taps, grad_two).astype(BF16).reshape(3, 2, 2, quarter, width)
    two = Terms(
        two_grads.transpose(1, 2, 0, 3, 4).reshape(2, 2, 3 * quarter, width), ["x", "core"]
    )
    grad_two, encoded = tie([two, ffn], grad_two, encoded)
    encoded = take_back(*encoded)
    core_hop(two)
    for bit in bits[1:2]:
        ffn.dp_hop(bit)
    follow = send(grad_two[0:1], [(1, 0), (3, 2)])
    vectors = jnp.concatenate(
        [
            jnp.stack(
                [
                    q_shift, v_shift, grad_gain_one, grad_shift_one, two_shift,
                    down_shift, grad_gain_two, grad_shift_two, out_shift,
                ]
            ),
            up_shift.reshape(-1, width),
            grad_lang,
        ]
    )
    hid_grad_even = mm_nt(grad_two, two_full[width : 2 * width])
    grad_even = (hid_grad_even * slope_even.astype(F32)).astype(BF16)
    grad_even, grad_two, follow, vectors = tie([two, ffn], grad_even, grad_two, follow, vectors)
    two = split_rows(two)
    first_hops(two)
    for bit in bits[2:]:
        ffn.dp_hop(bit)
    vectors += send(vectors, CORE)
    hid_grad_last = mm_nt(grad_two, two_full[2 * width :])
    grad_next = jnp.concatenate([grad_two[1:], follow])
    hid_grad_odd = hid_grad_last + mm_nt(grad_next, two_full[:width])
    grad_odd = (hid_grad_odd * slope_odd.astype(F32)).astype(BF16)
    grad_odd, vectors = tie(qkv + [ffn], grad_odd, vectors)
    second_hops(qkv)
    backs = list(reversed(bits))
    ffn = Gather(ffn.total())
    ffn.hop((backs[0],))
    vectors += send(vectors, CROSS)
    one_grads = mm_tn(grad_even, cols_even) + mm_tn(grad_odd, cols_odd)
    spare = width // 3 - one_grads.shape[1]
    one = owner_terms(jnp.pad(one_grads, ((0, 0), (0, spare))))
    grad_even, grad_odd, vectors = tie([one] + two, grad_even, grad_odd, vectors)
    second_hops(two)
    core_hop(one)
    vectors += over_dp(vectors, 1)
    terms_even = mm(grad_even, one_whole)
    terms_odd = mm(grad_odd, one_whole)
    before, mid_e, late = (terms_even[:, k * mels : (k + 1) * mels] for k in range(3))
    early, mid_o, last = (terms_odd[:, k * mels : (k + 1) * mels] for k in range(3))
    spill = send(jnp.where(c == 0, last[-1:], before[0:1]), CORE)
    zero_spill = jnp.zeros_like(spill)
    last_prev = jnp.concatenate([jnp.where(c == 1, spill, zero_spill), last[:-1]])
    before_next = jnp.concatenate([before[1:], jnp.where(c == 0, spill, zero_spill)])
    mel_grad = jnp.concatenate(
        [mid_e + early + last_prev, late + mid_o + before_next], axis=1
    ).astype(BF16)
    mel_grad, vectors = tie([one, ffn] + qkv, mel_grad, vectors)
    x_hop(one)
    for bit in backs[1:-1]:
        ffn.hop((bit,))
    for side in qkv:
        side.terms, side.fixed = [(side.total(), tuple(bits[1:]))], {}
    qkv = Terms(jnp.stack([side.arrays[0] for side in qkv], axis=len(bits) - 1), bits[1:])
    qkv.rest_hops()
    mel_grad, vectors = tie([one], mel_grad, vectors)
    one_share = one.total()
    one_rows = one_share.shape[0] // 3
    flat = jnp.concatenate([one_share[k * one_rows : (k + 1) * one_rows] for k in range(3)], axis=1)
    flat = Terms(
        jnp.stack([flat[:, : width // 2], flat[:, width // 2 :]]).swapaxes(0, 1).reshape(
            (2,) * len(bits) + (one_rows // 2 ** len(bits), 2, width // 2)
        ).swapaxes(-3, -2),
        bits,
    )
    flat.dp_hop(1)
    mel_grad = send_back(mel_grad)
    mel_grad, vectors = tie([flat, ffn] + two, mel_grad, vectors)
    conv = jnp.stack([side.total() for side in two], axis=len(bits) - 1)
    conv = Terms(jnp.concatenate([conv, flat.total()], axis=-2), bits[1:])
    conv.rest_hops()
    ffn.hop((1,))
    vectors = tie([qkv, conv], vectors)
    qkv = Gather(qkv.total(), 1)
    qkv.rest_hops()
    conv = Gather(conv.total(), 1)
    conv.rest_hops()
    for bit in bits[1:2]:
        vectors += over_dp(vectors, bit)
    mel_grad = take_back(*mel_grad).astype(F32).reshape(slots, 2 * part, mels)
    mel_grad, vectors = tie([qkv, conv, ffn], mel_grad, vectors)
    qkv.hop((1,))
    conv.hop((1,))
    for bit in bits[2:]:
        vectors += over_dp(vectors, bit)
    tie([qkv])
    qkv_share = qkv.settle()
    vectors = tie([conv], vectors)
    conv = conv.settle()
    ffn = ffn.settle().astype(F32)
    down_sum = ffn[: hidden // 4]
    up_sum = jnp.concatenate(
        [ffn[hidden // 4 + k * quarter : hidden // 4 + (k + 1) * quarter] for k in range(blocks)],
        axis=1,
    )

    def columns(sides):
        return jnp.concatenate([sides[0], sides[1]], axis=1).astype(F32)

    qkv_out = columns(qkv_share)
    pieces = 2 ** len(bits)
    conv_pieces = columns(conv).reshape(pieces, -1, width)
    taken = 3 * quarter // pieces
    two_sum = conv_pieces[:, :taken].reshape(conv_two.shape)
    one_flat = conv_pieces[:, taken:].reshape(one_rows, width)
    one_sum = jnp.concatenate(
        [one_flat[:, k * width // 3 : (k + 1) * width // 3] for k in range(3)]
    )
    vec = lambda k: vectors[k]
    return (
        encoded,
        mel_grad,
        one_sum[:, : 3 * mels].T,
        one_sum[:, 3 * mels],
        two_sum,
        vec(4),
        vectors[9 + blocks :],
        vec(2),
        vec(3),
        qkv_out[:, : 3 * width],
        vec(0),
        vec(1),
        qkv_out[:, 3 * width :],
        vec(8),
        vec(6),
        vec(7),
        up_sum,
        vectors[9 : 9 + blocks].reshape(-1),
        down_sum,
        vec(5),
    )


def solution(mesh):
    in_specs = (
        P("dp", "chan", None),
        P("dp"),
        P(),
        P(None, "chan"),
        P("chan"),
        P(None, "chan", None),
        P(),
        P(),
        P(),
        P(),
        P("chan", None),
        P(),
        P(),
        P("chan", None),
        P(),
        P(),
        P(),
        P("chan", None),
        P(),
        P("chan", None),
        P(),
        P("dp", "chan", None),
    )
    out_specs = (
        P("dp", "chan", None),
        P("dp", "chan", None),
        P(None, "chan"),
        P("chan"),
        P(None, "chan", None),
        P(),
        P(),
        P(),
        P(),
        P("chan", None),
        P(),
        P(),
        P("chan", None),
        P(),
        P(),
        P(),
        P("chan", None),
        P(),
        P("chan", None),
        P(),
    )
    return jax.shard_map(
        on_device, mesh=mesh, in_specs=in_specs, out_specs=out_specs, check_vma=False
    )
```
